256 devices in a mesh: seq: 32 (over z, y), grp: 8 (over x, core).
Axes of the slice: x: 4, y: 4, z: 8, core: 2. Of those that a mesh axis runs over, the one named last changes fastest.
Arguments:
- output_grad: bfloat16 [32768, 4096], P(('seq', 'grp')), may hold values from -24 to 24
- router_logit: float32 [32768], P(('seq', 'grp')), may hold values from -6 to 6
- chosen_index: int32 [8192], P(('seq', 'grp')), may hold values from 0 to 127, as said below
- chosen_count: int32 [256], replicated, may hold values from 0 to 32, as said below
- out_weight: bfloat16 [2048, 4096], P('grp'), may hold values from -0.125 to 0.125
- queries: bfloat16 [4096, 2048], P('seq', 'grp'), may hold values from -6 to 6
- key_rows: bfloat16 [4096, 2048], P('seq', 'grp'), may hold values from -6 to 6
- value_rows: bfloat16 [4096, 2048], P('seq', 'grp'), may hold values from -6 to 6
Outputs:
- query_grad: bfloat16 [4096, 2048], P('seq', 'grp')
- key_grad: bfloat16 [4096, 2048], P('seq', 'grp')
- value_grad: bfloat16 [4096, 2048], P('seq', 'grp')
- out_weight_grad: float32 [4096, 2048], P('seq', 'grp')
- logit_grad: float32 [32768], P(('seq', 'grp'))
The draws below stay inside these ranges and needn't reach their ends.
Inputs may be any that keep to these rules, and one draw needn't show every extreme that they name: `chosen_count`: for each seq index, the counts of its 8 shards (consecutive in the list) sum to 128. `chosen_index`: in each shard's 32 slots the first chosen_count entries are distinct local token positions in increasing order; the other slots hold 0.
All inputs are finite; a program needn't handle non-finite values.
Results may differ from the reference program's by a relative error of at most 0.034.
Values may be sent and summed in bfloat16 or wider, within the bound.
A program may use at most 64 MiB of HBM per device.

```python
import jax
import jax.numpy as jnp
from jax import lax

D = 4096
HQ = 16
HD = 128
TOK_DEV = 128
CAP = 32
SEL_BLK = 128
SEL = 4096
TOKENS = 32768
SHARDS = 256


def routing_counts(key):
    key = jax.random.fold_in(key, 101)
    blocks = SEL // SEL_BLK
    members = SHARDS // blocks
    half_cap = CAP // 2
    key_list = jax.random.split(key, 2)
    shifts = jax.random.randint(key_list[0], (blocks, members // 2), 0, half_cap + 1)
    shifts = shifts.at[:, 0].set(half_cap)
    paired = jnp.concatenate([half_cap + shifts, half_cap - shifts], axis=1)
    orders = jax.vmap(lambda shard_key: jax.random.permutation(shard_key, members))(jax.random.split(key_list[1], blocks))
    counts = jnp.take_along_axis(paired, orders, axis=1)
    return counts.reshape(-1).astype(jnp.int32)


def draw_chosen_count(key, part):
    return routing_counts(key)


def draw_chosen_index(key, part):
    counts = routing_counts(key)
    key = jax.random.fold_in(key, 7)
    shard_keys = jax.random.split(key, SHARDS)

    def one_shard(shard_key, shard_count):
        shuffled = jax.random.permutation(shard_key, TOK_DEV)[:CAP]
        slot_ids = jnp.arange(CAP)
        ranked = jnp.where(slot_ids < shard_count, shuffled, TOK_DEV + slot_ids)
        ordered = jnp.sort(ranked)
        return jnp.where(slot_ids < shard_count, ordered, 0)
    return jax.vmap(one_shard)(shard_keys, counts).reshape(-1).astype(jnp.int32)


def draw_queries(key, part):
    base = jax.random.truncated_normal(jax.random.fold_in(key, 11), -6.0, 6.0, (SEL, HQ * HD), jnp.float32)
    return base.astype(jnp.bfloat16)


def draw_key_rows(key, part):
    base = jax.random.truncated_normal(jax.random.fold_in(key, 13), -6.0, 6.0, (SEL, HQ * HD), jnp.float32)
    return base.astype(jnp.bfloat16)


def spiked(array, own_key, source, target, shards_of, factor):
    owner, partner = [(jnp.arange(array.shape[axis_at]) // (array.shape[axis_at] // shards_of)).reshape([-1 if axis == axis_at else 1 for axis in range(array.ndim)]) for axis_at in (source, target)]
    chosen = jax.random.permutation(own_key, shards_of)[partner]
    strong = (owner == chosen) | (owner == (partner + shards_of // 2) % shards_of)
    return jnp.where(strong, factor * array, array)


def levels(key, shape, cuts, smallest, top_value):
    factor_of, own = 1.0, jax.random.fold_in(key, 6)
    for axis_at, parts in cuts:
        steps = jnp.exp(jax.random.uniform(jax.random.fold_in(own, axis_at), (parts,), jnp.float32, smallest / len(cuts), top_value / len(cuts)))
        factor_of = factor_of * jnp.repeat(steps, shape[axis_at] // parts).reshape([-1 if axis == axis_at else 1 for axis in range(len(shape))])
    return factor_of


def gaussian(rng, shape, deviation, most, pieces=(), kind=jnp.bfloat16):
    result = jax.random.normal(rng, shape, jnp.float32) * deviation
    if len(pieces) > 0:
        result = levels(rng, shape, pieces, -0.22, 0.18) * result
    return jnp.clip(result, min=-most, max=most).astype(kind)


def heavy_noise(rng, dims, width, most, shards, heavy, held_as=jnp.bfloat16):
    result = width * jax.random.normal(rng, dims, jnp.float32)
    if shards:
        result = result * levels(rng, dims, shards, -0.22, 0.18)
    return jnp.clip(spiked(result, jax.random.fold_in(rng, 3), *heavy), -most, most).astype(held_as)


def setup_inputs(seed: int = 0) -> dict:
    seeds = jax.random.split(jax.random.key(seed), 9)
    output_grad = heavy_noise(seeds[0], (TOKENS, D), 1.0, 24.0, ((0, 256),), (0, 1, 256, 6.0))
    router_logit = gaussian(seeds[1], (TOKENS,), 1.5, 6.0, ((0, 256),), jnp.float32)
    chosen_index = draw_chosen_index(jax.random.fold_in(seeds[8], 71), 0)
    chosen_count = draw_chosen_count(jax.random.fold_in(seeds[8], 71), 0)
    out_weight = gaussian(seeds[4], (HQ * HD, D), (HQ * HD) ** -0.5, 0.125, ((0, 8),))
    queries = draw_queries(jax.random.fold_in(seeds[8], 71), 0)
    key_rows = draw_key_rows(jax.random.fold_in(seeds[8], 71), 0)
    value_rows = gaussian(seeds[7], (SEL, HQ * HD), 1.0, 6.0, ((0, 32), (1, 8)))
    return dict(output_grad=output_grad, router_logit=router_logit, chosen_index=chosen_index, chosen_count=chosen_count, out_weight=out_weight, queries=queries, key_rows=key_rows, value_rows=value_rows)


def product(left, right):
    return jnp.dot(left.astype(jnp.float32), right.astype(jnp.float32), preferred_element_type=jnp.float32, precision=lax.Precision.HIGHEST)


def reference(output_grad, router_logit, chosen_index, chosen_count, out_weight, queries, key_rows, value_rows):
    factor = HD ** -0.5
    slot_ids = jnp.arange(CAP, dtype=jnp.int32)
    live_slots = slot_ids[None, :] < chosen_count[:, None]
    positions = jnp.arange(SHARDS, dtype=jnp.int32)[:, None] * TOK_DEV + chosen_index.reshape(SHARDS, CAP)
    picked_slots = jnp.nonzero(live_slots.reshape(-1), size=SEL)[0].astype(jnp.int32)
    chosen_pos = positions.reshape(-1)[picked_slots].astype(jnp.int32)
    grad_rows = output_grad[chosen_pos]
    sigmoid_val = jax.nn.sigmoid(router_logit[chosen_pos])
    gate_bf = lax.optimization_barrier(sigmoid_val.astype(jnp.bfloat16))
    gate_row = gate_bf.astype(jnp.float32)
    row_ids = jnp.arange(SEL, dtype=jnp.int32)
    allowed = row_ids[:, None] >= row_ids[None, :]

    def by_heads(rows):
        return rows.reshape(SEL, HQ, HD).transpose(1, 0, 2)

    def from_heads(stacked):
        return stacked.transpose(1, 0, 2).reshape(SEL, HQ * HD)

    def forward_head(inputs):
        query_head, key_head, value_head = inputs
        scores = product(query_head, key_head.T) * factor
        masked = jnp.where(allowed, scores, -jnp.inf)
        row_max = jnp.max(masked, axis=1)
        log_norm = row_max + jnp.log(jnp.sum(jnp.exp(masked - row_max[:, None]), axis=1))
        weights = jnp.exp(masked - log_norm[:, None]).astype(jnp.bfloat16)
        return product(weights, value_head).astype(jnp.bfloat16), log_norm

    query_stack = by_heads(queries)
    key_stack = by_heads(key_rows)
    value_stack = by_heads(value_rows)
    out_stack, norm_stack = lax.map(forward_head, (query_stack, key_stack, value_stack))
    attn_out = from_heads(out_stack)
    projected = product(grad_rows, out_weight.T)
    router_part = jnp.sum(attn_out.astype(jnp.float32) * projected, axis=1)
    out_grad_bf = (gate_row[:, None] * projected).astype(jnp.bfloat16)
    gated_out = (gate_row[:, None] * attn_out.astype(jnp.float32)).astype(jnp.bfloat16)
    out_weight_grad = product(grad_rows.T, gated_out)

    def backward_head(inputs):
        query_head, key_head, value_head, grad_head, out_head, log_norm = inputs
        scores = product(query_head, key_head.T) * factor
        weights = jnp.exp(jnp.where(allowed, scores - log_norm[:, None], -jnp.inf))
        weights_bf = weights.astype(jnp.bfloat16)
        row_delta = jnp.sum(grad_head.astype(jnp.float32) * out_head.astype(jnp.float32), axis=1)
        grad_weights = product(grad_head, value_head.T)
        grad_scores = (weights * (grad_weights - row_delta[:, None])).astype(jnp.bfloat16)
        query_part = (product(grad_scores, key_head) * factor).astype(jnp.bfloat16)
        key_part = (product(grad_scores.T, query_head) * factor).astype(jnp.bfloat16)
        value_part = product(weights_bf.T, grad_head).astype(jnp.bfloat16)
        return query_part, key_part, value_part

    grads = lax.map(backward_head, (query_stack, key_stack, value_stack, by_heads(out_grad_bf), out_stack, norm_stack))
    logit_term = router_part * sigmoid_val * (1.0 - sigmoid_val)
    logit_grad = jnp.zeros((TOKENS,), jnp.float32).at[chosen_pos].set(logit_term)
    return from_heads(grads[0]), from_heads(grads[1]), from_heads(grads[2]), out_weight_grad, logit_grad
```

```python
import jax
import jax.numpy as jnp
from jax import lax
from jax.experimental import pallas as pl
from jax.experimental.pallas import tpu as pltpu
from jax.sharding import PartitionSpec as P

HD = 128
NY = 4
MESH = pl.DeviceIdType.MESH
BF = jnp.bfloat16
F32 = jnp.float32
NEG = -1e30


def dot(a, b, ca, cb, precision=None):
    return lax.dot_general(
        a, b, (((ca,), (cb,)), ((), ())), preferred_element_type=F32, precision=precision
    )


class Layout:
    def __init__(self, nz, nx, tok, cap, d):
        self.nz, self.nx, self.tok, self.cap, self.d = nz, nx, tok, cap, d
        self.dh = d // 2
        self.hz = nz // 2
        self.far = nz // 2
        self.near = nz - 1 - self.far

    def scratch(self):
        nz, nx, cap, d, dh, hz = self.nz, self.nx, self.cap, self.d, self.dh, self.hz
        v = pltpu.VMEM
        steps = max(self.far, 1)
        names = dict(
            grads=v((self.tok, d), BF),
            weight=v((2, 2 * HD, dh), BF),
            picked=v((2, cap, dh + HD), BF),
            rows=v((2 * nx * cap, dh + HD), BF),
            block=v((HD, dh + HD), BF),
            slice_out=v((NY, HD, (hz + 1) * HD), BF),
            slices=v((NY * HD, (hz + 1) * HD), BF),
            proj_part=v((2, HD, 2 * HD), F32),
            proj_in=v((HD, 2 * HD), F32),
            proj=v((HD, 2 * HD), F32),
            go_out=v((2, HD, HD), BF),
            qh=v((NY, HD, HD), BF),
            goh=v((NY, HD, HD), BF),
            kk=v((nz, 2 * HD, HD), BF),
            vv=v((nz, 2 * HD, HD), BF),
            soft=v((NY, HD + 16, HD), F32),
            soft_in=v((NY, HD + 16, HD), F32),
            lse=v((NY, 8, HD), F32),
            delta=v((NY, 8, HD), F32),
            outs=v((NY, NY * HD, HD), BF),
            gated=v((NY * HD, NY * HD), BF),
            dqt=v((NY, HD, HD), F32),
            dkp=v((nz, 2 * HD, HD), F32),
            dvp=v((nz, 2 * HD, HD), F32),
            dwp=v((2, hz, HD, 2 * HD), F32),
            kv_send=v((2, 2, steps, 2 * HD, HD), BF),
            kv_recv=v((2, 2, steps, 2 * HD, HD), BF),
            dw_send=v((2, 2, steps, HD, 2 * HD), BF),
            dw_recv=v((2, 2, steps, HD, 2 * HD), BF),
            kv_fin=v((2, 2, HD, HD), BF),
            kv_land=v((2, 2, HD, HD), BF),
            dq_out=v((NY, HD, HD), BF),
            dq_land=v((2, 2, HD, HD), BF),
            dw_fin=v((2, HD, 2 * HD), F32),
            dw_land=v((HD, 2 * HD), F32),
            router=v((8, HD), F32),
            router_in=v((2 * nx, 8, HD), F32),
        )
        return names


def fused(lay, names, *refs):
    (g_ref, logit_ref, idx_ref, cnt_ref, w_ref, q_ref, k_ref, v_ref) = refs[:8]
    (dq_ref, dk_ref, dv_ref, dw_ref, lg_ref) = refs[8:13]
    buf = dict(zip(names, refs[13 : 13 + len(names)]))
    send_sems, recv_sems, local_sems = refs[13 + len(names) :]
    nz, nx, cap, dh, hz = lay.nz, lay.nx, lay.cap, lay.dh, lay.hz
    shards = 2 * nx
    factor = HD ** (-0.5)

    s, g = lax.axis_index("seq"), lax.axis_index("grp")
    z, y, x, c = s // NY, s % NY, g // 2, g % 2
    sib = 1 - c

    def dev(z_, y_, x_, c_):
        return (z_ * NY + y_, x_ * 2 + c_)

    up, down = (z + 1) % nz, (z + nz - 1) % nz
    dev_up, dev_down = dev(up, y, x, c), dev(down, y, x, c)
    dev_sib = dev(z, y, x, sib)

    counter = {"send": 0, "recv": 0, "local": 0}

    def alloc(kind, n=1):
        first = counter[kind]
        counter[kind] += n
        return first

    sent = []

    def send(src, dst, recv_id, to, unless=None):
        copy = pltpu.make_async_remote_copy(
            src_ref=src,
            dst_ref=dst,
            send_sem=send_sems.at[alloc("send")],
            recv_sem=recv_sems.at[recv_id],
            device_id=to,
            device_id_type=MESH,
        )
        sent.append((unless, copy))
        if unless is None:
            copy.start()
        else:
            pl.when(jnp.logical_not(unless))(lambda: copy.start())

    def recv(dst, recv_id, unless=None):
        copy = pltpu.make_async_remote_copy(
            src_ref=dst,
            dst_ref=dst,
            send_sem=send_sems.at[0],
            recv_sem=recv_sems.at[recv_id],
            device_id=dev_sib,
            device_id_type=MESH,
        )
        if unless is None:
            copy.wait_recv()
        else:
            pl.when(jnp.logical_not(unless))(lambda: copy.wait_recv())

    grads_in = pltpu.make_async_copy(g_ref, buf["grads"], local_sems.at[alloc("local")])
    grads_in.start()
    own_half = pl.multiple_of(c * dh, HD)
    other_half = pl.multiple_of(sib * dh, HD)
    weight_in = pltpu.make_async_copy(
        w_ref.at[:, pl.ds(own_half, dh)], buf["weight"].at[c], local_sems.at[alloc("local")]
    )
    weight_in.start()

    partners = [dev_sib, dev_up, dev_down]
    for dy in range(1, NY):
        for cc in range(2):
            partners.append(dev(z, (y + dy) % NY, x, cc))
    for dx in range(1, nx):
        for cc in range(2):
            partners.append(dev(z, y, (x + dx) % nx, cc))
    barrier = pltpu.get_barrier_semaphore()
    for partner in partners:
        pl.semaphore_signal(barrier, inc=1, device_id=partner, device_id_type=MESH)
    pl.semaphore_wait(barrier, len(partners))

    half_y = y // 2
    id_k, id_v, id_q = alloc("recv", 2), alloc("recv", 2), alloc("recv", NY)
    own_copies = []
    for j in range(2):
        y_to = 2 * c + j
        own = jnp.logical_and(y_to == y, half_y == c)
        cols = slice(j * HD, (j + 1) * HD)
        part = pl.ds(pl.multiple_of((y % 2) * HD, HD), HD)
        for src, name, base in ((k_ref, "kk", id_k), (v_ref, "vv", id_v)):
            dst = buf[name].at[z, part, :]
            send(src.at[:, cols], dst, base + y % 2, dev(z, y_to, x, half_y), own)
            own_copies.append(
                (own, pltpu.make_async_copy(src.at[:, cols], dst, local_sems.at[alloc("local")]))
            )
            pl.when(own)(lambda: own_copies[-1][1].start())
    for j in range(2):
        y_to = 2 * c + j
        cols = slice(j * HD, (j + 1) * HD)
        for cc in range(2):
            own = jnp.logical_and(y_to == y, c == cc)
            dst = buf["qh"].at[y]
            send(q_ref.at[:, cols], dst, id_q + y, dev(z, y_to, x, cc), own)
            own_copies.append(
                (own, pltpu.make_async_copy(q_ref.at[:, cols], dst, local_sems.at[alloc("local")]))
            )
            pl.when(own)(lambda: own_copies[-1][1].start())
    id_w = alloc("recv")
    send(w_ref.at[:, pl.ds(other_half, dh)], buf["weight"].at[c], id_w, dev_sib)

    slot = lax.broadcasted_iota(jnp.int32, (cap, HD), 0)
    lane = lax.broadcasted_iota(jnp.int32, (cap, HD), 1)
    index = jnp.zeros((cap, HD), jnp.int32)
    for j in range(cap):
        index = jnp.where(slot == j, idx_ref[j], index)
    first = s * shards
    starts, total = [], jnp.int32(0)
    counts = []
    for i in range(shards):
        starts.append(total)
        counts.append(cnt_ref[first + i])
        total = total + counts[-1]
    own_start, own_count = jnp.int32(0), jnp.int32(0)
    for i in range(shards):
        own_start = jnp.where(g == i, starts[i], own_start)
        own_count = jnp.where(g == i, counts[i], own_count)
    pick = jnp.logical_and(index == lane, slot < own_count)
    pick_bf = pick.astype(F32).astype(BF)
    logit_row = logit_ref[...]
    chosen_logit = jnp.sum(
        jnp.where(pick, jnp.broadcast_to(logit_row, (cap, HD)), 0.0), axis=1, keepdims=True
    )
    gate_col = 1.0 / (1.0 + jnp.exp(-chosen_logit))
    gate_tile = jnp.broadcast_to(gate_col, (cap, HD)).astype(BF)
    grads_in.wait()
    for h in range(2):
        buf["picked"][h, :, pl.ds(dh, HD)] = gate_tile
    for h in range(2):
        buf["picked"][h, :, pl.ds(0, dh)] = dot(
            pick_bf, buf["grads"][:, h * dh : (h + 1) * dh], 1, 0
        ).astype(BF)

    right, left = (x + 1) % nx, (x + nx - 1) % nx
    rows = buf["rows"]

    def row_slot(shard):
        return rows.at[pl.ds(pl.multiple_of(shard * cap, cap), cap), :]

    id_rows_sib = alloc("recv")
    id_from_left, id_from_right = alloc("recv", 2), alloc("recv", 2)
    id_far_left, id_far_right = alloc("recv"), alloc("recv")
    send(buf["picked"].at[sib], row_slot(g), id_rows_sib, dev_sib)
    if nx > 1:
        for h in range(2):
            send(buf["picked"].at[h], row_slot(g), id_from_left + c, dev(z, y, right, h))
            send(buf["picked"].at[h], row_slot(g), id_from_right + c, dev(z, y, left, h))
    rows[pl.ds(pl.multiple_of(g * cap, cap), cap), :] = buf["picked"][c]

    buf["dkp"][...] = jnp.zeros_like(buf["dkp"])
    buf["dvp"][...] = jnp.zeros_like(buf["dvp"])
    buf["dqt"][...] = jnp.zeros_like(buf["dqt"])
    soft = buf["soft"]
    soft[...] = jnp.zeros_like(soft)
    for i in range(NY):
        soft[i, HD : HD + 8, :] = jnp.full((8, HD), NEG, F32)

    kv_own = pl.ds(pl.multiple_of(0, HD), HD)
    for j in range(2):
        own = jnp.logical_and(c == half_y, y == 2 * c + j)
        part = slice(j * HD, (j + 1) * HD)
        recv(buf["kk"].at[z, part, :], id_k + j, own)
        recv(buf["vv"].at[z, part, :], id_v + j, own)
    for own, copy in own_copies:
        pl.when(own)(lambda: copy.wait())

    ring = (("kk", lay.far, lay.near), ("vv", lay.near, lay.far))
    id_up = {n: alloc("recv", lay.far + 1) for n in ("kk", "vv")}
    id_down = {n: alloc("recv", lay.far + 1) for n in ("kk", "vv")}

    def ring_send(t):
        for name, n_up, n_down in ring:
            if t <= n_up:
                b = (z + nz - t + 1) % nz
                send(buf[name].at[b], buf[name].at[b], id_up[name] + t, dev_up)
            if t <= n_down:
                b = (z + t - 1) % nz
                send(buf[name].at[b], buf[name].at[b], id_down[name] + t, dev_down)

    def ring_recv(t):
        for name, n_up, n_down in ring:
            if t <= n_up:
                recv(buf[name].at[(z + nz - t) % nz], id_up[name] + t)
            if t <= n_down:
                recv(buf[name].at[(z + t) % nz], id_down[name] + t)

    ring_send(1)

    def allowed(i):
        key = c * 2 * HD + lax.broadcasted_iota(jnp.int32, (2 * HD, HD), 0)
        query = i * HD + lax.broadcasted_iota(jnp.int32, (2 * HD, HD), 1)
        return key <= query

    def forward_block(b, diagonal):
        keys, values = buf["kk"][b], buf["vv"][b]
        for i in range(NY):
            scores = dot(keys, buf["qh"][i], 1, 1) * factor
            if diagonal:
                scores = jnp.where(allowed(i), scores, NEG)
            old = soft[i, HD : HD + 1, :]
            new = jnp.maximum(old, jnp.max(scores, axis=0, keepdims=True))
            weights = jnp.exp(scores - new)
            decay = jnp.exp(old - new)
            norm = soft[i, HD + 8 : HD + 9, :] * decay + jnp.sum(weights, axis=0, keepdims=True)
            soft[i, 0:HD, :] = soft[i, 0:HD, :] * decay + dot(values, weights.astype(BF), 0, 0)
            soft[i, HD : HD + 1, :] = new
            soft[i, HD + 8 : HD + 9, :] = norm

    def forward_pair(t):
        pl.when(z >= t)(lambda: forward_block((z + nz - t) % nz, False))
        if t <= nz - 1 - t:
            pl.when(z + t >= nz)(lambda: forward_block((z + t) % nz, False))

    for i in range(NY):
        own = jnp.logical_and(c == half_y, y == i)
        recv(buf["qh"].at[i], id_q + i, own)
    forward_block(z, True)

    def rows_step_two():
        if nx == 1:
            return
        for cc in range(2):
            recv(row_slot(2 * left + cc), id_from_left + cc)
            recv(row_slot(2 * right + cc), id_from_right + cc)
        send(row_slot(2 * left), row_slot(2 * left), id_far_left, dev(z, y, right, c))
        send(row_slot(2 * right + 1), row_slot(2 * right + 1), id_far_right, dev(z, y, left, c))

    id_slice, id_proj, id_go = alloc("recv", NY), alloc("recv"), alloc("recv", NY)
    row_iota = lax.broadcasted_iota(jnp.int32, (HD, shards * cap), 0)

    def project():
        recv(row_slot(2 * x + sib), id_rows_sib)
        if nx > 1:
            opposite = (x + 2) % nx
            recv(row_slot(2 * opposite), id_far_left)
            recv(row_slot(2 * opposite + 1), id_far_right)
        lanes = lax.broadcasted_iota(jnp.int32, (1, shards * cap), 1)
        place = jnp.full((1, shards * cap), -1, jnp.int32)
        for i in range(shards):
            within = lanes - i * cap
            live = jnp.logical_and(within >= 0, within < counts[i])
            place = jnp.where(live, starts[i] + within, place)
        compact = (row_iota == place).astype(F32).astype(BF)
        block = buf["block"]
        block[...] = dot(compact, rows[...], 1, 0).astype(BF)
        for i in range(hz):
            for yy in range(NY):
                k = i * NY + yy
                buf["slice_out"][yy, :, i * HD : (i + 1) * HD] = block[:, k * HD : (k + 1) * HD]
        for yy in range(NY):
            buf["slice_out"][yy, :, hz * HD :] = block[:, dh:]
        weight_in.wait()
        recv(buf["weight"].at[sib], id_w)
        part = buf["proj_part"]
        part[sib] = dot(block[:, :dh], buf["weight"][sib], 1, 1)
        send(part.at[sib], buf["proj_in"], id_proj, dev_sib)
        part[c] = dot(block[:, :dh], buf["weight"][c], 1, 1)

    def out_gradient():
        recv(buf["proj_in"], id_proj)
        total = buf["proj_part"][c] + buf["proj_in"][...]
        buf["proj"][...] = total
        gate = buf["block"][:, dh:].astype(F32)
        for j in range(2):
            buf["go_out"][j] = (gate * total[:, j * HD : (j + 1) * HD]).astype(BF)
        for j in range(2):
            y_to = 2 * c + j
            for cc in range(2):
                own = jnp.logical_and(y_to == y, c == cc)
                send(buf["go_out"].at[j], buf["goh"].at[y], id_go + y, dev(z, y_to, x, cc), own)

                @pl.when(own)
                def _():
                    buf["goh"][y] = buf["go_out"][j]

        for dy in range(1, NY):
            y_to = (y + dy) % NY
            mine = pl.ds(pl.multiple_of(y * HD, HD), HD)
            send(
                buf["slice_out"].at[y_to],
                buf["slices"].at[mine, :],
                id_slice + y,
                dev(z, y_to, x, c),
            )
        buf["slices"][mine, :] = buf["slice_out"][y]

    for t in range(1, lay.far + 1):
        ring_recv(t)
        if t < lay.far:
            ring_send(t + 1)
        if t == 1:
            rows_step_two()
        if t == min(2, lay.far):
            project()
        if t == min(3, lay.far):
            out_gradient()
        forward_pair(t)

    id_soft = alloc("recv")
    send(soft, buf["soft_in"], id_soft, dev_sib)
    for i in range(NY):
        own = jnp.logical_and(c == half_y, y == i)
        recv(buf["goh"].at[i], id_go + i, own)
    recv(buf["soft_in"], id_soft)
    soft_in = buf["soft_in"]
    for i in range(NY):
        max_a, max_b = soft[i, HD : HD + 1, :], soft_in[i, HD : HD + 1, :]
        top = jnp.maximum(max_a, max_b)
        scale_a, scale_b = jnp.exp(max_a - top), jnp.exp(max_b - top)
        norm = soft[i, HD + 8 : HD + 9, :] * scale_a + soft_in[i, HD + 8 : HD + 9, :] * scale_b
        out_t = (soft[i, 0:HD, :] * scale_a + soft_in[i, 0:HD, :] * scale_b) / norm
        out = out_t.T.astype(BF)
        buf["outs"][y, i * HD : (i + 1) * HD, :] = out
        buf["lse"][i, 0:1, :] = top + jnp.log(norm)
        terms = out.astype(F32) * buf["goh"][i].astype(F32)
        buf["delta"][i, 0:1, :] = jnp.sum(terms.T, axis=0, keepdims=True)

    id_outs = alloc("recv", NY)
    for dy in range(1, NY):
        y_to = (y + dy) % NY
        send(buf["outs"].at[y], buf["outs"].at[y], id_outs + y, dev(z, y_to, x, c))

    def backward_block(b, diagonal):
        keys, values = buf["kk"][b], buf["vv"][b]
        for i in range(NY):
            queries, go = buf["qh"][i], buf["goh"][i]
            scores = dot(keys, queries, 1, 1) * factor
            weights = jnp.exp(scores - buf["lse"][i, 0:1, :])
            if diagonal:
                weights = jnp.where(allowed(i), weights, 0.0)
            grad_weights = dot(values, go, 1, 1)
            grad_scores = (weights * (grad_weights - buf["delta"][i, 0:1, :])).astype(BF)
            value_part = dot(weights.astype(BF), go, 1, 0)
            key_part = dot(grad_scores, queries, 1, 0)
            if i == 0:
                buf["dvp"][b] = value_part
                buf["dkp"][b] = key_part
            else:
                buf["dvp"][b] += value_part
                buf["dkp"][b] += key_part
            buf["dqt"][i] += dot(keys, grad_scores, 0, 0)

    def backward_pair(t):
        pl.when(z >= t)(lambda: backward_block((z + nz - t) % nz, False))
        if t <= nz - 1 - t:
            pl.when(z + t >= nz)(lambda: backward_block((z + t) % nz, False))

    hops = ((lay.far, lay.near), (lay.near, lay.far))
    id_kv = alloc("recv", 4 * (lay.far + 1))
    id_dw = alloc("recv", 4 * (lay.far + 1))

    def target(direction, d):
        return (z + nz - d) % nz if direction == 0 else (z + d) % nz

    def reduce_step(d, dw):
        for kind in range(2):
            for direction in range(2):
                n = hops[kind][direction]
                if d > n:
                    continue
                t = n - d
                b = target(direction, d)
                out, inc = (
                    (buf["dw_send"], buf["dw_recv"]) if dw else (buf["kv_send"], buf["kv_recv"])
                )
                base = (id_dw if dw else id_kv) + (2 * kind + direction) * (lay.far + 1)
                to = dev_down if direction == 0 else dev_up
                skip = b // hz != c if dw else None

                def value(kind=kind, direction=direction, t=t, b=b, inc=inc):
                    if dw:
                        mine = buf["dwp"][kind, b % hz]
                    else:
                        mine = (buf["dkp"] if kind == 0 else buf["dvp"])[b]
                    if t > 0:
                        mine = mine + inc[kind, direction, t - 1].astype(F32)
                    out[kind, direction, t] = mine.astype(BF)

                if t > 0:
                    recv(inc.at[kind, direction, t - 1], base + t - 1, skip)
                if skip is None:
                    value()
                else:
                    pl.when(jnp.logical_not(skip))(value)
                send(out.at[kind, direction, t], inc.at[kind, direction, t], base + t, to, skip)

    def reduce_last(dw):
        results = []
        skip = z // hz != c if dw else None
        for kind in range(2):
            for direction in range(2):
                n = hops[kind][direction]
                inc = buf["dw_recv"] if dw else buf["kv_recv"]
                base = (id_dw if dw else id_kv) + (2 * kind + direction) * (lay.far + 1)
                if n > 0:
                    recv(inc.at[kind, direction, n - 1], base + n - 1, skip)

        def value(kind):
            if dw:
                mine = buf["dwp"][kind, z % hz]
            else:
                mine = (buf["dkp"] if kind == 0 else buf["dvp"])[z]
            for direction in range(2):
                n = hops[kind][direction]
                inc = buf["dw_recv"] if dw else buf["kv_recv"]
                if n > 0:
                    mine = mine + inc[kind, direction, n - 1].astype(F32)
            return mine

        return value, skip

    id_router = alloc("recv", shards)

    def weight_gradient():
        for dy in range(1, NY):
            yy = (y + dy) % NY
            recv(buf["outs"].at[yy], id_outs + yy)
            recv(buf["slices"].at[pl.ds(pl.multiple_of(yy * HD, HD), HD), :], id_slice + yy)
        gate = buf["slices"][:, hz * HD :].astype(F32)
        for h in range(NY):
            buf["gated"][:, h * HD : (h + 1) * HD] = (gate * buf["outs"][h].astype(F32)).astype(BF)
        for i in range(hz):
            for kind in range(2):
                buf["dwp"][kind, i] = dot(
                    buf["slices"][:, i * HD : (i + 1) * HD],
                    buf["gated"][:, kind * 2 * HD : (kind + 1) * 2 * HD],
                    0,
                    0,
                )

    def router_send():
        mine = pl.ds(pl.multiple_of(y * HD, HD), HD)
        part = jnp.zeros((HD, HD), F32)
        for j in range(2):
            part = part + buf["outs"][2 * c + j, mine, :].astype(F32) * buf["proj"][
                :, j * HD : (j + 1) * HD
            ]
        row = jnp.sum(part.T, axis=0, keepdims=True)
        buf["router"][...] = jnp.broadcast_to(row, (8, HD))
        buf["router_in"][g] = jnp.broadcast_to(row, (8, HD))
        for dx in range(nx):
            for cc in range(2):
                if dx == 0 and cc == 1:
                    continue
                to = dev_sib if dx == 0 else dev(z, y, (x + dx) % nx, cc)
                send(buf["router"], buf["router_in"].at[g], id_router + g, to)

    def router_last():
        for dx in range(nx):
            for cc in range(2):
                if dx == 0 and cc == 1:
                    continue
                src = 2 * x + sib if dx == 0 else 2 * ((x + dx) % nx) + cc
                recv(buf["router_in"].at[src], id_router + src)
        total = buf["router_in"][0]
        for i in range(1, shards):
            total = total + buf["router_in"][i]
        token_row = lax.broadcasted_iota(jnp.int32, (HD, cap), 0)
        token_slot = lax.broadcasted_iota(jnp.int32, (HD, cap), 1)
        own = jnp.logical_and(token_row == own_start + token_slot, token_slot < own_count)
        spread = dot(own.astype(F32).astype(BF), pick_bf, 1, 0)
        placed = dot(total, spread, 1, 0, lax.Precision.HIGHEST)
        sig = 1.0 / (1.0 + jnp.exp(-logit_row))
        lg_ref[...] = placed[0:1, :] * sig * (1.0 - sig)

    id_kv_fin, id_dq = alloc("recv", 4), alloc("recv", 4)
    id_dw_fin = alloc("recv")

    def send_key_value_grads():
        value, _ = reduce_last(False)
        for kind in range(2):
            final = value(kind)
            if kind == 0:
                final = final * factor
            for j in range(2):
                buf["kv_fin"][kind, j] = final[j * HD : (j + 1) * HD, :].astype(BF)
        side = y % 2
        for kind in range(2):
            for j in range(2):
                y_to = 2 * c + j
                own = jnp.logical_and(y_to == y, half_y == c)
                send(
                    buf["kv_fin"].at[kind, j],
                    buf["kv_land"].at[kind, side],
                    id_kv_fin + 2 * kind + side,
                    dev(z, y_to, x, half_y),
                    own,
                )

                @pl.when(own)
                def _():
                    buf["kv_land"][kind, side] = buf["kv_fin"][kind, j]

    def send_query_grads():
        side = y % 2
        for i in range(NY):
            buf["dq_out"][i] = (buf["dqt"][i].T * factor).astype(BF)
            own = jnp.logical_and(y == i, half_y == c)
            send(
                buf["dq_out"].at[i],
                buf["dq_land"].at[side, c],
                id_dq + 2 * side + c,
                dev(z, i, x, half_y),
                own,
            )

            @pl.when(own)
            def _():
                buf["dq_land"][side, c] = buf["dq_out"][i]

    dw_delay = 2
    for d in range(lay.far, -1, -1):
        if d > 0:
            backward_pair(d)
            reduce_step(d, False)
        else:
            backward_block(z, True)
            send_query_grads()
        if d == lay.far - 1 or lay.far == 1 and d == 0:
            weight_gradient()
            router_send()
        if d + dw_delay - 1 <= lay.far and d + dw_delay - 1 > 0 and lay.far > 1:
            reduce_step(d + dw_delay - 1, True)
    if lay.far == 1:
        reduce_step(1, True)
    send_key_value_grads()

    value, skip = reduce_last(True)

    @pl.when(jnp.logical_not(skip))
    def _():
        for kind in range(2):
            buf["dw_fin"][kind] = value(kind)

    holder = jnp.logical_not(skip)
    send(buf["dw_fin"].at[sib], buf["dw_land"], id_dw_fin, dev_sib, skip)
    router_last()

    for j in range(2):
        for cc in range(2):
            own = jnp.logical_and(y == 2 * c + j, c == cc)
            recv(buf["dq_land"].at[j, cc], id_dq + 2 * j + cc, own)
        dq_ref[:, j * HD : (j + 1) * HD] = (
            buf["dq_land"][j, 0].astype(F32) + buf["dq_land"][j, 1].astype(F32)
        ).astype(BF)
    for kind, ref in ((0, dk_ref), (1, dv_ref)):
        for j in range(2):
            own = jnp.logical_and(y == 2 * c + j, half_y == c)
            recv(buf["kv_land"].at[kind, j], id_kv_fin + 2 * kind + j, own)
            ref[:, j * HD : (j + 1) * HD] = buf["kv_land"][kind, j]

    recv(buf["dw_land"], id_dw_fin, holder)

    @pl.when(holder)
    def _():
        dw_ref[...] = buf["dw_fin"][c]

    @pl.when(skip)
    def _():
        dw_ref[...] = buf["dw_land"][...]

    for unless, copy in sent:
        if unless is None:
            copy.wait_send()
        else:
            pl.when(jnp.logical_not(unless))(lambda: copy.wait_send())

    lay.used = dict(counter)


SEMS = 160


def shards_fn(nz, nx):
    def run(grad, logit, index, count, weight, q, k, v):
        lay = Layout(nz, nx, grad.shape[0], index.shape[0], grad.shape[1])
        scratch = lay.scratch()
        names = list(scratch)
        any_ = pl.BlockSpec(memory_space=pl.ANY)
        smem = pl.BlockSpec(memory_space=pltpu.SMEM)
        vmem = pl.BlockSpec(memory_space=pltpu.VMEM)

        def kernel(*refs):
            fused(lay, names, *refs)

        out = pl.pallas_call(
            kernel,
            out_shape=(
                jax.ShapeDtypeStruct(q.shape, BF),
                jax.ShapeDtypeStruct(q.shape, BF),
                jax.ShapeDtypeStruct(q.shape, BF),
                jax.ShapeDtypeStruct((HD, q.shape[1]), F32),
                jax.ShapeDtypeStruct((1, logit.shape[0]), F32),
            ),
            in_specs=[any_, vmem, smem, smem, any_, any_, any_, any_],
            out_specs=(vmem,) * 5,
            scratch_shapes=list(scratch.values())
            + [
                pltpu.SemaphoreType.DMA((SEMS,)),
                pltpu.SemaphoreType.DMA((SEMS,)),
                pltpu.SemaphoreType.DMA((16,)),
            ],
            compiler_params=pltpu.CompilerParams(
                collective_id=0, has_side_effects=True, vmem_limit_bytes=48 * 1024 * 1024
            ),
            name="routed_backward",
        )(grad, logit.reshape(1, -1), index, count, weight, q, k, v)
        return (*out[:4], out[4].reshape(-1))

    return run


def solution(mesh):
    nz = mesh.shape["seq"] // NY
    nx = mesh.shape["grp"] // 2
    placed = (
        P(("seq", "grp"), None),
        P(("seq", "grp")),
        P(("seq", "grp")),
        P(),
        P("grp", None),
        P("seq", "grp"),
        P("seq", "grp"),
        P("seq", "grp"),
    )
    return jax.shard_map(
        shards_fn(nz, nx),
        mesh=mesh,
        in_specs=placed,
        out_specs=(
            P("seq", "grp"),
            P("seq", "grp"),
            P("seq", "grp"),
            P("seq", "grp"),
            P(("seq", "grp")),
        ),
        check_vma=False,
    )
```

```python
import jax
import jax.numpy as jnp
from jax import lax
from jax.experimental import pallas as pl
from jax.experimental.pallas import tpu as pltpu
from jax.sharding import PartitionSpec as P

HD = 128
NY = 4
MESH = pl.DeviceIdType.MESH
BF = jnp.bfloat16
F32 = jnp.float32
NEG = -1e30


def dot(a, b, ca, cb, precision=None):
    return lax.dot_general(
        a, b, (((ca,), (cb,)), ((), ())), preferred_element_type=F32, precision=precision
    )


class Layout:
    def __init__(self, nz, nx, tok, cap, d):
        self.nz, self.nx, self.tok, self.cap, self.d = nz, nx, tok, cap, d
        self.dh = d // 2
        self.hz = nz // 2
        self.far = nz // 2
        self.near = nz - 1 - self.far

    def scratch(self):
        nz, nx, cap, d, dh, hz = self.nz, self.nx, self.cap, self.d, self.dh, self.hz
        v = pltpu.VMEM
        steps = max(self.far, 1)
        names = dict(
            grads=v((self.tok, d), BF),
            weight=v((2, 2 * HD, dh), BF),
            picked=v((2, cap, dh + HD), BF),
            rows=v((2 * nx * cap, dh + HD), BF),
            block=v((HD, dh + HD), BF),
            slice_out=v((NY, HD, hz * HD), BF),
            slices=v((NY * HD, hz * HD), BF),
            gates=v((NY, 8, HD), F32),
            proj_part=v((2, HD, 2 * HD), F32),
            proj_in=v((HD, 2 * HD), F32),
            go_out=v((2, HD, HD), BF),
            qh=v((NY, HD, HD), BF),
            goh=v((NY, HD, HD), BF),
            kk=v((nz, 2 * HD, HD), BF),
            vv=v((nz, 2 * HD, HD), BF),
            soft=v((NY, HD + 16, HD), F32),
            soft_in=v((NY, HD + 16, HD), F32),
            lse=v((NY, 8, HD), F32),
            delta=v((NY, 8, HD), F32),
            outs=v((NY * HD, NY * HD), BF),
            dqt=v((NY, HD, HD), F32),
            dkp=v((nz, 2 * HD, HD), F32),
            dvp=v((nz, 2 * HD, HD), F32),
            dwp=v((2, hz, HD, 2 * HD), F32),
            kv_send=v((2, 2, steps, 2 * HD, HD), BF),
            kv_recv=v((2, 2, steps, 2 * HD, HD), BF),
            dw_send=v((2, 2, steps, HD, 2 * HD), BF),
            dw_recv=v((2, 2, steps, HD, 2 * HD), BF),
            kv_fin=v((2, 2, HD, HD), BF),
            dq_out=v((NY, HD, HD), BF),
            dw_fin=v((2, HD, 2 * HD), F32),
            router_out=v((NY, 8, HD), F32),
            router_y=v((NY, 8, HD), F32),
            router_x=v((nx, 8, HD), F32),
        )
        return names


def fused(lay, names, *refs):
    (g_ref, logit_ref, idx_ref, cnt_ref, w_ref, q_ref, k_ref, v_ref) = refs[:8]
    (dq_land, kv_land, dw_land, lg_ref) = refs[8:12]
    buf = dict(zip(names, refs[12 : 12 + len(names)]))
    send_sems, recv_sems, local_sems = refs[12 + len(names) :]
    nz, nx, cap, dh, hz = lay.nz, lay.nx, lay.cap, lay.dh, lay.hz
    shards = 2 * nx
    factor = HD ** (-0.5)

    s, g = lax.axis_index("seq"), lax.axis_index("grp")
    z, y, x, c = s // NY, s % NY, g // 2, g % 2
    sib = 1 - c

    def dev(z_, y_, x_, c_):
        return (z_ * NY + y_, x_ * 2 + c_)

    up, down = (z + 1) % nz, (z + nz - 1) % nz
    dev_up, dev_down = dev(up, y, x, c), dev(down, y, x, c)
    dev_sib = dev(z, y, x, sib)

    counter = {"send": 0, "recv": 0, "local": 0}

    def alloc(kind, n=1):
        first = counter[kind]
        counter[kind] += n
        return first

    sent = []

    def send(src, dst, recv_id, to, unless=None):
        copy = pltpu.make_async_remote_copy(
            src_ref=src,
            dst_ref=dst,
            send_sem=send_sems.at[alloc("send")],
            recv_sem=recv_sems.at[recv_id],
            device_id=to,
            device_id_type=MESH,
        )
        sent.append((unless, copy))
        if unless is None:
            copy.start()
        else:
            pl.when(jnp.logical_not(unless))(lambda: copy.start())

    def recv(dst, recv_id, unless=None):
        copy = pltpu.make_async_remote_copy(
            src_ref=dst,
            dst_ref=dst,
            send_sem=send_sems.at[0],
            recv_sem=recv_sems.at[recv_id],
            device_id=dev_sib,
            device_id_type=MESH,
        )
        if unless is None:
            copy.wait_recv()
        else:
            pl.when(jnp.logical_not(unless))(lambda: copy.wait_recv())

    local = []

    def keep(src, dst, own):
        copy = pltpu.make_async_copy(src, dst, local_sems.at[alloc("local")])
        pl.when(own)(lambda: copy.start())
        local.append((own, copy))

    grads_in = pltpu.make_async_copy(g_ref, buf["grads"], local_sems.at[alloc("local")])
    grads_in.start()
    own_half = pl.multiple_of(c * dh, HD)
    other_half = pl.multiple_of(sib * dh, HD)
    weight_in = pltpu.make_async_copy(
        w_ref.at[:, pl.ds(own_half, dh)], buf["weight"].at[c], local_sems.at[alloc("local")]
    )
    weight_in.start()

    partners = [dev_sib, dev_up, dev_down]
    for dy in range(1, NY):
        for cc in range(2):
            partners.append(dev(z, (y + dy) % NY, x, cc))
    for dx in range(1, nx):
        for cc in range(2):
            partners.append(dev(z, y, (x + dx) % nx, cc))
    barrier = pltpu.get_barrier_semaphore()
    for partner in partners:
        pl.semaphore_signal(barrier, inc=1, device_id=partner, device_id_type=MESH)
    pl.semaphore_wait(barrier, len(partners))

    half_y = y // 2
    id_k, id_v, id_q = alloc("recv", 2), alloc("recv", 2), alloc("recv", NY)
    own_copies = []
    for j in range(2):
        y_to = 2 * c + j
        own = jnp.logical_and(y_to == y, half_y == c)
        cols = slice(j * HD, (j + 1) * HD)
        part = pl.ds(pl.multiple_of((y % 2) * HD, HD), HD)
        for src, name, base in ((k_ref, "kk", id_k), (v_ref, "vv", id_v)):
            dst = buf[name].at[z, part, :]
            send(src.at[:, cols], dst, base + y % 2, dev(z, y_to, x, half_y), own)
            own_copies.append(
                (own, pltpu.make_async_copy(src.at[:, cols], dst, local_sems.at[alloc("local")]))
            )
            pl.when(own)(lambda: own_copies[-1][1].start())
    for j in range(2):
        y_to = 2 * c + j
        cols = slice(j * HD, (j + 1) * HD)
        for cc in range(2):
            own = jnp.logical_and(y_to == y, c == cc)
            dst = buf["qh"].at[y]
            send(q_ref.at[:, cols], dst, id_q + y, dev(z, y_to, x, cc), own)
            own_copies.append(
                (own, pltpu.make_async_copy(q_ref.at[:, cols], dst, local_sems.at[alloc("local")]))
            )
            pl.when(own)(lambda: own_copies[-1][1].start())
    id_w = alloc("recv")
    send(w_ref.at[:, pl.ds(other_half, dh)], buf["weight"].at[c], id_w, dev_sib)

    slot = lax.broadcasted_iota(jnp.int32, (cap, HD), 0)
    lane = lax.broadcasted_iota(jnp.int32, (cap, HD), 1)
    index = jnp.zeros((cap, HD), jnp.int32)
    for j in range(cap):
        index = jnp.where(slot == j, idx_ref[j], index)
    first = s * shards
    starts, total = [], jnp.int32(0)
    counts = []
    for i in range(shards):
        starts.append(total)
        counts.append(cnt_ref[first + i])
        total = total + counts[-1]
    own_start, own_count = jnp.int32(0), jnp.int32(0)
    for i in range(shards):
        own_start = jnp.where(g == i, starts[i], own_start)
        own_count = jnp.where(g == i, counts[i], own_count)
    pick = jnp.logical_and(index == lane, slot < own_count)
    pick_bf = pick.astype(F32).astype(BF)
    logit_row = logit_ref[...]
    chosen_logit = jnp.sum(
        jnp.where(pick, jnp.broadcast_to(logit_row, (cap, HD)), 0.0), axis=1, keepdims=True
    )
    gate_col = 1.0 / (1.0 + jnp.exp(-chosen_logit))
    gate_tile = jnp.broadcast_to(gate_col, (cap, HD)).astype(BF)
    grads_in.wait()
    for h in range(2):
        buf["picked"][h, :, pl.ds(dh, HD)] = gate_tile
    for h in range(2):
        buf["picked"][h, :, pl.ds(0, dh)] = dot(
            pick_bf, buf["grads"][:, h * dh : (h + 1) * dh], 1, 0
        ).astype(BF)

    right, left = (x + 1) % nx, (x + nx - 1) % nx
    rows = buf["rows"]

    def row_slot(shard):
        return rows.at[pl.ds(pl.multiple_of(shard * cap, cap), cap), :]

    id_rows_sib = alloc("recv")
    id_step_one = alloc("recv", 4)
    id_from_left, id_from_right = id_step_one, id_step_one + 2
    id_far_left, id_far_right = alloc("recv"), alloc("recv")
    send(buf["picked"].at[sib], row_slot(g), id_rows_sib, dev_sib)
    if nx > 1:
        for to, side in ((jnp.where(c == 0, right, left), c), (jnp.where(c == 0, left, right), sib)):
            for h in range(2):
                send(buf["picked"].at[h], row_slot(g), id_step_one + 2 * side + c, dev(z, y, to, h))
    rows[pl.ds(pl.multiple_of(g * cap, cap), cap), :] = buf["picked"][c]

    buf["dkp"][...] = jnp.zeros_like(buf["dkp"])
    buf["dvp"][...] = jnp.zeros_like(buf["dvp"])
    buf["dqt"][...] = jnp.zeros_like(buf["dqt"])
    soft = buf["soft"]
    soft[...] = jnp.zeros_like(soft)
    for i in range(NY):
        soft[i, HD : HD + 8, :] = jnp.full((8, HD), NEG, F32)

    for j in range(2):
        own = jnp.logical_and(c == half_y, y == 2 * c + j)
        part = slice(j * HD, (j + 1) * HD)
        recv(buf["kk"].at[z, part, :], id_k + j, own)
        recv(buf["vv"].at[z, part, :], id_v + j, own)
    for own, copy in own_copies:
        pl.when(own)(lambda: copy.wait())

    halves = (slice(0, HD), slice(HD, 2 * HD))
    ring = [
        (name, half, n_up, n_down)
        for name, n_up, n_down in (("kk", lay.far, lay.near), ("vv", lay.near, lay.far))
        for half in range(2)
    ]
    id_ring = {(name, half): alloc("recv", 2 * (lay.far + 1)) for name, half, _, _ in ring}

    def ring_step(t):
        for name, half, n_up, n_down in ring:
            base = id_ring[name, half]
            for side, hops in ((0, n_up), (1, n_down)):
                b = (z + nz - t) % nz if side == 0 else (z + t) % nz
                ref = buf[name].at[b, halves[half], :]
                if 1 <= t <= hops:
                    recv(ref, base + 2 * t + side)
                if t + 1 <= hops:
                    send(ref, ref, base + 2 * (t + 1) + side, dev_up if side == 0 else dev_down)

    ring_step(0)

    def allowed(i):
        key = c * 2 * HD + lax.broadcasted_iota(jnp.int32, (2 * HD, HD), 0)
        query = i * HD + lax.broadcasted_iota(jnp.int32, (2 * HD, HD), 1)
        return key <= query

    def forward_block(b, diagonal):
        keys, values = buf["kk"][b], buf["vv"][b]
        for i in range(NY):
            scores = dot(keys, buf["qh"][i], 1, 1) * factor
            if diagonal:
                scores = jnp.where(allowed(i), scores, NEG)
            old = soft[i, HD : HD + 1, :]
            new = jnp.maximum(old, jnp.max(scores, axis=0, keepdims=True))
            weights = jnp.exp(scores - new)
            decay = jnp.exp(old - new)
            norm = soft[i, HD + 8 : HD + 9, :] * decay + jnp.sum(weights, axis=0, keepdims=True)
            soft[i, 0:HD, :] = soft[i, 0:HD, :] * decay + dot(values, weights.astype(BF), 0, 0)
            soft[i, HD : HD + 1, :] = new
            soft[i, HD + 8 : HD + 9, :] = norm

    def forward_pair(t):
        pl.when(z >= t)(lambda: forward_block((z + nz - t) % nz, False))
        if t <= nz - 1 - t:
            pl.when(z + t >= nz)(lambda: forward_block((z + t) % nz, False))

    for i in range(NY):
        own = jnp.logical_and(c == half_y, y == i)
        recv(buf["qh"].at[i], id_q + i, own)
    forward_block(z, True)

    def rows_step_two():
        if nx == 1:
            return
        for cc in range(2):
            recv(row_slot(2 * left + cc), id_from_left + cc)
            recv(row_slot(2 * right + cc), id_from_right + cc)
        send(row_slot(2 * left), row_slot(2 * left), id_far_left, dev(z, y, right, c))
        send(row_slot(2 * right + 1), row_slot(2 * right + 1), id_far_right, dev(z, y, left, c))

    id_slice, id_proj, id_go = alloc("recv", NY), alloc("recv"), alloc("recv", NY)
    id_gate = alloc("recv", NY)
    row_iota = lax.broadcasted_iota(jnp.int32, (HD, shards * cap), 0)

    def project():
        recv(row_slot(2 * x + sib), id_rows_sib)
        if nx > 1:
            opposite = (x + 2) % nx
            recv(row_slot(2 * opposite), id_far_left)
            recv(row_slot(2 * opposite + 1), id_far_right)
        lanes = lax.broadcasted_iota(jnp.int32, (1, shards * cap), 1)
        place = jnp.full((1, shards * cap), -1, jnp.int32)
        for i in range(shards):
            within = lanes - i * cap
            live = jnp.logical_and(within >= 0, within < counts[i])
            place = jnp.where(live, starts[i] + within, place)
        compact = (row_iota == place).astype(F32).astype(BF)
        block = buf["block"]
        block[...] = dot(compact, rows[...], 1, 0).astype(BF)
        for i in range(hz):
            for yy in range(NY):
                k = i * NY + yy
                buf["slice_out"][yy, :, i * HD : (i + 1) * HD] = block[:, k * HD : (k + 1) * HD]
        gate_rows = block[:, dh:].astype(F32).T
        buf["gates"][y] = gate_rows[0:8, :]
        for dy in range(1, NY):
            y_to = (y + dy) % NY
            send(buf["gates"].at[y], buf["gates"].at[y], id_gate + y, dev(z, y_to, x, c))
        weight_in.wait()
        recv(buf["weight"].at[sib], id_w)
        part = buf["proj_part"]
        part[sib] = dot(block[:, :dh], buf["weight"][sib], 1, 1)
        send(part.at[sib], buf["proj_in"], id_proj, dev_sib)
        part[c] = dot(block[:, :dh], buf["weight"][c], 1, 1)

    def out_gradient():
        recv(buf["proj_in"], id_proj)
        total = buf["proj_part"][c] + buf["proj_in"][...]
        gate = buf["block"][:, dh:].astype(F32)
        for j in range(2):
            buf["go_out"][j] = (gate * total[:, j * HD : (j + 1) * HD]).astype(BF)
        for j in range(2):
            y_to = 2 * c + j
            for cc in range(2):
                own = jnp.logical_and(y_to == y, c == cc)
                send(buf["go_out"].at[j], buf["goh"].at[y], id_go + y, dev(z, y_to, x, cc), own)

                @pl.when(own)
                def _():
                    buf["goh"][y] = buf["go_out"][j]

        for dy in range(1, NY):
            y_to = (y + dy) % NY
            mine = pl.ds(pl.multiple_of(y * HD, HD), HD)
            send(
                buf["slice_out"].at[y_to],
                buf["slices"].at[mine, :],
                id_slice + y,
                dev(z, y_to, x, c),
            )
        buf["slices"][mine, :] = buf["slice_out"][y]

    for t in range(1, lay.far + 1):
        ring_step(t)
        if t == 1:
            rows_step_two()
        if t == min(2, lay.far):
            project()
        if t == min(3, lay.far):
            out_gradient()
        forward_pair(t)

    id_soft = alloc("recv")
    send(soft, buf["soft_in"], id_soft, dev_sib)
    for i in range(NY):
        own = jnp.logical_and(c == half_y, y == i)
        recv(buf["goh"].at[i], id_go + i, own)
    for dy in range(1, NY):
        yy = (y + dy) % NY
        recv(buf["gates"].at[yy], id_gate + yy)
    recv(buf["soft_in"], id_soft)
    head_cols = pl.ds(pl.multiple_of(y * HD, HD), HD)
    soft_in = buf["soft_in"]
    for i in range(NY):
        max_a, max_b = soft[i, HD : HD + 1, :], soft_in[i, HD : HD + 1, :]
        top = jnp.maximum(max_a, max_b)
        scale_a, scale_b = jnp.exp(max_a - top), jnp.exp(max_b - top)
        norm = soft[i, HD + 8 : HD + 9, :] * scale_a + soft_in[i, HD + 8 : HD + 9, :] * scale_b
        out_t = (soft[i, 0:HD, :] * scale_a + soft_in[i, 0:HD, :] * scale_b) / norm
        out_t = out_t.astype(BF).astype(F32)
        gate_row = buf["gates"][i, 0:1, :]
        buf["outs"][i * HD : (i + 1) * HD, head_cols] = (gate_row * out_t).T.astype(BF)
        buf["lse"][i, 0:1, :] = top + jnp.log(norm)
        delta = jnp.sum(out_t * buf["goh"][i].astype(F32).T, axis=0, keepdims=True)
        buf["delta"][i, 0:1, :] = delta
        buf["router_out"][i] = jnp.broadcast_to(delta / gate_row, (8, HD))

    id_outs, id_outs_sib, id_router_y = alloc("recv", NY), alloc("recv", NY), alloc("recv", NY)

    def out_part(head, core):
        return buf["outs"].at[
            pl.ds(pl.multiple_of(core * 2 * HD, HD), 2 * HD),
            pl.ds(pl.multiple_of(head * HD, HD), HD),
        ]

    for dy in range(1, NY):
        y_to = (y + dy) % NY
        to = dev(z, y_to, x, c)
        send(out_part(y, c), out_part(y, c), id_outs + y, to)
        send(buf["router_out"].at[y_to], buf["router_y"].at[y], id_router_y + y, to)
    buf["router_y"][y] = buf["router_out"][y]

    def backward_block(b, diagonal):
        keys, values = buf["kk"][b], buf["vv"][b]
        for i in range(NY):
            queries, go = buf["qh"][i], buf["goh"][i]
            scores = dot(keys, queries, 1, 1) * factor
            weights = jnp.exp(scores - buf["lse"][i, 0:1, :])
            if diagonal:
                weights = jnp.where(allowed(i), weights, 0.0)
            grad_weights = dot(values, go, 1, 1)
            grad_scores = (weights * (grad_weights - buf["delta"][i, 0:1, :])).astype(BF)
            value_part = dot(weights.astype(BF), go, 1, 0)
            key_part = dot(grad_scores, queries, 1, 0)
            if i == 0:
                buf["dvp"][b] = value_part
                buf["dkp"][b] = key_part
            else:
                buf["dvp"][b] += value_part
                buf["dkp"][b] += key_part
            buf["dqt"][i] += dot(keys, grad_scores, 0, 0)

    def backward_pair(t):
        pl.when(z >= t)(lambda: backward_block((z + nz - t) % nz, False))
        if t <= nz - 1 - t:
            pl.when(z + t >= nz)(lambda: backward_block((z + t) % nz, False))

    hops = ((lay.far, lay.near), (lay.near, lay.far))
    id_kv = alloc("recv", 8 * (lay.far + 1))
    id_dw = alloc("recv", 4 * (lay.far + 1))

    def target(direction, d):
        return (z + nz - d) % nz if direction == 0 else (z + d) % nz

    def chain_id(dw, kind, direction, part):
        steps = lay.far + 1
        if dw:
            return id_dw + (2 * kind + direction) * steps
        return id_kv + (4 * (part.start // HD) + 2 * kind + direction) * steps

    def reduce_step(d, dw):
        for kind in range(2):
            for part in halves if not dw else (slice(0, HD),):
                for direction in range(2):
                    n = hops[kind][direction]
                    if d > n:
                        continue
                    t = n - d
                    b = target(direction, d)
                    base = chain_id(dw, kind, direction, part)
                    to = dev_down if direction == 0 else dev_up
                    skip = b // hz != c if dw else None
                    if dw:
                        mine, out, inc = buf["dwp"].at[kind, b % hz], buf["dw_send"], buf["dw_recv"]
                    else:
                        mine = (buf["dkp"] if kind == 0 else buf["dvp"]).at[b, part, :]
                        out, inc = buf["kv_send"], buf["kv_recv"]

                    def value():
                        total = mine[...]
                        if t > 0:
                            total = total + inc[kind, direction, t - 1, part, :].astype(F32)
                        out[kind, direction, t, part, :] = total.astype(BF)

                    if t > 0:
                        recv(inc.at[kind, direction, t - 1, part, :], base + t - 1, skip)
                    if skip is None:
                        value()
                    else:
                        pl.when(jnp.logical_not(skip))(value)
                    send(
                        out.at[kind, direction, t, part, :],
                        inc.at[kind, direction, t, part, :],
                        base + t,
                        to,
                        skip,
                    )

    def reduce_last(dw, kind, part, skip=None):
        inc = buf["dw_recv"] if dw else buf["kv_recv"]
        for direction in range(2):
            n = hops[kind][direction]
            if n > 0:
                base = chain_id(dw, kind, direction, part)
                recv(inc.at[kind, direction, n - 1, part, :], base + n - 1, skip)

        def value():
            if dw:
                total = buf["dwp"][kind, z % hz]
            else:
                total = (buf["dkp"] if kind == 0 else buf["dvp"])[z, part, :]
            for direction in range(2):
                n = hops[kind][direction]
                if n > 0:
                    total = total + inc[kind, direction, n - 1, part, :].astype(F32)
            return total

        return value

    def share_outs():
        for dy in range(1, NY):
            yy = (y + dy) % NY
            recv(out_part(yy, c), id_outs + yy)
            send(out_part(yy, c), out_part(yy, c), id_outs_sib + yy, dev_sib)

    def weight_gradient():
        for dy in range(1, NY):
            yy = (y + dy) % NY
            recv(buf["slices"].at[pl.ds(pl.multiple_of(yy * HD, HD), HD), :], id_slice + yy)
            recv(out_part(yy, sib), id_outs_sib + yy)
        for i in range(hz):
            for kind in range(2):
                buf["dwp"][kind, i] = dot(
                    buf["slices"][:, i * HD : (i + 1) * HD],
                    buf["outs"][:, kind * 2 * HD : (kind + 1) * 2 * HD],
                    0,
                    0,
                )

    id_router_x = alloc("recv", nx)

    def router_send():
        for dy in range(1, NY):
            yy = (y + dy) % NY
            recv(buf["router_y"].at[yy], id_router_y + yy)
        total = buf["router_y"][0]
        for i in range(1, NY):
            total = total + buf["router_y"][i]
        buf["router_x"][x] = total
        for dx in range(1, nx):
            x_to = (x + dx) % nx
            ref = buf["router_x"].at[x]
            send(ref, ref, id_router_x + x, dev(z, y, x_to, c))

    def router_last():
        for dx in range(1, nx):
            xx = (x + dx) % nx
            recv(buf["router_x"].at[xx], id_router_x + xx)
        total = buf["router_x"][0]
        for i in range(1, nx):
            total = total + buf["router_x"][i]
        token_row = lax.broadcasted_iota(jnp.int32, (HD, cap), 0)
        token_slot = lax.broadcasted_iota(jnp.int32, (HD, cap), 1)
        own = jnp.logical_and(token_row == own_start + token_slot, token_slot < own_count)
        spread = dot(own.astype(F32).astype(BF), pick_bf, 1, 0)
        placed = dot(total, spread, 1, 0, lax.Precision.HIGHEST)
        sig = 1.0 / (1.0 + jnp.exp(-logit_row))
        lg_ref[...] = placed[0:1, :] * sig * (1.0 - sig)

    id_kv_fin, id_dq = alloc("recv", 4), alloc("recv", 4)
    id_dw_fin = alloc("recv")
    side = y % 2

    def send_key_value_grads():
        for kind in range(2):
            for j in range(2):
                final = reduce_last(False, kind, halves[j])()
                if kind == 0:
                    final = final * factor
                buf["kv_fin"][kind, j] = final.astype(BF)
                y_to = 2 * c + j
                own = jnp.logical_and(y_to == y, half_y == c)
                src, dst = buf["kv_fin"].at[kind, j], kv_land.at[kind, side]
                send(src, dst, id_kv_fin + 2 * kind + side, dev(z, y_to, x, half_y), own)
                keep(src, dst, own)

    def send_query_grads():
        for i in range(NY):
            buf["dq_out"][i] = (buf["dqt"][i].T * factor).astype(BF)
            own = jnp.logical_and(y == i, half_y == c)
            src, dst = buf["dq_out"].at[i], dq_land.at[side, c]
            send(src, dst, id_dq + 2 * side + c, dev(z, i, x, half_y), own)
            keep(src, dst, own)

    late = min(2, lay.far)
    for d in range(lay.far, 0, -1):
        backward_pair(d)
        reduce_step(d, False)
        if d == lay.far:
            share_outs()
        if d == late:
            weight_gradient()
            router_send()
            reduce_step(lay.far, True)
        elif d < late:
            reduce_step(lay.far - late + d, True)
    backward_block(z, True)
    send_query_grads()
    for d in range(lay.far - late, 1, -1):
        reduce_step(d, True)
    send_key_value_grads()
    if lay.far - late >= 1:
        reduce_step(1, True)
    router_last()

    skip = z // hz != c
    holder = jnp.logical_not(skip)
    for kind in range(2):
        value = reduce_last(True, kind, slice(0, HD), skip)

        @pl.when(holder)
        def _():
            buf["dw_fin"][kind] = value()

    send(buf["dw_fin"].at[sib], dw_land, id_dw_fin, dev_sib, skip)
    keep(buf["dw_fin"].at[c], dw_land, holder)

    for j in range(2):
        for cc in range(2):
            own = jnp.logical_and(y == 2 * c + j, c == cc)
            recv(dq_land.at[j, cc], id_dq + 2 * j + cc, own)
    for kind in range(2):
        for j in range(2):
            own = jnp.logical_and(y == 2 * c + j, half_y == c)
            recv(kv_land.at[kind, j], id_kv_fin + 2 * kind + j, own)
    recv(dw_land, id_dw_fin, holder)
    for own, copy in local:
        pl.when(own)(lambda: copy.wait())
    for unless, copy in sent:
        if unless is None:
            copy.wait_send()
        else:
            pl.when(jnp.logical_not(unless))(lambda: copy.wait_send())


SEMS = 220
VMEM_LIMIT = 60 * 1024 * 1024


def finish(dq_land, kv_land, dw_land, lg_in, dq_ref, dk_ref, dv_ref, dw_ref, lg_ref):
    for j in range(2):
        cols = slice(j * HD, (j + 1) * HD)
        dq_ref[:, cols] = (dq_land[j, 0].astype(F32) + dq_land[j, 1].astype(F32)).astype(BF)
        dk_ref[:, cols] = kv_land[0, j]
        dv_ref[:, cols] = kv_land[1, j]
    dw_ref[...] = dw_land[...]
    lg_ref[...] = lg_in[...]


def shards_fn(nz, nx):
    def run(grad, logit, index, count, weight, q, k, v):
        lay = Layout(nz, nx, grad.shape[0], index.shape[0], grad.shape[1])
        scratch = lay.scratch()
        names = list(scratch)
        any_ = pl.BlockSpec(memory_space=pl.ANY)
        smem = pl.BlockSpec(memory_space=pltpu.SMEM)
        vmem = pl.BlockSpec(memory_space=pltpu.VMEM)

        def kernel(*refs):
            fused(lay, names, *refs)

        lands = pl.pallas_call(
            kernel,
            out_shape=(
                jax.ShapeDtypeStruct((2, 2, HD, HD), BF),
                jax.ShapeDtypeStruct((2, 2, HD, HD), BF),
                jax.ShapeDtypeStruct((HD, 2 * HD), F32),
                jax.ShapeDtypeStruct((1, HD), F32),
            ),
            in_specs=[any_, vmem, smem, smem, any_, any_, any_, any_],
            out_specs=(any_, any_, any_, vmem),
            scratch_shapes=list(scratch.values())
            + [
                pltpu.SemaphoreType.DMA((SEMS,)),
                pltpu.SemaphoreType.DMA((SEMS,)),
                pltpu.SemaphoreType.DMA((32,)),
            ],
            compiler_params=pltpu.CompilerParams(
                collective_id=0, has_side_effects=True, vmem_limit_bytes=VMEM_LIMIT
            ),
            name="routed_backward",
        )(grad, logit.reshape(1, -1), index, count, weight, q, k, v)
        out = pl.pallas_call(
            finish,
            out_shape=(
                jax.ShapeDtypeStruct(q.shape, BF),
                jax.ShapeDtypeStruct(q.shape, BF),
                jax.ShapeDtypeStruct(q.shape, BF),
                jax.ShapeDtypeStruct((HD, q.shape[1]), F32),
                jax.ShapeDtypeStruct((1, HD), F32),
            ),
            in_specs=[vmem] * 4,
            out_specs=(vmem,) * 5,
            compiler_params=pltpu.CompilerParams(vmem_limit_bytes=VMEM_LIMIT),
            name="finish",
        )(*lands)
        return (*out[:4], out[4].reshape(-1))

    return run


def solution(mesh):
    nz = mesh.shape["seq"] // NY
    nx = mesh.shape["grp"] // 2
    placed = (
        P(("seq", "grp"), None),
        P(("seq", "grp")),
        P(("seq", "grp")),
        P(),
        P("grp", None),
        P("seq", "grp"),
        P("seq", "grp"),
        P("seq", "grp"),
    )
    return jax.shard_map(
        shards_fn(nz, nx),
        mesh=mesh,
        in_specs=placed,
        out_specs=(
            P("seq", "grp"),
            P("seq", "grp"),
            P("seq", "grp"),
            P("seq", "grp"),
            P(("seq", "grp")),
        ),
        check_vma=False,
    )
```

```python
import jax
import jax.numpy as jnp
from jax import lax
from jax.experimental import pallas as pl
from jax.experimental.pallas import tpu as pltpu
from jax.sharding import PartitionSpec as P

HD = 128
NY = 4
MESH = pl.DeviceIdType.MESH
BF = jnp.bfloat16
F32 = jnp.float32
NEG = -1e30


def dot(a, b, ca, cb, precision=None):
    return lax.dot_general(
        a, b, (((ca,), (cb,)), ((), ())), preferred_element_type=F32, precision=precision
    )


class Layout:
    def __init__(self, nz, nx, tok, cap, d):
        self.nz, self.nx, self.tok, self.cap, self.d = nz, nx, tok, cap, d
        self.dh = d // 2
        self.hz = nz // 2
        self.far = nz // 2
        self.near = nz - 1 - self.far

    def scratch(self):
        nz, nx, cap, d, dh, hz = self.nz, self.nx, self.cap, self.d, self.dh, self.hz
        v = pltpu.VMEM
        steps = max(self.far, 1)
        names = dict(
            grads=v((self.tok, d), BF),
            weight=v((2, 2 * HD, dh), BF),
            picked=v((2, cap, dh + HD), BF),
            rows=v((2 * nx * cap, dh + HD), BF),
            block=v((HD, dh + HD), BF),
            slice_out=v((NY, HD, hz * HD), BF),
            slices=v((NY * HD, hz * HD), BF),
            gates=v((NY, 8, HD), F32),
            proj_part=v((2, HD, 2 * HD), F32),
            proj_in=v((HD, 2 * HD), F32),
            go_out=v((2, HD, HD), BF),
            qh=v((NY, HD, HD), BF),
            goh=v((NY, HD, HD), BF),
            kk=v((nz, 2 * HD, HD), BF),
            vv=v((nz, 2 * HD, HD), BF),
            soft=v((NY, HD + 16, HD), F32),
            soft_in=v((NY, HD + 16, HD), F32),
            lse=v((NY, 8, HD), F32),
            delta=v((NY, 8, HD), F32),
            outs=v((NY * HD, NY * HD), BF),
            dqt=v((NY, HD, HD), F32),
            dkp=v((nz, 2 * HD, HD), F32),
            dvp=v((nz, 2 * HD, HD), F32),
            dwp=v((hz, HD, NY * HD), F32),
            kv_send=v((2, 2, steps, 2 * HD, HD), BF),
            kv_recv=v((2, 2, steps, 2 * HD, HD), BF),
            dw_send=v((2, steps, HD, NY * HD), BF),
            dw_recv=v((2, steps, HD, NY * HD), BF),
            kv_fin=v((2, 2, HD, HD), BF),
            dq_out=v((NY, HD, HD), BF),
            dw_fin=v((2, HD, 2 * HD), F32),
            router_out=v((NY, 8, HD), F32),
            router_y=v((NY, 8, HD), F32),
            router_x=v((nx, 8, HD), F32),
        )
        return names


def fused(lay, names, *refs):
    (g_ref, logit_ref, idx_ref, cnt_ref, w_ref, q_ref, k_ref, v_ref) = refs[:8]
    (dq_land, kv_land, dw_land, lg_ref) = refs[8:12]
    buf = dict(zip(names, refs[12 : 12 + len(names)]))
    send_sems, recv_sems, local_sems = refs[12 + len(names) :]
    nz, nx, cap, dh, hz = lay.nz, lay.nx, lay.cap, lay.dh, lay.hz
    shards = 2 * nx
    factor = HD ** (-0.5)

    s, g = lax.axis_index("seq"), lax.axis_index("grp")
    z, y, x, c = s // NY, s % NY, g // 2, g % 2
    sib = 1 - c

    def dev(z_, y_, x_, c_):
        return (z_ * NY + y_, x_ * 2 + c_)

    up, down = (z + 1) % nz, (z + nz - 1) % nz
    dev_up, dev_down = dev(up, y, x, c), dev(down, y, x, c)
    dev_sib = dev(z, y, x, sib)

    counter = {"send": 0, "recv": 0, "local": 0}

    def alloc(kind, n=1):
        first = counter[kind]
        counter[kind] += n
        return first

    ids = {}

    def ident(*key):
        if key not in ids:
            ids[key] = alloc("recv")
        return ids[key]

    pool = [None] * POOL
    singles = []

    def wait_sent(entry):
        unless, copy = entry
        if unless is None:
            copy.wait_send()
        else:
            pl.when(jnp.logical_not(unless))(lambda: copy.wait_send())

    def send(src, dst, recv_id, to, unless=None, single=False):
        if single:
            slot = POOL + len(singles)
        else:
            slot = alloc("send") % POOL
            if pool[slot] is not None:
                wait_sent(pool[slot])
        copy = pltpu.make_async_remote_copy(
            src_ref=src,
            dst_ref=dst,
            send_sem=send_sems.at[slot],
            recv_sem=recv_sems.at[recv_id],
            device_id=to,
            device_id_type=MESH,
        )
        if single:
            singles.append((unless, copy))
        else:
            pool[slot] = (unless, copy)
        if unless is None:
            copy.start()
        else:
            pl.when(jnp.logical_not(unless))(lambda: copy.start())

    def keep(src, dst, recv_id, own):
        copy = pltpu.make_async_copy(src, dst, recv_sems.at[recv_id])
        pl.when(own)(lambda: copy.start())

    def recv(dst, recv_id, unless=None):
        copy = pltpu.make_async_remote_copy(
            src_ref=dst,
            dst_ref=dst,
            send_sem=send_sems.at[0],
            recv_sem=recv_sems.at[recv_id],
            device_id=dev_sib,
            device_id_type=MESH,
        )
        if unless is None:
            copy.wait_recv()
        else:
            pl.when(jnp.logical_not(unless))(lambda: copy.wait_recv())

    grads_in = pltpu.make_async_copy(g_ref, buf["grads"], local_sems.at[alloc("local")])
    grads_in.start()
    own_half = pl.multiple_of(c * dh, HD)
    other_half = pl.multiple_of(sib * dh, HD)
    weight_in = pltpu.make_async_copy(
        w_ref.at[:, pl.ds(own_half, dh)], buf["weight"].at[c], local_sems.at[alloc("local")]
    )
    weight_in.start()

    partners = [dev_sib, dev_up, dev_down]
    for dy in range(1, NY):
        for cc in range(2):
            partners.append(dev(z, (y + dy) % NY, x, cc))
    for dx in range(1, nx):
        for cc in range(2):
            partners.append(dev(z, y, (x + dx) % nx, cc))
    barrier = pltpu.get_barrier_semaphore()
    for partner in partners:
        pl.semaphore_signal(barrier, inc=1, device_id=partner, device_id_type=MESH)
    pl.semaphore_wait(barrier, len(partners))

    half_y = y // 2
    id_k, id_v, id_q = alloc("recv"), alloc("recv"), alloc("recv")
    for src, name, base in ((k_ref, "kk", id_k), (v_ref, "vv", id_v)):
        for j in range(2):
            y_to = 2 * c + j
            own = jnp.logical_and(y_to == y, half_y == c)
            part = pl.ds(pl.multiple_of((y % 2) * HD, HD), HD)
            mine, dst = src.at[:, j * HD : (j + 1) * HD], buf[name].at[z, part, :]
            send(mine, dst, base, dev(z, y_to, x, half_y), own)
            keep(mine, dst, base, own)
    for j in range(2):
        y_to = 2 * c + j
        for cc in range(2):
            own = jnp.logical_and(y_to == y, c == cc)
            mine, dst = q_ref.at[:, j * HD : (j + 1) * HD], buf["qh"].at[y]
            send(mine, dst, id_q, dev(z, y_to, x, cc), own)
            keep(mine, dst, id_q, own)
    id_w = alloc("recv")
    send(w_ref.at[:, pl.ds(other_half, dh)], buf["weight"].at[c], id_w, dev_sib, single=True)

    slot = lax.broadcasted_iota(jnp.int32, (cap, HD), 0)
    lane = lax.broadcasted_iota(jnp.int32, (cap, HD), 1)
    index = jnp.zeros((cap, HD), jnp.int32)
    for j in range(cap):
        index = jnp.where(slot == j, idx_ref[j], index)
    first = s * shards
    starts, total = [], jnp.int32(0)
    counts = []
    for i in range(shards):
        starts.append(total)
        counts.append(cnt_ref[first + i])
        total = total + counts[-1]
    own_start, own_count = jnp.int32(0), jnp.int32(0)
    for i in range(shards):
        own_start = jnp.where(g == i, starts[i], own_start)
        own_count = jnp.where(g == i, counts[i], own_count)
    pick = jnp.logical_and(index == lane, slot < own_count)
    pick_bf = pick.astype(F32).astype(BF)
    logit_row = logit_ref[...]
    chosen_logit = jnp.sum(
        jnp.where(pick, jnp.broadcast_to(logit_row, (cap, HD)), 0.0), axis=1, keepdims=True
    )
    gate_col = 1.0 / (1.0 + jnp.exp(-chosen_logit))
    gate_tile = jnp.broadcast_to(gate_col, (cap, HD)).astype(BF)
    grads_in.wait()
    for h in range(2):
        buf["picked"][h, :, pl.ds(dh, HD)] = gate_tile
    for h in range(2):
        buf["picked"][h, :, pl.ds(0, dh)] = dot(
            pick_bf, buf["grads"][:, h * dh : (h + 1) * dh], 1, 0
        ).astype(BF)

    right, left = (x + 1) % nx, (x + nx - 1) % nx
    rows = buf["rows"]

    def row_slot(shard):
        return rows.at[pl.ds(pl.multiple_of(shard * cap, cap), cap), :]

    id_rows_sib = alloc("recv")
    id_step_one = alloc("recv", 4)
    id_from_left, id_from_right = id_step_one, id_step_one + 2
    id_far = alloc("recv")
    send(buf["picked"].at[sib], row_slot(g), id_rows_sib, dev_sib, single=True)
    if nx > 1:
        for to, side in ((jnp.where(c == 0, right, left), c), (jnp.where(c == 0, left, right), sib)):
            for h in range(2):
                dst, recv_id = row_slot(g), id_step_one + 2 * side + c
                send(buf["picked"].at[h], dst, recv_id, dev(z, y, to, h), single=True)
    rows[pl.ds(pl.multiple_of(g * cap, cap), cap), :] = buf["picked"][c]

    buf["dkp"][...] = jnp.zeros_like(buf["dkp"])
    buf["dvp"][...] = jnp.zeros_like(buf["dvp"])
    buf["dqt"][...] = jnp.zeros_like(buf["dqt"])
    soft = buf["soft"]
    soft[...] = jnp.zeros_like(soft)
    for i in range(NY):
        soft[i, HD : HD + 8, :] = jnp.full((8, HD), NEG, F32)

    recv(buf["kk"].at[z], id_k)
    recv(buf["vv"].at[z], id_v)

    halves = (slice(0, HD), slice(HD, 2 * HD))
    ring = [
        (name, half, n_up, n_down)
        for name, n_up, n_down in (("kk", lay.far, lay.near), ("vv", lay.near, lay.far))
        for half in range(2)
    ]

    def ring_step(t):
        for name, half, n_up, n_down in ring:
            for side, hops in ((0, n_up), (1, n_down)):
                b = (z + nz - t) % nz if side == 0 else (z + t) % nz
                ref = buf[name].at[b, halves[half], :]
                if 1 <= t <= hops:
                    recv(ref, ident(name, half, t, side))
                if t + 1 <= hops:
                    to = dev_up if side == 0 else dev_down
                    send(ref, ref, ident(name, half, t + 1, side), to)

    ring_step(0)

    def allowed(i):
        key = c * 2 * HD + lax.broadcasted_iota(jnp.int32, (2 * HD, HD), 0)
        query = i * HD + lax.broadcasted_iota(jnp.int32, (2 * HD, HD), 1)
        return key <= query

    def forward_block(b, diagonal):
        keys, values = buf["kk"][b], buf["vv"][b]
        for i in range(NY):
            scores = dot(keys, buf["qh"][i], 1, 1) * factor
            if diagonal:
                scores = jnp.where(allowed(i), scores, NEG)
            old = soft[i, HD : HD + 1, :]
            new = jnp.maximum(old, jnp.max(scores, axis=0, keepdims=True))
            weights = jnp.exp(scores - new)
            decay = jnp.exp(old - new)
            norm = soft[i, HD + 8 : HD + 9, :] * decay + jnp.sum(weights, axis=0, keepdims=True)
            soft[i, 0:HD, :] = soft[i, 0:HD, :] * decay + dot(values, weights.astype(BF), 0, 0)
            soft[i, HD : HD + 1, :] = new
            soft[i, HD + 8 : HD + 9, :] = norm

    def forward_pair(t):
        pl.when(z >= t)(lambda: forward_block((z + nz - t) % nz, False))
        if t <= nz - 1 - t:
            pl.when(z + t >= nz)(lambda: forward_block((z + t) % nz, False))

    def rows_step_two():
        if nx == 1:
            return
        for cc in range(2):
            recv(row_slot(2 * left + cc), id_from_left + cc)
            recv(row_slot(2 * right + cc), id_from_right + cc)
        send(row_slot(2 * left), row_slot(2 * left), id_far, dev(z, y, right, c), single=True)
        ref = row_slot(2 * right + 1)
        send(ref, ref, id_far, dev(z, y, left, c), single=True)

    id_slice, id_proj, id_go = alloc("recv"), alloc("recv"), alloc("recv")
    id_gate = alloc("recv")
    row_iota = lax.broadcasted_iota(jnp.int32, (HD, shards * cap), 0)

    def project():
        recv(row_slot(2 * x + sib), id_rows_sib)
        if nx > 1:
            recv(rows.at[pl.ds(0, 2 * cap), :], id_far)
        lanes = lax.broadcasted_iota(jnp.int32, (1, shards * cap), 1)
        place = jnp.full((1, shards * cap), -1, jnp.int32)
        for i in range(shards):
            within = lanes - i * cap
            live = jnp.logical_and(within >= 0, within < counts[i])
            place = jnp.where(live, starts[i] + within, place)
        compact = (row_iota == place).astype(F32).astype(BF)
        block = buf["block"]
        block[...] = dot(compact, rows[...], 1, 0).astype(BF)
        for i in range(hz):
            for yy in range(NY):
                k = i * NY + yy
                buf["slice_out"][yy, :, i * HD : (i + 1) * HD] = block[:, k * HD : (k + 1) * HD]
        gate_rows = block[:, dh:].astype(F32).T
        buf["gates"][y] = gate_rows[0:8, :]
        for dy in range(1, NY):
            y_to = (y + dy) % NY
            send(buf["gates"].at[y], buf["gates"].at[y], id_gate, dev(z, y_to, x, c))
        weight_in.wait()
        recv(buf["weight"].at[sib], id_w)
        part = buf["proj_part"]
        part[sib] = dot(block[:, :dh], buf["weight"][sib], 1, 1)
        send(part.at[sib], buf["proj_in"], id_proj, dev_sib)
        part[c] = dot(block[:, :dh], buf["weight"][c], 1, 1)

    def out_gradient():
        recv(buf["proj_in"], id_proj)
        total = buf["proj_part"][c] + buf["proj_in"][...]
        gate = buf["block"][:, dh:].astype(F32)
        for j in range(2):
            buf["go_out"][j] = (gate * total[:, j * HD : (j + 1) * HD]).astype(BF)
        for j in range(2):
            y_to = 2 * c + j
            for cc in range(2):
                own = jnp.logical_and(y_to == y, c == cc)
                send(buf["go_out"].at[j], buf["goh"].at[y], id_go, dev(z, y_to, x, cc), own)
                keep(buf["go_out"].at[j], buf["goh"].at[y], id_go, own)

        for dy in range(1, NY):
            y_to = (y + dy) % NY
            mine = pl.ds(pl.multiple_of(y * HD, HD), HD)
            send(
                buf["slice_out"].at[y_to],
                buf["slices"].at[mine, :],
                id_slice,
                dev(z, y_to, x, c),
                single=True,
            )
        buf["slices"][mine, :] = buf["slice_out"][y]

    rows_step_two()
    recv(buf["qh"], id_q)
    forward_block(z, True)
    for t in range(1, lay.far + 1):
        ring_step(t)
        if t == 1:
            project()
        if t == min(2, lay.far):
            out_gradient()
        forward_pair(t)

    id_soft = alloc("recv")
    send(soft, buf["soft_in"], id_soft, dev_sib)
    recv(buf["goh"], id_go)
    recv(buf["gates"].at[pl.ds(0, NY - 1)], id_gate)
    recv(buf["soft_in"], id_soft)
    head_cols = pl.ds(pl.multiple_of(y * HD, HD), HD)
    soft_in = buf["soft_in"]
    for i in range(NY):
        max_a, max_b = soft[i, HD : HD + 1, :], soft_in[i, HD : HD + 1, :]
        top = jnp.maximum(max_a, max_b)
        scale_a, scale_b = jnp.exp(max_a - top), jnp.exp(max_b - top)
        norm = soft[i, HD + 8 : HD + 9, :] * scale_a + soft_in[i, HD + 8 : HD + 9, :] * scale_b
        out_t = (soft[i, 0:HD, :] * scale_a + soft_in[i, 0:HD, :] * scale_b) / norm
        out_t = out_t.astype(BF).astype(F32)
        gate_row = buf["gates"][i, 0:1, :]
        buf["outs"][i * HD : (i + 1) * HD, head_cols] = (gate_row * out_t).T.astype(BF)
        buf["lse"][i, 0:1, :] = top + jnp.log(norm)
        delta = jnp.sum(out_t * buf["goh"][i].astype(F32).T, axis=0, keepdims=True)
        buf["delta"][i, 0:1, :] = delta
        buf["router_out"][i] = jnp.broadcast_to(delta / gate_row, (8, HD))

    id_outs, id_outs_sib, id_router_y = alloc("recv"), alloc("recv"), alloc("recv")

    def out_part(head, core):
        return buf["outs"].at[
            pl.ds(pl.multiple_of(core * 2 * HD, HD), 2 * HD),
            pl.ds(pl.multiple_of(head * HD, HD), HD),
        ]

    for dy in range(1, NY):
        y_to = (y + dy) % NY
        to = dev(z, y_to, x, c)
        send(out_part(y, c), out_part(y, c), id_outs, to)
        send(buf["router_out"].at[y_to], buf["router_y"].at[y], id_router_y, to)
    buf["router_y"][y] = buf["router_out"][y]

    def backward_block(b, diagonal):
        keys, values = buf["kk"][b], buf["vv"][b]
        for i in range(NY):
            queries, go = buf["qh"][i], buf["goh"][i]
            scores = dot(keys, queries, 1, 1) * factor
            weights = jnp.exp(scores - buf["lse"][i, 0:1, :])
            if diagonal:
                weights = jnp.where(allowed(i), weights, 0.0)
            grad_weights = dot(values, go, 1, 1)
            grad_scores = (weights * (grad_weights - buf["delta"][i, 0:1, :])).astype(BF)
            value_part = dot(weights.astype(BF), go, 1, 0)
            key_part = dot(grad_scores, queries, 1, 0)
            if i == 0:
                buf["dvp"][b] = value_part
                buf["dkp"][b] = key_part
            else:
                buf["dvp"][b] += value_part
                buf["dkp"][b] += key_part
            buf["dqt"][i] += dot(keys, grad_scores, 0, 0)

    def backward_pair(t):
        pl.when(z >= t)(lambda: backward_block((z + nz - t) % nz, False))
        if t <= nz - 1 - t:
            pl.when(z + t >= nz)(lambda: backward_block((z + t) % nz, False))

    hops = ((lay.far, lay.near), (lay.near, lay.far))

    def target(direction, d):
        return (z + nz - d) % nz if direction == 0 else (z + d) % nz

    dev_next = (dev_down, dev_up)

    def kv_step(d, first):
        inc = buf["kv_recv"]
        for kind in range(2):
            for part in halves:
                for direction in range(2):
                    n = hops[kind][direction]
                    t = n - d
                    if t < 0 or (t == 0) != first:
                        continue
                    key = ("chain", kind, direction, part.start)
                    total = (buf["dkp"] if kind == 0 else buf["dvp"])[target(direction, d), part, :]
                    if t > 0:
                        recv(inc.at[kind, direction, t - 1, part, :], ident(*key, t - 1))
                        total = total + inc[kind, direction, t - 1, part, :].astype(F32)
                    out = buf["kv_send"].at[kind, direction, t, part, :]
                    out[...] = total.astype(BF)
                    to = dev_next[direction]
                    send(out, inc.at[kind, direction, t, part, :], ident(*key, t), to)

    def kv_last(kind, part):
        inc = buf["kv_recv"]
        total = (buf["dkp"] if kind == 0 else buf["dvp"])[z, part, :]
        for direction in range(2):
            n = hops[kind][direction]
            if n > 0:
                last = ident("chain", kind, direction, part.start, n - 1)
                recv(inc.at[kind, direction, n - 1, part, :], last)
                total = total + inc[kind, direction, n - 1, part, :].astype(F32)
        return total

    def dw_step(d):
        inc = buf["dw_recv"]
        for direction, n in enumerate(hops[0]):
            t = n - d
            if t < 0:
                continue
            b = target(direction, d)
            skip = b // hz != c
            out = buf["dw_send"].at[direction, t]
            if t > 0:
                recv(inc.at[direction, t - 1], ident("dw", direction, t - 1), skip)

            @pl.when(jnp.logical_not(skip))
            def _():
                total = buf["dwp"][b % hz]
                if t > 0:
                    total = total + inc[direction, t - 1].astype(F32)
                out[...] = total.astype(BF)

            send(out, inc.at[direction, t], ident("dw", direction, t), dev_next[direction], skip)

    def share_outs():
        recv(buf["outs"].at[: 2 * HD, : (NY - 1) * HD], id_outs)
        for dy in range(1, NY):
            ref = out_part((y + dy) % NY, c)
            send(ref, ref, id_outs_sib, dev_sib)

    def weight_gradient():
        recv(buf["slices"].at[: (NY - 1) * HD, :], id_slice)
        recv(buf["outs"].at[: 2 * HD, : (NY - 1) * HD], id_outs_sib)
        for i in range(hz):
            part = buf["slices"][:, i * HD : (i + 1) * HD]
            buf["dwp"][i] = dot(part, buf["outs"][...], 0, 0)

    id_router_x = alloc("recv")

    def router_send():
        recv(buf["router_y"].at[: NY - 1], id_router_y)
        total = buf["router_y"][0]
        for i in range(1, NY):
            total = total + buf["router_y"][i]
        buf["router_x"][x] = total
        for dx in range(1, nx):
            x_to = (x + dx) % nx
            ref = buf["router_x"].at[x]
            send(ref, ref, id_router_x, dev(z, y, x_to, c))

    def router_last():
        if nx > 1:
            recv(buf["router_x"].at[: nx - 1], id_router_x)
        total = buf["router_x"][0]
        for i in range(1, nx):
            total = total + buf["router_x"][i]
        token_row = lax.broadcasted_iota(jnp.int32, (HD, cap), 0)
        token_slot = lax.broadcasted_iota(jnp.int32, (HD, cap), 1)
        own = jnp.logical_and(token_row == own_start + token_slot, token_slot < own_count)
        spread = dot(own.astype(F32).astype(BF), pick_bf, 1, 0)
        placed = dot(total, spread, 1, 0, lax.Precision.HIGHEST)
        sig = 1.0 / (1.0 + jnp.exp(-logit_row))
        lg_ref[...] = placed[0:1, :] * sig * (1.0 - sig)

    id_kv_fin, id_dq = alloc("recv"), alloc("recv")
    id_dw_fin = alloc("recv")
    side = y % 2

    def send_key_value_grads():
        for kind in range(2):
            for j in range(2):
                final = kv_last(kind, halves[j])
                if kind == 0:
                    final = final * factor
                buf["kv_fin"][kind, j] = final.astype(BF)
                y_to = 2 * c + j
                own = jnp.logical_and(y_to == y, half_y == c)
                src, dst = buf["kv_fin"].at[kind, j], kv_land.at[kind, side]
                send(src, dst, id_kv_fin, dev(z, y_to, x, half_y), own)
                keep(src, dst, id_kv_fin, own)

    def send_query_grads():
        for i in range(NY):
            buf["dq_out"][i] = (buf["dqt"][i].T * factor).astype(BF)
            own = jnp.logical_and(y == i, half_y == c)
            src, dst = buf["dq_out"].at[i], dq_land.at[side, c]
            send(src, dst, id_dq, dev(z, i, x, half_y), own)
            keep(src, dst, id_dq, own)

    for d in range(lay.far, 0, -1):
        backward_pair(d)
        kv_step(d, True)
    backward_block(z, True)
    send_query_grads()
    share_outs()
    if lay.far == 1:
        weight_gradient()
        router_send()
    for d in range(lay.far - 1, 0, -1):
        kv_step(d, False)
        if d == lay.far - 1:
            weight_gradient()
            router_send()
        dw_step(d + 1)
    send_key_value_grads()
    dw_step(1)
    router_last()

    skip = z // hz != c
    holder = jnp.logical_not(skip)
    for direction, n in enumerate(hops[0]):
        if n > 0:
            recv(buf["dw_recv"].at[direction, n - 1], ident("dw", direction, n - 1), skip)

    @pl.when(holder)
    def _():
        total = buf["dwp"][z % hz]
        for direction, n in enumerate(hops[0]):
            if n > 0:
                total = total + buf["dw_recv"][direction, n - 1].astype(F32)
        for core in range(2):
            buf["dw_fin"][core] = total[:, core * 2 * HD : (core + 1) * 2 * HD]

    send(buf["dw_fin"].at[sib], dw_land, id_dw_fin, dev_sib, skip)
    keep(buf["dw_fin"].at[c], dw_land, id_dw_fin, holder)

    recv(dq_land, id_dq)
    recv(kv_land, id_kv_fin)
    recv(dw_land, id_dw_fin)
    for entry in pool + singles:
        if entry is not None:
            wait_sent(entry)


POOL = 24
RECV_SEMS = 85
SEND_SEMS = 35
VMEM_LIMIT = 60 * 1024 * 1024


def finish(dq_land, kv_land, dw_land, lg_in, dq_ref, dk_ref, dv_ref, dw_ref, lg_ref):
    for j in range(2):
        cols = slice(j * HD, (j + 1) * HD)
        dq_ref[:, cols] = (dq_land[j, 0].astype(F32) + dq_land[j, 1].astype(F32)).astype(BF)
        dk_ref[:, cols] = kv_land[0, j]
        dv_ref[:, cols] = kv_land[1, j]
    dw_ref[...] = dw_land[...]
    lg_ref[...] = lg_in[...]


def shards_fn(nz, nx):
    def run(grad, logit, index, count, weight, q, k, v):
        lay = Layout(nz, nx, grad.shape[0], index.shape[0], grad.shape[1])
        scratch = lay.scratch()
        names = list(scratch)
        any_ = pl.BlockSpec(memory_space=pl.ANY)
        smem = pl.BlockSpec(memory_space=pltpu.SMEM)
        vmem = pl.BlockSpec(memory_space=pltpu.VMEM)

        def kernel(*refs):
            fused(lay, names, *refs)

        lands = pl.pallas_call(
            kernel,
            out_shape=(
                jax.ShapeDtypeStruct((2, 2, HD, HD), BF),
                jax.ShapeDtypeStruct((2, 2, HD, HD), BF),
                jax.ShapeDtypeStruct((HD, 2 * HD), F32),
                jax.ShapeDtypeStruct((1, HD), F32),
            ),
            in_specs=[any_, vmem, smem, smem, any_, any_, any_, any_],
            out_specs=(any_, any_, any_, vmem),
            scratch_shapes=list(scratch.values())
            + [
                pltpu.SemaphoreType.DMA((SEND_SEMS,)),
                pltpu.SemaphoreType.DMA((RECV_SEMS,)),
                pltpu.SemaphoreType.DMA((2,)),
            ],
            compiler_params=pltpu.CompilerParams(
                collective_id=0, has_side_effects=True, vmem_limit_bytes=VMEM_LIMIT
            ),
            name="routed_backward",
        )(grad, logit.reshape(1, -1), index, count, weight, q, k, v)
        out = pl.pallas_call(
            finish,
            out_shape=(
                jax.ShapeDtypeStruct(q.shape, BF),
                jax.ShapeDtypeStruct(q.shape, BF),
                jax.ShapeDtypeStruct(q.shape, BF),
                jax.ShapeDtypeStruct((HD, q.shape[1]), F32),
                jax.ShapeDtypeStruct((1, HD), F32),
            ),
            in_specs=[vmem] * 4,
            out_specs=(vmem,) * 5,
            compiler_params=pltpu.CompilerParams(vmem_limit_bytes=VMEM_LIMIT),
            name="finish",
        )(*lands)
        return (*out[:4], out[4].reshape(-1))

    return run


def solution(mesh):
    nz = mesh.shape["seq"] // NY
    nx = mesh.shape["grp"] // 2
    placed = (
        P(("seq", "grp"), None),
        P(("seq", "grp")),
        P(("seq", "grp")),
        P(),
        P("grp", None),
        P("seq", "grp"),
        P("seq", "grp"),
        P("seq", "grp"),
    )
    return jax.shard_map(
        shards_fn(nz, nx),
        mesh=mesh,
        in_specs=placed,
        out_specs=(
            P("seq", "grp"),
            P("seq", "grp"),
            P("seq", "grp"),
            P("seq", "grp"),
            P(("seq", "grp")),
        ),
        check_vma=False,
    )
```

```python
import jax
import jax.numpy as jnp
from jax import lax
from jax.experimental import pallas as pl
from jax.experimental.pallas import tpu as pltpu
from jax.sharding import PartitionSpec as P

HD = 128
NY = 4
MESH = pl.DeviceIdType.MESH
BF = jnp.bfloat16
F32 = jnp.float32
NEG = -1e30


def dot(a, b, ca, cb, precision=None):
    return lax.dot_general(
        a, b, (((ca,), (cb,)), ((), ())), preferred_element_type=F32, precision=precision
    )


class Layout:
    def __init__(self, nz, nx, tok, cap, d):
        self.nz, self.nx, self.tok, self.cap, self.d = nz, nx, tok, cap, d
        self.dh = d // 2
        self.hz = nz // 2
        self.far = nz // 2
        self.near = nz - 1 - self.far

    def scratch(self):
        nz, nx, cap, d, dh, hz = self.nz, self.nx, self.cap, self.d, self.dh, self.hz
        v = pltpu.VMEM
        steps = max(self.far, 1)
        names = dict(
            grads=v((self.tok, d), BF),
            weight=v((2, 2 * HD, dh), BF),
            picked=v((2, cap, dh + HD), BF),
            rows=v((2 * nx * cap, dh + HD), BF),
            block=v((HD, dh + HD), BF),
            slice_out=v((NY, HD, hz * HD), BF),
            slices=v((NY * HD, hz * HD), BF),
            gates=v((NY, 8, HD), F32),
            proj_part=v((2, HD, 2 * HD), F32),
            proj_in=v((HD, 2 * HD), F32),
            go_out=v((2, HD, HD), BF),
            qh=v((NY, HD, HD), BF),
            goh=v((NY, HD, HD), BF),
            kk=v((nz, 2 * HD, HD), BF),
            vv=v((nz, 2 * HD, HD), BF),
            soft=v((NY, HD + 16, HD), F32),
            soft_in=v((NY, HD + 16, HD), F32),
            lse=v((NY, 8, HD), F32),
            delta=v((NY, 8, HD), F32),
            outs=v((NY * HD, NY * HD), BF),
            dqt=v((NY, HD, HD), F32),
            dkp=v((nz, 2 * HD, HD), F32),
            dvp=v((nz, 2 * HD, HD), F32),
            dwp=v((hz, HD, NY * HD), F32),
            kv_send=v((2, 2, steps, 2 * HD, HD), BF),
            kv_recv=v((2, 2, steps, 2 * HD, HD), BF),
            dw_send=v((2, 2, steps, HD, 2 * HD), BF),
            dw_recv=v((2, 2, steps, HD, 2 * HD), BF),
            kv_fin=v((2, 2, HD, HD), BF),
            dq_out=v((NY, HD, HD), BF),
            dw_fin=v((2, HD, 2 * HD), F32),
            router_out=v((NY, 8, HD), F32),
            router_y=v((NY, 8, HD), F32),
            router_x=v((nx, 8, HD), F32),
        )
        return names


def fused(lay, names, *refs):
    (g_ref, logit_ref, idx_ref, cnt_ref, w_ref, q_ref, k_ref, v_ref) = refs[:8]
    (dq_land, kv_land, dw_land, lg_ref) = refs[8:12]
    buf = dict(zip(names, refs[12 : 12 + len(names)]))
    send_sems, recv_sems, local_sems = refs[12 + len(names) :]
    nz, nx, cap, dh, hz = lay.nz, lay.nx, lay.cap, lay.dh, lay.hz
    shards = 2 * nx
    factor = HD ** (-0.5)

    s, g = lax.axis_index("seq"), lax.axis_index("grp")
    z, y, x, c = s // NY, s % NY, g // 2, g % 2
    sib = 1 - c

    def dev(z_, y_, x_, c_):
        return (z_ * NY + y_, x_ * 2 + c_)

    up, down = (z + 1) % nz, (z + nz - 1) % nz
    dev_up, dev_down = dev(up, y, x, c), dev(down, y, x, c)
    dev_sib = dev(z, y, x, sib)

    counter = {"send": 0, "recv": 0, "local": 0}

    def alloc(kind, n=1):
        first = counter[kind]
        counter[kind] += n
        return first

    ids = {}

    def ident(*key):
        if key not in ids:
            ids[key] = alloc("recv")
        return ids[key]

    pool = [None] * POOL
    singles = []

    def wait_sent(entry):
        unless, copy = entry
        if unless is None:
            copy.wait_send()
        else:
            pl.when(jnp.logical_not(unless))(lambda: copy.wait_send())

    def send(src, dst, recv_id, to, unless=None, single=False):
        if single:
            slot = POOL + len(singles)
        else:
            slot = alloc("send") % POOL
            if pool[slot] is not None:
                wait_sent(pool[slot])
        copy = pltpu.make_async_remote_copy(
            src_ref=src,
            dst_ref=dst,
            send_sem=send_sems.at[slot],
            recv_sem=recv_sems.at[recv_id],
            device_id=to,
            device_id_type=MESH,
        )
        if single:
            singles.append((unless, copy))
        else:
            pool[slot] = (unless, copy)
        if unless is None:
            copy.start()
        else:
            pl.when(jnp.logical_not(unless))(lambda: copy.start())

    def keep(src, dst, recv_id, own):
        copy = pltpu.make_async_copy(src, dst, recv_sems.at[recv_id])
        pl.when(own)(lambda: copy.start())

    def recv(dst, recv_id, unless=None):
        copy = pltpu.make_async_remote_copy(
            src_ref=dst,
            dst_ref=dst,
            send_sem=send_sems.at[0],
            recv_sem=recv_sems.at[recv_id],
            device_id=dev_sib,
            device_id_type=MESH,
        )
        if unless is None:
            copy.wait_recv()
        else:
            pl.when(jnp.logical_not(unless))(lambda: copy.wait_recv())

    grads_in = pltpu.make_async_copy(g_ref, buf["grads"], local_sems.at[alloc("local")])
    grads_in.start()
    own_half = pl.multiple_of(c * dh, HD)
    other_half = pl.multiple_of(sib * dh, HD)
    weight_in = pltpu.make_async_copy(
        w_ref.at[:, pl.ds(own_half, dh)], buf["weight"].at[c], local_sems.at[alloc("local")]
    )
    weight_in.start()

    partners = [dev_sib, dev_up, dev_down]
    for dy in range(1, NY):
        for cc in range(2):
            partners.append(dev(z, (y + dy) % NY, x, cc))
    for dx in range(1, nx):
        for cc in range(2):
            partners.append(dev(z, y, (x + dx) % nx, cc))
    barrier = pltpu.get_barrier_semaphore()
    for partner in partners:
        pl.semaphore_signal(barrier, inc=1, device_id=partner, device_id_type=MESH)
    pl.semaphore_wait(barrier, len(partners))

    half_y = y // 2
    id_k, id_v, id_q = alloc("recv"), alloc("recv"), alloc("recv")
    for src, name, base in ((k_ref, "kk", id_k), (v_ref, "vv", id_v)):
        for j in range(2):
            y_to = 2 * c + j
            own = jnp.logical_and(y_to == y, half_y == c)
            part = pl.ds(pl.multiple_of((y % 2) * HD, HD), HD)
            mine, dst = src.at[:, j * HD : (j + 1) * HD], buf[name].at[z, part, :]
            send(mine, dst, base, dev(z, y_to, x, half_y), own)
            keep(mine, dst, base, own)
    for j in range(2):
        y_to = 2 * c + j
        for cc in range(2):
            own = jnp.logical_and(y_to == y, c == cc)
            mine, dst = q_ref.at[:, j * HD : (j + 1) * HD], buf["qh"].at[y]
            send(mine, dst, id_q, dev(z, y_to, x, cc), own)
            keep(mine, dst, id_q, own)
    id_w = alloc("recv")
    send(w_ref.at[:, pl.ds(other_half, dh)], buf["weight"].at[c], id_w, dev_sib, single=True)

    slot = lax.broadcasted_iota(jnp.int32, (cap, HD), 0)
    lane = lax.broadcasted_iota(jnp.int32, (cap, HD), 1)
    index = jnp.zeros((cap, HD), jnp.int32)
    for j in range(cap):
        index = jnp.where(slot == j, idx_ref[j], index)
    first = s * shards
    starts, total = [], jnp.int32(0)
    counts = []
    for i in range(shards):
        starts.append(total)
        counts.append(cnt_ref[first + i])
        total = total + counts[-1]
    own_start, own_count = jnp.int32(0), jnp.int32(0)
    for i in range(shards):
        own_start = jnp.where(g == i, starts[i], own_start)
        own_count = jnp.where(g == i, counts[i], own_count)
    pick = jnp.logical_and(index == lane, slot < own_count)
    pick_bf = pick.astype(F32).astype(BF)
    logit_row = logit_ref[...]
    chosen_logit = jnp.sum(
        jnp.where(pick, jnp.broadcast_to(logit_row, (cap, HD)), 0.0), axis=1, keepdims=True
    )
    gate_col = 1.0 / (1.0 + jnp.exp(-chosen_logit))
    gate_tile = jnp.broadcast_to(gate_col, (cap, HD)).astype(BF)
    grads_in.wait()
    for h in range(2):
        buf["picked"][h, :, pl.ds(dh, HD)] = gate_tile
    for h in range(2):
        buf["picked"][h, :, pl.ds(0, dh)] = dot(
            pick_bf, buf["grads"][:, h * dh : (h + 1) * dh], 1, 0
        ).astype(BF)

    right, left = (x + 1) % nx, (x + nx - 1) % nx
    rows = buf["rows"]

    def row_slot(shard):
        return rows.at[pl.ds(pl.multiple_of(shard * cap, cap), cap), :]

    id_rows_sib = alloc("recv")
    id_step_one = alloc("recv", 4)
    id_from_left, id_from_right = id_step_one, id_step_one + 2
    id_far = alloc("recv")
    send(buf["picked"].at[sib], row_slot(g), id_rows_sib, dev_sib, single=True)
    if nx > 1:
        for to, side in ((jnp.where(c == 0, right, left), c), (jnp.where(c == 0, left, right), sib)):
            for h in range(2):
                dst, recv_id = row_slot(g), id_step_one + 2 * side + c
                send(buf["picked"].at[h], dst, recv_id, dev(z, y, to, h), single=True)
    rows[pl.ds(pl.multiple_of(g * cap, cap), cap), :] = buf["picked"][c]

    buf["dkp"][...] = jnp.zeros_like(buf["dkp"])
    buf["dvp"][...] = jnp.zeros_like(buf["dvp"])
    buf["dqt"][...] = jnp.zeros_like(buf["dqt"])
    soft = buf["soft"]
    soft[...] = jnp.zeros_like(soft)
    for i in range(NY):
        soft[i, HD : HD + 8, :] = jnp.full((8, HD), NEG, F32)

    recv(buf["kk"].at[z], id_k)
    recv(buf["vv"].at[z], id_v)

    halves = (slice(0, HD), slice(HD, 2 * HD))
    ring = [
        (name, half, n_up, n_down)
        for name, n_up, n_down in (("kk", lay.far, lay.near), ("vv", lay.near, lay.far))
        for half in range(2)
    ]

    def ring_step(t):
        for name, half, n_up, n_down in ring:
            for side, hops in ((0, n_up), (1, n_down)):
                b = (z + nz - t) % nz if side == 0 else (z + t) % nz
                ref = buf[name].at[b, halves[half], :]
                if 1 <= t <= hops:
                    recv(ref, ident(name, half, t, side))
                if t + 1 <= hops:
                    to = dev_up if side == 0 else dev_down
                    send(ref, ref, ident(name, half, t + 1, side), to)

    ring_step(0)

    def allowed(i):
        key = c * 2 * HD + lax.broadcasted_iota(jnp.int32, (2 * HD, HD), 0)
        query = i * HD + lax.broadcasted_iota(jnp.int32, (2 * HD, HD), 1)
        return key <= query

    def forward_block(b, diagonal):
        keys, values = buf["kk"][b], buf["vv"][b]
        for i in range(NY):
            scores = dot(keys, buf["qh"][i], 1, 1) * factor
            if diagonal:
                scores = jnp.where(allowed(i), scores, NEG)
            old = soft[i, HD : HD + 1, :]
            new = jnp.maximum(old, jnp.max(scores, axis=0, keepdims=True))
            weights = jnp.exp(scores - new)
            decay = jnp.exp(old - new)
            norm = soft[i, HD + 8 : HD + 9, :] * decay + jnp.sum(weights, axis=0, keepdims=True)
            soft[i, 0:HD, :] = soft[i, 0:HD, :] * decay + dot(values, weights.astype(BF), 0, 0)
            soft[i, HD : HD + 1, :] = new
            soft[i, HD + 8 : HD + 9, :] = norm

    def forward_pair(t):
        pl.when(z >= t)(lambda: forward_block((z + nz - t) % nz, False))
        if t <= nz - 1 - t:
            pl.when(z + t >= nz)(lambda: forward_block((z + t) % nz, False))

    def rows_step_two():
        if nx == 1:
            return
        for cc in range(2):
            recv(row_slot(2 * left + cc), id_from_left + cc)
            recv(row_slot(2 * right + cc), id_from_right + cc)
        send(row_slot(2 * left), row_slot(2 * left), id_far, dev(z, y, right, c), single=True)
        ref = row_slot(2 * right + 1)
        send(ref, ref, id_far, dev(z, y, left, c), single=True)

    id_slice, id_proj, id_go = alloc("recv"), alloc("recv"), alloc("recv")
    id_gate = alloc("recv")
    row_iota = lax.broadcasted_iota(jnp.int32, (HD, shards * cap), 0)

    def project():
        recv(row_slot(2 * x + sib), id_rows_sib)
        if nx > 1:
            recv(rows.at[pl.ds(0, 2 * cap), :], id_far)
        lanes = lax.broadcasted_iota(jnp.int32, (1, shards * cap), 1)
        place = jnp.full((1, shards * cap), -1, jnp.int32)
        for i in range(shards):
            within = lanes - i * cap
            live = jnp.logical_and(within >= 0, within < counts[i])
            place = jnp.where(live, starts[i] + within, place)
        compact = (row_iota == place).astype(F32).astype(BF)
        block = buf["block"]
        block[...] = dot(compact, rows[...], 1, 0).astype(BF)
        for i in range(hz):
            for yy in range(NY):
                k = i * NY + yy
                buf["slice_out"][yy, :, i * HD : (i + 1) * HD] = block[:, k * HD : (k + 1) * HD]
        gate_rows = block[:, dh:].astype(F32).T
        buf["gates"][y] = gate_rows[0:8, :]
        for dy in range(1, NY):
            y_to = (y + dy) % NY
            send(buf["gates"].at[y], buf["gates"].at[y], id_gate, dev(z, y_to, x, c))
        weight_in.wait()
        recv(buf["weight"].at[sib], id_w)
        part = buf["proj_part"]
        part[sib] = dot(block[:, :dh], buf["weight"][sib], 1, 1)
        send(part.at[sib], buf["proj_in"], id_proj, dev_sib)
        part[c] = dot(block[:, :dh], buf["weight"][c], 1, 1)

    def out_gradient():
        recv(buf["proj_in"], id_proj)
        total = buf["proj_part"][c] + buf["proj_in"][...]
        gate = buf["block"][:, dh:].astype(F32)
        for j in range(2):
            buf["go_out"][j] = (gate * total[:, j * HD : (j + 1) * HD]).astype(BF)
        for j in range(2):
            y_to = 2 * c + j
            for cc in range(2):
                own = jnp.logical_and(y_to == y, c == cc)
                send(buf["go_out"].at[j], buf["goh"].at[y], id_go, dev(z, y_to, x, cc), own)
                keep(buf["go_out"].at[j], buf["goh"].at[y], id_go, own)

        for dy in range(1, NY):
            y_to = (y + dy) % NY
            mine = pl.ds(pl.multiple_of(y * HD, HD), HD)
            send(
                buf["slice_out"].at[y_to],
                buf["slices"].at[mine, :],
                id_slice,
                dev(z, y_to, x, c),
                single=True,
            )
        buf["slices"][mine, :] = buf["slice_out"][y]

    rows_step_two()
    recv(buf["qh"], id_q)
    forward_block(z, True)
    for t in range(1, lay.far + 1):
        ring_step(t)
        if t == min(2, lay.far):
            project()
            out_gradient()
        forward_pair(t)

    id_soft = alloc("recv")
    send(soft, buf["soft_in"], id_soft, dev_sib)
    recv(buf["goh"], id_go)
    recv(buf["gates"].at[pl.ds(0, NY - 1)], id_gate)
    recv(buf["soft_in"], id_soft)
    head_cols = pl.ds(pl.multiple_of(y * HD, HD), HD)
    soft_in = buf["soft_in"]
    for i in range(NY):
        max_a, max_b = soft[i, HD : HD + 1, :], soft_in[i, HD : HD + 1, :]
        top = jnp.maximum(max_a, max_b)
        scale_a, scale_b = jnp.exp(max_a - top), jnp.exp(max_b - top)
        norm = soft[i, HD + 8 : HD + 9, :] * scale_a + soft_in[i, HD + 8 : HD + 9, :] * scale_b
        out_t = (soft[i, 0:HD, :] * scale_a + soft_in[i, 0:HD, :] * scale_b) / norm
        out_t = out_t.astype(BF).astype(F32)
        gate_row = buf["gates"][i, 0:1, :]
        buf["outs"][i * HD : (i + 1) * HD, head_cols] = (gate_row * out_t).T.astype(BF)
        buf["lse"][i, 0:1, :] = top + jnp.log(norm)
        delta = jnp.sum(out_t * buf["goh"][i].astype(F32).T, axis=0, keepdims=True)
        buf["delta"][i, 0:1, :] = delta
        buf["router_out"][i] = jnp.broadcast_to(delta / gate_row, (8, HD))

    id_outs, id_outs_sib, id_router_y = alloc("recv"), alloc("recv"), alloc("recv")

    def out_part(head, core):
        return buf["outs"].at[
            pl.ds(pl.multiple_of(core * 2 * HD, HD), 2 * HD),
            pl.ds(pl.multiple_of(head * HD, HD), HD),
        ]

    for dy in range(1, NY):
        y_to = (y + dy) % NY
        to = dev(z, y_to, x, c)
        send(out_part(y, c), out_part(y, c), id_outs, to)
        send(buf["router_out"].at[y_to], buf["router_y"].at[y], id_router_y, to)
    buf["router_y"][y] = buf["router_out"][y]

    def backward_block(b, diagonal):
        keys, values = buf["kk"][b], buf["vv"][b]
        for i in range(NY):
            queries, go = buf["qh"][i], buf["goh"][i]
            scores = dot(keys, queries, 1, 1) * factor
            weights = jnp.exp(scores - buf["lse"][i, 0:1, :])
            if diagonal:
                weights = jnp.where(allowed(i), weights, 0.0)
            grad_weights = dot(values, go, 1, 1)
            grad_scores = (weights * (grad_weights - buf["delta"][i, 0:1, :])).astype(BF)
            value_part = dot(weights.astype(BF), go, 1, 0)
            key_part = dot(grad_scores, queries, 1, 0)
            if i == 0:
                buf["dvp"][b] = value_part
                buf["dkp"][b] = key_part
            else:
                buf["dvp"][b] += value_part
                buf["dkp"][b] += key_part
            buf["dqt"][i] += dot(keys, grad_scores, 0, 0)

    def backward_pair(t):
        pl.when(z >= t)(lambda: backward_block((z + nz - t) % nz, False))
        if t <= nz - 1 - t:
            pl.when(z + t >= nz)(lambda: backward_block((z + t) % nz, False))

    hops = ((lay.far, lay.near), (lay.near, lay.far))

    def target(direction, d):
        return (z + nz - d) % nz if direction == 0 else (z + d) % nz

    dev_next = (dev_down, dev_up)

    def kv_step(t):
        inc = buf["kv_recv"]
        for kind in range(2):
            for part in halves:
                for direction in range(2):
                    n = hops[kind][direction]
                    if t >= n:
                        continue
                    key = ("chain", kind, direction, part.start)
                    b = target(direction, n - t)
                    total = (buf["dkp"] if kind == 0 else buf["dvp"])[b, part, :]
                    if t > 0:
                        recv(inc.at[kind, direction, t - 1, part, :], ident(*key, t - 1))
                        total = total + inc[kind, direction, t - 1, part, :].astype(F32)
                    out = buf["kv_send"].at[kind, direction, t, part, :]
                    out[...] = total.astype(BF)
                    to = dev_next[direction]
                    send(out, inc.at[kind, direction, t, part, :], ident(*key, t), to)

    def kv_last(kind, part):
        inc = buf["kv_recv"]
        total = (buf["dkp"] if kind == 0 else buf["dvp"])[z, part, :]
        for direction in range(2):
            n = hops[kind][direction]
            if n > 0:
                last = ident("chain", kind, direction, part.start, n - 1)
                recv(inc.at[kind, direction, n - 1, part, :], last)
                total = total + inc[kind, direction, n - 1, part, :].astype(F32)
        return total

    def dw_step(t):
        inc = buf["dw_recv"]
        for half in range(2):
            for direction in range(2):
                n = hops[half][direction]
                if t >= n:
                    continue
                b = target(direction, n - t)
                skip = b // hz != c
                out = buf["dw_send"].at[half, direction, t]
                if t > 0:
                    recv(inc.at[half, direction, t - 1], ident("dw", half, direction, t - 1), skip)

                @pl.when(jnp.logical_not(skip))
                def _():
                    total = buf["dwp"][b % hz, :, half * 2 * HD : (half + 1) * 2 * HD]
                    if t > 0:
                        total = total + inc[half, direction, t - 1].astype(F32)
                    out[...] = total.astype(BF)

                to = dev_next[direction]
                send(out, inc.at[half, direction, t], ident("dw", half, direction, t), to, skip)

    def share_outs():
        recv(buf["outs"].at[: 2 * HD, : (NY - 1) * HD], id_outs)
        for dy in range(1, NY):
            ref = out_part((y + dy) % NY, c)
            send(ref, ref, id_outs_sib, dev_sib)

    def weight_gradient():
        recv(buf["slices"].at[: (NY - 1) * HD, :], id_slice)
        recv(buf["outs"].at[: 2 * HD, : (NY - 1) * HD], id_outs_sib)
        for i in range(hz):
            part = buf["slices"][:, i * HD : (i + 1) * HD]
            buf["dwp"][i] = dot(part, buf["outs"][...], 0, 0)

    id_router_x = alloc("recv")

    def router_send():
        recv(buf["router_y"].at[: NY - 1], id_router_y)
        total = buf["router_y"][0]
        for i in range(1, NY):
            total = total + buf["router_y"][i]
        buf["router_x"][x] = total
        for dx in range(1, nx):
            x_to = (x + dx) % nx
            ref = buf["router_x"].at[x]
            send(ref, ref, id_router_x, dev(z, y, x_to, c))

    def router_last():
        if nx > 1:
            recv(buf["router_x"].at[: nx - 1], id_router_x)
        total = buf["router_x"][0]
        for i in range(1, nx):
            total = total + buf["router_x"][i]
        token_row = lax.broadcasted_iota(jnp.int32, (HD, cap), 0)
        token_slot = lax.broadcasted_iota(jnp.int32, (HD, cap), 1)
        own = jnp.logical_and(token_row == own_start + token_slot, token_slot < own_count)
        spread = dot(own.astype(F32).astype(BF), pick_bf, 1, 0)
        placed = dot(total, spread, 1, 0, lax.Precision.HIGHEST)
        sig = 1.0 / (1.0 + jnp.exp(-logit_row))
        lg_ref[...] = placed[0:1, :] * sig * (1.0 - sig)

    id_kv_fin, id_dq = alloc("recv"), alloc("recv")
    id_dw_fin = alloc("recv")
    side = y % 2

    def send_key_value_grads():
        for kind in range(2):
            for j in range(2):
                final = kv_last(kind, halves[j])
                if kind == 0:
                    final = final * factor
                buf["kv_fin"][kind, j] = final.astype(BF)
                y_to = 2 * c + j
                own = jnp.logical_and(y_to == y, half_y == c)
                src, dst = buf["kv_fin"].at[kind, j], kv_land.at[kind, side]
                send(src, dst, id_kv_fin, dev(z, y_to, x, half_y), own)
                keep(src, dst, id_kv_fin, own)

    def send_query_grads():
        for i in range(NY):
            buf["dq_out"][i] = (buf["dqt"][i].T * factor).astype(BF)
            own = jnp.logical_and(y == i, half_y == c)
            src, dst = buf["dq_out"].at[i], dq_land.at[side, c]
            send(src, dst, id_dq, dev(z, i, x, half_y), own)
            keep(src, dst, id_dq, own)

    for d in range(lay.far, 0, -1):
        backward_pair(d)
        if d == max(lay.near, 1):
            kv_step(0)
    backward_block(z, True)
    send_query_grads()
    if lay.far > 1:
        kv_step(1)
    share_outs()
    router_send()
    weight_gradient()
    dw_step(0)
    for t in range(2, lay.far):
        kv_step(t)
        dw_step(t - 1)
    send_key_value_grads()
    router_last()
    if lay.far > 1:
        dw_step(lay.far - 1)

    skip = z // hz != c
    holder = jnp.logical_not(skip)
    for half in range(2):
        for direction in range(2):
            n = hops[half][direction]
            if n > 0:
                key = ident("dw", half, direction, n - 1)
                recv(buf["dw_recv"].at[half, direction, n - 1], key, skip)

    @pl.when(holder)
    def _():
        for half in range(2):
            total = buf["dwp"][z % hz, :, half * 2 * HD : (half + 1) * 2 * HD]
            for direction in range(2):
                n = hops[half][direction]
                if n > 0:
                    total = total + buf["dw_recv"][half, direction, n - 1].astype(F32)
            buf["dw_fin"][half] = total

    send(buf["dw_fin"].at[sib], dw_land, id_dw_fin, dev_sib, skip)
    keep(buf["dw_fin"].at[c], dw_land, id_dw_fin, holder)

    recv(dq_land, id_dq)
    recv(kv_land, id_kv_fin)
    recv(dw_land, id_dw_fin)
    for entry in pool + singles:
        if entry is not None:
            wait_sent(entry)


POOL = 24
RECV_SEMS = 92
SEND_SEMS = 35
VMEM_LIMIT = 60 * 1024 * 1024


def finish(dq_land, kv_land, dw_land, lg_in, dq_ref, dk_ref, dv_ref, dw_ref, lg_ref):
    for j in range(2):
        cols = slice(j * HD, (j + 1) * HD)
        dq_ref[:, cols] = (dq_land[j, 0].astype(F32) + dq_land[j, 1].astype(F32)).astype(BF)
        dk_ref[:, cols] = kv_land[0, j]
        dv_ref[:, cols] = kv_land[1, j]
    dw_ref[...] = dw_land[...]
    lg_ref[...] = lg_in[...]


def shards_fn(nz, nx):
    def run(grad, logit, index, count, weight, q, k, v):
        lay = Layout(nz, nx, grad.shape[0], index.shape[0], grad.shape[1])
        scratch = lay.scratch()
        names = list(scratch)
        any_ = pl.BlockSpec(memory_space=pl.ANY)
        smem = pl.BlockSpec(memory_space=pltpu.SMEM)
        vmem = pl.BlockSpec(memory_space=pltpu.VMEM)

        def kernel(*refs):
            fused(lay, names, *refs)

        lands = pl.pallas_call(
            kernel,
            out_shape=(
                jax.ShapeDtypeStruct((2, 2, HD, HD), BF),
                jax.ShapeDtypeStruct((2, 2, HD, HD), BF),
                jax.ShapeDtypeStruct((HD, 2 * HD), F32),
                jax.ShapeDtypeStruct((1, HD), F32),
            ),
            in_specs=[any_, vmem, smem, smem, any_, any_, any_, any_],
            out_specs=(any_, any_, any_, vmem),
            scratch_shapes=list(scratch.values())
            + [
                pltpu.SemaphoreType.DMA((SEND_SEMS,)),
                pltpu.SemaphoreType.DMA((RECV_SEMS,)),
                pltpu.SemaphoreType.DMA((2,)),
            ],
            compiler_params=pltpu.CompilerParams(
                collective_id=0, has_side_effects=True, vmem_limit_bytes=VMEM_LIMIT
            ),
            name="routed_backward",
        )(grad, logit.reshape(1, -1), index, count, weight, q, k, v)
        out = pl.pallas_call(
            finish,
            out_shape=(
                jax.ShapeDtypeStruct(q.shape, BF),
                jax.ShapeDtypeStruct(q.shape, BF),
                jax.ShapeDtypeStruct(q.shape, BF),
                jax.ShapeDtypeStruct((HD, q.shape[1]), F32),
                jax.ShapeDtypeStruct((1, HD), F32),
            ),
            in_specs=[vmem] * 4,
            out_specs=(vmem,) * 5,
            compiler_params=pltpu.CompilerParams(vmem_limit_bytes=VMEM_LIMIT),
            name="finish",
        )(*lands)
        return (*out[:4], out[4].reshape(-1))

    return run


def solution(mesh):
    nz = mesh.shape["seq"] // NY
    nx = mesh.shape["grp"] // 2
    placed = (
        P(("seq", "grp"), None),
        P(("seq", "grp")),
        P(("seq", "grp")),
        P(),
        P("grp", None),
        P("seq", "grp"),
        P("seq", "grp"),
        P("seq", "grp"),
    )
    return jax.shard_map(
        shards_fn(nz, nx),
        mesh=mesh,
        in_specs=placed,
        out_specs=(
            P("seq", "grp"),
            P("seq", "grp"),
            P("seq", "grp"),
            P("seq", "grp"),
            P(("seq", "grp")),
        ),
        check_vma=False,
    )
```

```python
import jax
import jax.numpy as jnp
from jax import lax
from jax.experimental import pallas as pl
from jax.experimental.pallas import tpu as pltpu
from jax.sharding import PartitionSpec as P

HD = 128
NY = 4
MESH = pl.DeviceIdType.MESH
BF = jnp.bfloat16
F32 = jnp.float32
NEG = -1e30
LOG2E = 1.4426950408889634


def dot(a, b, ca, cb, precision=None):
    return lax.dot_general(
        a, b, (((ca,), (cb,)), ((), ())), preferred_element_type=F32, precision=precision
    )


class Layout:
    def __init__(self, nz, nx, tok, cap, d):
        self.nz, self.nx, self.tok, self.cap, self.d = nz, nx, tok, cap, d
        self.dh = d // 2
        self.hz = nz // 2
        self.far = nz // 2
        self.near = nz - 1 - self.far

    def scratch(self):
        nz, nx, cap, d, dh, hz = self.nz, self.nx, self.cap, self.d, self.dh, self.hz
        v = pltpu.VMEM
        steps = max(self.far, 1)
        names = dict(
            grads=v((self.tok, d), BF),
            weight=v((2, 2 * HD, dh), BF),
            picked=v((2, cap, dh + HD), BF),
            rows=v((2 * nx * cap, dh + HD), BF),
            block=v((HD, dh + HD), BF),
            slice_out=v((NY, HD, hz * HD), BF),
            slices=v((NY * HD, hz * HD), BF),
            gates=v((NY, 8, HD), F32),
            proj_part=v((2, HD, 2 * HD), F32),
            proj_in=v((HD, 2 * HD), F32),
            go_out=v((2, HD, HD), BF),
            qh=v((NY * HD, HD), BF),
            goh=v((NY * HD, HD), BF),
            kk=v((nz, 2 * HD, HD), BF),
            vv=v((nz, 2 * HD, HD), BF),
            soft=v((HD + 16, NY * HD), F32),
            soft_in=v((HD + 16, NY * HD), F32),
            lse=v((8, NY * HD), F32),
            delta=v((8, NY * HD), F32),
            outs=v((NY * HD, NY * HD), BF),
            dqt=v((HD, NY * HD), F32),
            dkp=v((nz, 2 * HD, HD), F32),
            dvp=v((nz, 2 * HD, HD), F32),
            dw_mine=v((2, HD, 2 * HD), F32),
            dw_own=v((HD, 2 * HD), F32),
            kv_send=v((2, 2, steps, 2 * HD, HD), BF),
            kv_recv=v((2, 2, steps, 2 * HD, HD), BF),
            dw_send=v((2, 2, steps, HD, 2 * HD), BF),
            dw_recv=v((2, 2, steps, HD, 2 * HD), BF),
            kv_fin=v((2, 2, HD, HD), BF),
            dq_out=v((NY, HD, HD), BF),
            dw_fin=v((HD, 2 * HD), F32),
            router_out=v((NY, 8, HD), F32),
            router_y=v((NY, 8, HD), F32),
            router_x=v((nx, 8, HD), F32),
        )
        return names


def fused(lay, names, *refs):
    (g_ref, logit_ref, idx_ref, cnt_ref, w_ref, q_ref, k_ref, v_ref) = refs[:8]
    (dq_land, kv_land, dw_land, lg_ref) = refs[8:12]
    buf = dict(zip(names, refs[12 : 12 + len(names)]))
    send_sems, recv_sems, local_sems = refs[12 + len(names) :]
    nz, nx, cap, dh, hz = lay.nz, lay.nx, lay.cap, lay.dh, lay.hz
    shards = 2 * nx
    factor = HD ** (-0.5)

    s, g = lax.axis_index("seq"), lax.axis_index("grp")
    z, y, x, c = s // NY, s % NY, g // 2, g % 2
    sib = 1 - c

    def dev(z_, y_, x_, c_):
        return (z_ * NY + y_, x_ * 2 + c_)

    up, down = (z + 1) % nz, (z + nz - 1) % nz
    dev_up, dev_down = dev(up, y, x, c), dev(down, y, x, c)
    dev_sib = dev(z, y, x, sib)
    my_rows = pl.ds(pl.multiple_of(y * HD, HD), HD)

    counter = {"send": 0, "recv": 0, "local": 0}

    def alloc(kind, n=1):
        first = counter[kind]
        counter[kind] += n
        return first

    ids = {}

    def ident(*key):
        if key not in ids:
            ids[key] = alloc("recv")
        return ids[key]

    pool = [None] * POOL
    singles = []

    def wait_sent(entry):
        unless, copy = entry
        if unless is None:
            copy.wait_send()
        else:
            pl.when(jnp.logical_not(unless))(lambda: copy.wait_send())

    def send(src, dst, recv_id, to, unless=None, single=False):
        if single:
            slot = POOL + len(singles)
        else:
            slot = alloc("send") % POOL
            if pool[slot] is not None:
                wait_sent(pool[slot])
        copy = pltpu.make_async_remote_copy(
            src_ref=src,
            dst_ref=dst,
            send_sem=send_sems.at[slot],
            recv_sem=recv_sems.at[recv_id],
            device_id=to,
            device_id_type=MESH,
        )
        if single:
            singles.append((unless, copy))
        else:
            pool[slot] = (unless, copy)
        if unless is None:
            copy.start()
        else:
            pl.when(jnp.logical_not(unless))(lambda: copy.start())

    def keep(src, dst, recv_id, own):
        copy = pltpu.make_async_copy(src, dst, recv_sems.at[recv_id])
        pl.when(own)(lambda: copy.start())

    def recv(dst, recv_id, unless=None):
        copy = pltpu.make_async_remote_copy(
            src_ref=dst,
            dst_ref=dst,
            send_sem=send_sems.at[0],
            recv_sem=recv_sems.at[recv_id],
            device_id=dev_sib,
            device_id_type=MESH,
        )
        if unless is None:
            copy.wait_recv()
        else:
            pl.when(jnp.logical_not(unless))(lambda: copy.wait_recv())

    grads_in = pltpu.make_async_copy(g_ref, buf["grads"], local_sems.at[alloc("local")])
    grads_in.start()
    own_half = pl.multiple_of(c * dh, HD)
    other_half = pl.multiple_of(sib * dh, HD)
    weight_in = pltpu.make_async_copy(
        w_ref.at[:, pl.ds(own_half, dh)], buf["weight"].at[c], local_sems.at[alloc("local")]
    )
    weight_in.start()

    partners = [dev_sib, dev_up, dev_down]
    for dy in range(1, NY):
        for cc in range(2):
            partners.append(dev(z, (y + dy) % NY, x, cc))
    for dx in range(1, nx):
        for cc in range(2):
            partners.append(dev(z, y, (x + dx) % nx, cc))
    barrier = pltpu.get_barrier_semaphore()
    for partner in partners:
        pl.semaphore_signal(barrier, inc=1, device_id=partner, device_id_type=MESH)
    pl.semaphore_wait(barrier, len(partners))

    half_y = y // 2
    id_k, id_v, id_q = alloc("recv"), alloc("recv"), alloc("recv")
    for src, name, base in ((k_ref, "kk", id_k), (v_ref, "vv", id_v)):
        for j in range(2):
            y_to = 2 * c + j
            own = jnp.logical_and(y_to == y, half_y == c)
            part = pl.ds(pl.multiple_of((y % 2) * HD, HD), HD)
            mine, dst = src.at[:, j * HD : (j + 1) * HD], buf[name].at[z, part, :]
            send(mine, dst, base, dev(z, y_to, x, half_y), own)
            keep(mine, dst, base, own)
    for j in range(2):
        y_to = 2 * c + j
        for cc in range(2):
            own = jnp.logical_and(y_to == y, c == cc)
            mine, dst = q_ref.at[:, j * HD : (j + 1) * HD], buf["qh"].at[my_rows, :]
            send(mine, dst, id_q, dev(z, y_to, x, cc), own)
            keep(mine, dst, id_q, own)
    id_w = alloc("recv")
    send(w_ref.at[:, pl.ds(other_half, dh)], buf["weight"].at[c], id_w, dev_sib, single=True)

    slot = lax.broadcasted_iota(jnp.int32, (cap, HD), 0)
    lane = lax.broadcasted_iota(jnp.int32, (cap, HD), 1)
    index = jnp.zeros((cap, HD), jnp.int32)
    for j in range(cap):
        index = jnp.where(slot == j, idx_ref[j], index)
    first = s * shards
    starts, total = [], jnp.int32(0)
    counts = []
    for i in range(shards):
        starts.append(total)
        counts.append(cnt_ref[first + i])
        total = total + counts[-1]
    own_start, own_count = jnp.int32(0), jnp.int32(0)
    for i in range(shards):
        own_start = jnp.where(g == i, starts[i], own_start)
        own_count = jnp.where(g == i, counts[i], own_count)
    pick = jnp.logical_and(index == lane, slot < own_count)
    pick_bf = pick.astype(F32).astype(BF)
    logit_row = logit_ref[...]
    chosen_logit = jnp.sum(
        jnp.where(pick, jnp.broadcast_to(logit_row, (cap, HD)), 0.0), axis=1, keepdims=True
    )
    gate_col = 1.0 / (1.0 + jnp.exp(-chosen_logit))
    gate_tile = jnp.broadcast_to(gate_col, (cap, HD)).astype(BF)
    grads_in.wait()
    for h in range(2):
        buf["picked"][h, :, pl.ds(dh, HD)] = gate_tile
    for h in range(2):
        buf["picked"][h, :, pl.ds(0, dh)] = dot(
            pick_bf, buf["grads"][:, h * dh : (h + 1) * dh], 1, 0
        ).astype(BF)

    right, left = (x + 1) % nx, (x + nx - 1) % nx
    rows = buf["rows"]

    def row_slot(shard):
        return rows.at[pl.ds(pl.multiple_of(shard * cap, cap), cap), :]

    id_rows_sib = alloc("recv")
    id_step_one = alloc("recv", 4)
    id_from_left, id_from_right = id_step_one, id_step_one + 2
    id_far = alloc("recv")
    send(buf["picked"].at[sib], row_slot(g), id_rows_sib, dev_sib, single=True)
    if nx > 1:
        for to, side in ((jnp.where(c == 0, right, left), c), (jnp.where(c == 0, left, right), sib)):
            for h in range(2):
                dst, recv_id = row_slot(g), id_step_one + 2 * side + c
                send(buf["picked"].at[h], dst, recv_id, dev(z, y, to, h), single=True)
    rows[pl.ds(pl.multiple_of(g * cap, cap), cap), :] = buf["picked"][c]

    buf["dkp"][...] = jnp.zeros_like(buf["dkp"])
    buf["dvp"][...] = jnp.zeros_like(buf["dvp"])
    buf["dqt"][...] = jnp.zeros_like(buf["dqt"])
    soft = buf["soft"]
    soft[...] = jnp.zeros_like(soft)
    soft[HD : HD + 8, :] = jnp.full((8, NY * HD), NEG, F32)

    halves = (slice(0, HD), slice(HD, 2 * HD))
    ring = [
        (name, half, n_up, n_down)
        for name, n_up, n_down in (("kk", lay.far, lay.near), ("vv", lay.near, lay.far))
        for half in range(2)
    ]

    def ring_step(t):
        for name, half, n_up, n_down in ring:
            if t == 0 and half == 0:
                recv(buf[name].at[z], id_k if name == "kk" else id_v)
            for side, hops in ((0, n_up), (1, n_down)):
                b = (z + nz - t) % nz if side == 0 else (z + t) % nz
                ref = buf[name].at[b, halves[half], :]
                if 1 <= t <= hops:
                    recv(ref, ident(name, half, t, side))
                if t + 1 <= hops:
                    to = dev_up if side == 0 else dev_down
                    send(ref, ref, ident(name, half, t + 1, side), to)

    ring_step(0)

    def allowed():
        key = c * 2 * HD + lax.broadcasted_iota(jnp.int32, (2 * HD, NY * HD), 0)
        query = lax.broadcasted_iota(jnp.int32, (2 * HD, NY * HD), 1)
        return key <= query

    factor2 = factor * LOG2E

    def forward_block(b, diagonal):
        keys, values = buf["kk"][b], buf["vv"][b]
        scores = dot(keys, buf["qh"][...], 1, 1) * factor2
        if diagonal:
            scores = jnp.where(allowed(), scores, NEG)
        old = soft[HD : HD + 1, :]
        new = jnp.maximum(old, jnp.max(scores, axis=0, keepdims=True))
        weights = jnp.exp2(scores - new)
        decay = jnp.exp2(old - new)
        norm = soft[HD + 8 : HD + 9, :] * decay + jnp.sum(weights, axis=0, keepdims=True)
        soft[0:HD, :] = soft[0:HD, :] * decay + dot(values, weights.astype(BF), 0, 0)
        soft[HD : HD + 1, :] = new
        soft[HD + 8 : HD + 9, :] = norm

    def forward_pair(t):
        pl.when(z >= t)(lambda: forward_block((z + nz - t) % nz, False))
        if t <= nz - 1 - t:
            pl.when(z + t >= nz)(lambda: forward_block((z + t) % nz, False))

    def rows_step_two():
        if nx == 1:
            return
        for cc in range(2):
            recv(row_slot(2 * left + cc), id_from_left + cc)
            recv(row_slot(2 * right + cc), id_from_right + cc)
        send(row_slot(2 * left), row_slot(2 * left), id_far, dev(z, y, right, c), single=True)
        ref = row_slot(2 * right + 1)
        send(ref, ref, id_far, dev(z, y, left, c), single=True)

    id_slice, id_proj, id_go = alloc("recv"), alloc("recv"), alloc("recv")
    id_gate = alloc("recv")
    row_iota = lax.broadcasted_iota(jnp.int32, (HD, shards * cap), 0)

    def project():
        recv(row_slot(2 * x + sib), id_rows_sib)
        if nx > 1:
            recv(rows.at[pl.ds(0, 2 * cap), :], id_far)
        lanes = lax.broadcasted_iota(jnp.int32, (1, shards * cap), 1)
        place = jnp.full((1, shards * cap), -1, jnp.int32)
        for i in range(shards):
            within = lanes - i * cap
            live = jnp.logical_and(within >= 0, within < counts[i])
            place = jnp.where(live, starts[i] + within, place)
        compact = (row_iota == place).astype(F32).astype(BF)
        block = buf["block"]
        block[...] = dot(compact, rows[...], 1, 0).astype(BF)
        for i in range(hz):
            for yy in range(NY):
                k = i * NY + yy
                buf["slice_out"][yy, :, i * HD : (i + 1) * HD] = block[:, k * HD : (k + 1) * HD]
        gate_rows = block[:, dh:].astype(F32).T
        buf["gates"][y] = gate_rows[0:8, :]
        for dy in range(1, NY):
            y_to = (y + dy) % NY
            send(buf["gates"].at[y], buf["gates"].at[y], id_gate, dev(z, y_to, x, c))
        weight_in.wait()
        recv(buf["weight"].at[sib], id_w)
        part = buf["proj_part"]
        part[sib] = dot(block[:, :dh], buf["weight"][sib], 1, 1)
        send(part.at[sib], buf["proj_in"], id_proj, dev_sib)
        part[c] = dot(block[:, :dh], buf["weight"][c], 1, 1)

    def out_gradient():
        recv(buf["proj_in"], id_proj)
        total = buf["proj_part"][c] + buf["proj_in"][...]
        gate = buf["block"][:, dh:].astype(F32)
        for j in range(2):
            buf["go_out"][j] = (gate * total[:, j * HD : (j + 1) * HD]).astype(BF)
        for j in range(2):
            y_to = 2 * c + j
            for cc in range(2):
                own = jnp.logical_and(y_to == y, c == cc)
                send(buf["go_out"].at[j], buf["goh"].at[my_rows, :], id_go, dev(z, y_to, x, cc), own)
                keep(buf["go_out"].at[j], buf["goh"].at[my_rows, :], id_go, own)

        for dy in range(1, NY):
            y_to = (y + dy) % NY
            send(
                buf["slice_out"].at[y_to],
                buf["slices"].at[my_rows, :],
                id_slice,
                dev(z, y_to, x, c),
                single=True,
            )
        buf["slices"][my_rows, :] = buf["slice_out"][y]

    rows_step_two()
    recv(buf["qh"], id_q)
    forward_block(z, True)
    for t in range(1, lay.far + 1):
        ring_step(t)
        if t == min(2, lay.far):
            project()
            out_gradient()
        forward_pair(t)

    id_soft = alloc("recv")
    send(soft, buf["soft_in"], id_soft, dev_sib)
    recv(buf["goh"], id_go)
    recv(buf["gates"].at[pl.ds(0, NY - 1)], id_gate)
    recv(buf["soft_in"], id_soft)
    head_cols = pl.ds(pl.multiple_of(y * HD, HD), HD)
    soft_in = buf["soft_in"]
    max_a, max_b = soft[HD : HD + 1, :], soft_in[HD : HD + 1, :]
    top = jnp.maximum(max_a, max_b)
    scale_a, scale_b = jnp.exp2(max_a - top), jnp.exp2(max_b - top)
    norm = soft[HD + 8 : HD + 9, :] * scale_a + soft_in[HD + 8 : HD + 9, :] * scale_b
    buf["lse"][0:1, :] = top + jnp.log2(norm)
    scale_a, scale_b = scale_a / norm, scale_b / norm
    for i in range(NY):
        span = slice(i * HD, (i + 1) * HD)
        out_t = soft[0:HD, span] * scale_a[:, span] + soft_in[0:HD, span] * scale_b[:, span]
        out_t = out_t.astype(BF).astype(F32)
        gate_row = buf["gates"][i, 0:1, :]
        buf["outs"][span, head_cols] = (gate_row * out_t).T.astype(BF)
        delta = jnp.sum(out_t * buf["goh"][span, :].astype(F32).T, axis=0, keepdims=True)
        buf["delta"][0:1, span] = delta
        buf["router_out"][i] = jnp.broadcast_to(delta / gate_row, (8, HD))

    id_outs, id_outs_sib, id_router_y = alloc("recv"), alloc("recv"), alloc("recv")

    def out_part(head, core):
        return buf["outs"].at[
            pl.ds(pl.multiple_of(core * 2 * HD, HD), 2 * HD),
            pl.ds(pl.multiple_of(head * HD, HD), HD),
        ]

    for dy in range(1, NY):
        y_to = (y + dy) % NY
        to = dev(z, y_to, x, c)
        send(out_part(y, c), out_part(y, c), id_outs, to)
        send(buf["router_out"].at[y_to], buf["router_y"].at[y], id_router_y, to)
    buf["router_y"][y] = buf["router_out"][y]

    def backward_block(b, diagonal):
        keys, values = buf["kk"][b], buf["vv"][b]
        queries, go = buf["qh"][...], buf["goh"][...]
        scores = dot(keys, queries, 1, 1) * factor2
        weights = jnp.exp2(scores - buf["lse"][0:1, :])
        if diagonal:
            weights = jnp.where(allowed(), weights, 0.0)
        grad_weights = dot(values, go, 1, 1)
        grad_scores = (weights * (grad_weights - buf["delta"][0:1, :])).astype(BF)
        buf["dvp"][b] = dot(weights.astype(BF), go, 1, 0)
        buf["dkp"][b] = dot(grad_scores, queries, 1, 0)
        buf["dqt"][...] += dot(keys, grad_scores, 0, 0)

    def backward_pair(t):
        pl.when(z >= t)(lambda: backward_block((z + nz - t) % nz, False))
        if t <= nz - 1 - t:
            pl.when(z + t >= nz)(lambda: backward_block((z + t) % nz, False))

    hops = ((lay.far, lay.near), (lay.near, lay.far))

    def target(direction, d):
        return (z + nz - d) % nz if direction == 0 else (z + d) % nz

    dev_next = (dev_down, dev_up)

    def kv_step(t):
        inc = buf["kv_recv"]
        for kind in range(2):
            for part in halves:
                for direction in range(2):
                    n = hops[kind][direction]
                    if t >= n:
                        continue
                    key = ("chain", kind, direction, part.start)
                    b = target(direction, n - t)
                    total = (buf["dkp"] if kind == 0 else buf["dvp"])[b, part, :]
                    if t > 0:
                        recv(inc.at[kind, direction, t - 1, part, :], ident(*key, t - 1))
                        total = total + inc[kind, direction, t - 1, part, :].astype(F32)
                    out = buf["kv_send"].at[kind, direction, t, part, :]
                    out[...] = total.astype(BF)
                    to = dev_next[direction]
                    send(out, inc.at[kind, direction, t, part, :], ident(*key, t), to)

    def kv_last(kind, part):
        inc = buf["kv_recv"]
        total = (buf["dkp"] if kind == 0 else buf["dvp"])[z, part, :]
        for direction in range(2):
            n = hops[kind][direction]
            if n > 0:
                last = ident("chain", kind, direction, part.start, n - 1)
                recv(inc.at[kind, direction, n - 1, part, :], last)
                total = total + inc[kind, direction, n - 1, part, :].astype(F32)
        return total

    def dw_part(b, half):
        rows_of = buf["slices"][:, pl.ds(pl.multiple_of((b % hz) * HD, HD), HD)]
        return dot(rows_of, buf["outs"][:, half * 2 * HD : (half + 1) * 2 * HD], 0, 0)

    def dw_step(t):
        inc = buf["dw_recv"]
        for half in range(2):
            for direction in range(2):
                n = hops[half][direction]
                if t >= n:
                    continue
                b = target(direction, n - t)
                skip = b // hz != c
                out = buf["dw_send"].at[half, direction, t]
                if t > 0:
                    recv(inc.at[half, direction, t - 1], ident("dw", half, direction, t - 1), skip)

                @pl.when(jnp.logical_not(skip))
                def _():
                    total = dw_part(b, half)
                    if t > 0:
                        total = total + inc[half, direction, t - 1].astype(F32)
                    out[...] = total.astype(BF)

                to = dev_next[direction]
                if t == n - 1:
                    to = dev(down if direction == 0 else up, y, x, half)
                send(out, inc.at[half, direction, t], ident("dw", half, direction, t), to, skip)

    id_dw_own = alloc("recv")
    not_holder = z // hz != c
    holder = jnp.logical_not(not_holder)

    def dw_own_block():
        @pl.when(holder)
        def _():
            for half in range(2):
                buf["dw_mine"][half] = dw_part(z, half)
            buf["dw_own"][...] = buf["dw_mine"][c]

        send(buf["dw_mine"].at[sib], buf["dw_own"], id_dw_own, dev_sib, not_holder)

    def dw_last():
        recv(buf["dw_own"], id_dw_own, holder)
        for half in range(2):

            @pl.when(c == half)
            def _():
                total = buf["dw_own"][...]
                for direction in range(2):
                    n = hops[half][direction]
                    if n > 0:
                        recv(
                            buf["dw_recv"].at[half, direction, n - 1],
                            ident("dw", half, direction, n - 1),
                        )
                        total = total + buf["dw_recv"][half, direction, n - 1].astype(F32)
                buf["dw_fin"][...] = total

    def share_outs():
        recv(buf["outs"].at[: 2 * HD, : (NY - 1) * HD], id_outs)
        for dy in range(1, NY):
            ref = out_part((y + dy) % NY, c)
            send(ref, ref, id_outs_sib, dev_sib)

    def take_outs():
        recv(buf["slices"].at[: (NY - 1) * HD, :], id_slice)
        recv(buf["outs"].at[: 2 * HD, : (NY - 1) * HD], id_outs_sib)

    id_router_x = alloc("recv")

    def router_send():
        recv(buf["router_y"].at[: NY - 1], id_router_y)
        total = buf["router_y"][0]
        for i in range(1, NY):
            total = total + buf["router_y"][i]
        buf["router_x"][x] = total
        for dx in range(1, nx):
            x_to = (x + dx) % nx
            ref = buf["router_x"].at[x]
            send(ref, ref, id_router_x, dev(z, y, x_to, c))

    def router_last():
        if nx > 1:
            recv(buf["router_x"].at[: nx - 1], id_router_x)
        total = buf["router_x"][0]
        for i in range(1, nx):
            total = total + buf["router_x"][i]
        token_row = lax.broadcasted_iota(jnp.int32, (HD, cap), 0)
        token_slot = lax.broadcasted_iota(jnp.int32, (HD, cap), 1)
        own = jnp.logical_and(token_row == own_start + token_slot, token_slot < own_count)
        spread = dot(own.astype(F32).astype(BF), pick_bf, 1, 0)
        placed = dot(total, spread, 1, 0, lax.Precision.HIGHEST)
        sig = 1.0 / (1.0 + jnp.exp(-logit_row))
        lg_ref[...] = placed[0:1, :] * sig * (1.0 - sig)

    id_kv_fin, id_dq = alloc("recv"), alloc("recv")
    side = y % 2

    def send_key_value_grads():
        for kind in range(2):
            for j in range(2):
                final = kv_last(kind, halves[j])
                if kind == 0:
                    final = final * factor
                buf["kv_fin"][kind, j] = final.astype(BF)
                y_to = 2 * c + j
                own = jnp.logical_and(y_to == y, half_y == c)
                src, dst = buf["kv_fin"].at[kind, j], kv_land.at[kind, side]
                send(src, dst, id_kv_fin, dev(z, y_to, x, half_y), own)
                keep(src, dst, id_kv_fin, own)

    def send_query_grads():
        for i in range(NY):
            buf["dq_out"][i] = (buf["dqt"][:, i * HD : (i + 1) * HD].T * factor).astype(BF)
            own = jnp.logical_and(y == i, half_y == c)
            src, dst = buf["dq_out"].at[i], dq_land.at[side, c]
            send(src, dst, id_dq, dev(z, i, x, half_y), own)
            keep(src, dst, id_dq, own)

    for d in range(lay.far, 0, -1):
        backward_pair(d)
        if d == max(lay.near, 1):
            kv_step(0)
    backward_block(z, True)
    send_query_grads()
    if lay.far > 1:
        kv_step(1)
    share_outs()
    router_send()
    take_outs()
    dw_step(0)
    for t in range(2, lay.far):
        kv_step(t)
        dw_step(t - 1)
    send_key_value_grads()
    dw_own_block()
    router_last()
    if lay.far > 1:
        dw_step(lay.far - 1)

    dw_last()
    dw_out = pltpu.make_async_copy(buf["dw_fin"], dw_land, local_sems.at[alloc("local")])
    dw_out.start()

    recv(dq_land, id_dq)
    recv(kv_land, id_kv_fin)
    dw_out.wait()
    for entry in pool + singles:
        if entry is not None:
            wait_sent(entry)


POOL = 24
RECV_SEMS = 92
SEND_SEMS = 35
VMEM_LIMIT = 60 * 1024 * 1024


def finish(dq_land, kv_land, dw_land, lg_in, dq_ref, dk_ref, dv_ref, dw_ref, lg_ref):
    for j in range(2):
        cols = slice(j * HD, (j + 1) * HD)
        dq_ref[:, cols] = (dq_land[j, 0].astype(F32) + dq_land[j, 1].astype(F32)).astype(BF)
        dk_ref[:, cols] = kv_land[0, j]
        dv_ref[:, cols] = kv_land[1, j]
    dw_ref[...] = dw_land[...]
    lg_ref[...] = lg_in[...]


def shards_fn(nz, nx):
    def run(grad, logit, index, count, weight, q, k, v):
        lay = Layout(nz, nx, grad.shape[0], index.shape[0], grad.shape[1])
        scratch = lay.scratch()
        names = list(scratch)
        any_ = pl.BlockSpec(memory_space=pl.ANY)
        smem = pl.BlockSpec(memory_space=pltpu.SMEM)
        vmem = pl.BlockSpec(memory_space=pltpu.VMEM)

        def kernel(*refs):
            fused(lay, names, *refs)

        lands = pl.pallas_call(
            kernel,
            out_shape=(
                jax.ShapeDtypeStruct((2, 2, HD, HD), BF),
                jax.ShapeDtypeStruct((2, 2, HD, HD), BF),
                jax.ShapeDtypeStruct((HD, 2 * HD), F32),
                jax.ShapeDtypeStruct((1, HD), F32),
            ),
            in_specs=[any_, vmem, smem, smem, any_, any_, any_, any_],
            out_specs=(any_, any_, any_, vmem),
            scratch_shapes=list(scratch.values())
            + [
                pltpu.SemaphoreType.DMA((SEND_SEMS,)),
                pltpu.SemaphoreType.DMA((RECV_SEMS,)),
                pltpu.SemaphoreType.DMA((3,)),
            ],
            compiler_params=pltpu.CompilerParams(
                collective_id=0, has_side_effects=True, vmem_limit_bytes=VMEM_LIMIT
            ),
            name="routed_backward",
        )(grad, logit.reshape(1, -1), index, count, weight, q, k, v)
        out = pl.pallas_call(
            finish,
            out_shape=(
                jax.ShapeDtypeStruct(q.shape, BF),
                jax.ShapeDtypeStruct(q.shape, BF),
                jax.ShapeDtypeStruct(q.shape, BF),
                jax.ShapeDtypeStruct((HD, q.shape[1]), F32),
                jax.ShapeDtypeStruct((1, HD), F32),
            ),
            in_specs=[vmem] * 4,
            out_specs=(vmem,) * 5,
            compiler_params=pltpu.CompilerParams(vmem_limit_bytes=VMEM_LIMIT),
            name="finish",
        )(*lands)
        return (*out[:4], out[4].reshape(-1))

    return run


def solution(mesh):
    nz = mesh.shape["seq"] // NY
    nx = mesh.shape["grp"] // 2
    placed = (
        P(("seq", "grp"), None),
        P(("seq", "grp")),
        P(("seq", "grp")),
        P(),
        P("grp", None),
        P("seq", "grp"),
        P("seq", "grp"),
        P("seq", "grp"),
    )
    return jax.shard_map(
        shards_fn(nz, nx),
        mesh=mesh,
        in_specs=placed,
        out_specs=(
            P("seq", "grp"),
            P("seq", "grp"),
            P("seq", "grp"),
            P("seq", "grp"),
            P(("seq", "grp")),
        ),
        check_vma=False,
    )
```

```python
import functools

import jax
import jax.numpy as jnp
from jax import lax
from jax.experimental import pallas as pl
from jax.experimental.pallas import tpu as pltpu
from jax.sharding import PartitionSpec as P

HD = 128
NY = 4
MESH = pl.DeviceIdType.MESH
BF = jnp.bfloat16
F32 = jnp.float32
NEG = -1e30
FAR_WAY = dict(kk=1, vv=0)
LOG2E = 1.4426950408889634


def dot(a, b, ca, cb, precision=None):
    return lax.dot_general(
        a, b, (((ca,), (cb,)), ((), ())), preferred_element_type=F32, precision=precision
    )


class Layout:
    def __init__(self, nz, nx, tok, cap, d):
        self.nz, self.nx, self.tok, self.cap, self.d = nz, nx, tok, cap, d
        self.dh = d // 2
        self.hz = nz // 2
        self.far = nz // 2
        self.near = nz - 1 - self.far
        self.relay = max(self.near - 1, 0)

    def needed(self, b, wrapped, d, is_far):
        if not wrapped:
            return b + d <= self.nz - 1
        if d == self.far:
            return b <= self.far - 1
        return b <= (self.far if is_far and d <= self.relay else self.near) - 1

    def scratch(self):
        nz, nx, cap, d, dh, hz = self.nz, self.nx, self.cap, self.d, self.dh, self.hz
        v = pltpu.VMEM
        steps = max(self.far, 1)
        names = dict(
            grads=v((self.tok, d), BF),
            weight=v((2, 2 * HD, dh), BF),
            picked=v((2, cap, dh + HD), BF),
            rows=v((2 * nx * cap, dh + HD), BF),
            block=v((HD, dh + HD), BF),
            slice_out=v((NY, HD, hz * HD), BF),
            slices=v((NY * HD, hz * HD), BF),
            gates=v((NY, 8, HD), F32),
            proj_part=v((2, HD, 2 * HD), F32),
            proj_in=v((HD, 2 * HD), F32),
            go_out=v((2, HD, HD), BF),
            qh=v((NY * HD, HD), BF),
            goh=v((NY * HD, HD), BF),
            kk=v((nz, 2 * HD, HD), BF),
            vv=v((nz, 2 * HD, HD), BF),
            soft=v((HD + 16, NY * HD), F32),
            soft_in=v((HD + 16, NY * HD), F32),
            lse=v((8, NY * HD), F32),
            delta=v((8, NY * HD), F32),
            outs=v((NY * HD, NY * HD), BF),
            dqt=v((HD, NY * HD), F32),
            dkp=v((nz, 2 * HD, HD), F32),
            dvp=v((nz, 2 * HD, HD), F32),
            dw_mine=v((2, HD, 2 * HD), F32),
            dw_own=v((HD, 2 * HD), F32),
            kv_send=v((2, 2, steps, 2 * HD, HD), BF),
            kv_recv=v((2, 2, steps, 2 * HD, HD), BF),
            dw_send=v((2, 2, steps, HD, 2 * HD), BF),
            dw_recv=v((2, 2, steps, HD, 2 * HD), BF),
            kv_fin=v((2, 2, HD, HD), BF),
            dq_out=v((NY, HD, HD), BF),
            dw_fin=v((HD, 2 * HD), F32),
            router_out=v((NY, 8, HD), F32),
            router_y=v((NY, 8, HD), F32),
            router_x=v((nx, 8, HD), F32),
        )
        return names


def fused(lay, names, *refs):
    (g_ref, logit_ref, idx_ref, cnt_ref, w_ref, q_ref, k_ref, v_ref) = refs[:8]
    (dq_land, kv_land, dw_land, lg_ref) = refs[8:12]
    buf = dict(zip(names, refs[12 : 12 + len(names)]))
    send_sems, recv_sems, local_sems = refs[12 + len(names) :]
    nz, nx, cap, dh, hz = lay.nz, lay.nx, lay.cap, lay.dh, lay.hz
    shards = 2 * nx
    factor = HD ** (-0.5)

    s, g = lax.axis_index("seq"), lax.axis_index("grp")
    z, y, x, c = s // NY, s % NY, g // 2, g % 2
    sib = 1 - c

    def dev(z_, y_, x_, c_):
        return (z_ * NY + y_, x_ * 2 + c_)

    up, down = (z + 1) % nz, (z + nz - 1) % nz
    dev_up, dev_down = dev(up, y, x, c), dev(down, y, x, c)
    dev_sib = dev(z, y, x, sib)
    near, far, relay = lay.near, lay.far, lay.relay
    jump = far - relay
    z_jump = ((z + nz - jump) % nz, (z + jump) % nz)
    my_rows = pl.ds(pl.multiple_of(y * HD, HD), HD)
    share = hz // nx * HD
    my_cols = pl.ds(pl.multiple_of(x * share, HD), share)

    counter = {"send": 0, "recv": 0, "local": 0}

    def alloc(kind, n=1):
        first = counter[kind]
        counter[kind] += n
        return first

    ids = {}

    def ident(*key):
        if key not in ids:
            ids[key] = alloc("recv")
        return ids[key]

    pool = [None] * POOL
    singles = []

    def wait_sent(entry):
        unless, copy = entry
        if unless is None:
            copy.wait_send()
        else:
            pl.when(jnp.logical_not(unless))(lambda: copy.wait_send())

    def send(src, dst, recv_id, to, unless=None, single=False):
        if single:
            slot = POOL + len(singles)
        else:
            slot = alloc("send") % POOL
            if pool[slot] is not None:
                wait_sent(pool[slot])
        copy = pltpu.make_async_remote_copy(
            src_ref=src,
            dst_ref=dst,
            send_sem=send_sems.at[slot],
            recv_sem=recv_sems.at[recv_id],
            device_id=to,
            device_id_type=MESH,
        )
        if single:
            singles.append((unless, copy))
        else:
            pool[slot] = (unless, copy)
        if unless is None:
            copy.start()
        else:
            pl.when(jnp.logical_not(unless))(lambda: copy.start())

    def keep(src, dst, recv_id, own):
        copy = pltpu.make_async_copy(src, dst, recv_sems.at[recv_id])
        pl.when(own)(lambda: copy.start())

    def recv(dst, recv_id, unless=None):
        copy = pltpu.make_async_remote_copy(
            src_ref=dst,
            dst_ref=dst,
            send_sem=send_sems.at[0],
            recv_sem=recv_sems.at[recv_id],
            device_id=dev_sib,
            device_id_type=MESH,
        )
        if unless is None:
            copy.wait_recv()
        else:
            pl.when(jnp.logical_not(unless))(lambda: copy.wait_recv())

    grads_in = pltpu.make_async_copy(g_ref, buf["grads"], local_sems.at[alloc("local")])
    grads_in.start()
    own_half = pl.multiple_of(c * dh, HD)
    other_half = pl.multiple_of(sib * dh, HD)
    weight_in = pltpu.make_async_copy(
        w_ref.at[:, pl.ds(own_half, dh)], buf["weight"].at[c], local_sems.at[alloc("local")]
    )
    weight_in.start()

    partners = [dev_sib, dev_up, dev_down]
    partners += [dev(up, y, x, sib), dev(down, y, x, sib)]
    partners += [dev(z_jump[0], y, x, c), dev(z_jump[1], y, x, c)]
    for dy in range(1, NY):
        for cc in range(2):
            partners.append(dev(z, (y + dy) % NY, x, cc))
    for dx in range(1, nx):
        for cc in range(2):
            partners.append(dev(z, y, (x + dx) % nx, cc))
    barrier = pltpu.get_barrier_semaphore()
    for partner in partners:
        pl.semaphore_signal(barrier, inc=1, device_id=partner, device_id_type=MESH)
    pl.semaphore_wait(barrier, len(partners))

    half_y = y // 2
    id_k, id_v, id_q = alloc("recv"), alloc("recv"), alloc("recv")
    for src, name, base in ((k_ref, "kk", id_k), (v_ref, "vv", id_v)):
        for j in range(2):
            y_to = 2 * c + j
            own = jnp.logical_and(y_to == y, half_y == c)
            part = pl.ds(pl.multiple_of((y % 2) * HD, HD), HD)
            mine, dst = src.at[:, j * HD : (j + 1) * HD], buf[name].at[z, part, :]
            send(mine, dst, base, dev(z, y_to, x, half_y), own)
            keep(mine, dst, base, own)
    id_w = alloc("recv")
    send(w_ref.at[:, pl.ds(other_half, dh)], buf["weight"].at[c], id_w, dev_sib, single=True)

    slot = lax.broadcasted_iota(jnp.int32, (cap, HD), 0)
    lane = lax.broadcasted_iota(jnp.int32, (cap, HD), 1)
    index = jnp.zeros((cap, HD), jnp.int32)
    for j in range(cap):
        index = jnp.where(slot == j, idx_ref[j], index)
    first = s * shards
    starts, total = [], jnp.int32(0)
    counts = []
    for i in range(shards):
        starts.append(total)
        counts.append(cnt_ref[first + i])
        total = total + counts[-1]
    own_start, own_count = jnp.int32(0), jnp.int32(0)
    for i in range(shards):
        own_start = jnp.where(g == i, starts[i], own_start)
        own_count = jnp.where(g == i, counts[i], own_count)
    pick = jnp.logical_and(index == lane, slot < own_count)
    pick_bf = pick.astype(F32).astype(BF)
    logit_row = logit_ref[...]
    chosen_logit = jnp.sum(
        jnp.where(pick, jnp.broadcast_to(logit_row, (cap, HD)), 0.0), axis=1, keepdims=True
    )
    gate_col = 1.0 / (1.0 + jnp.exp(-chosen_logit))
    gate_tile = jnp.broadcast_to(gate_col, (cap, HD)).astype(BF)
    grads_in.wait()
    for h in range(2):
        buf["picked"][h, :, pl.ds(dh, HD)] = gate_tile
    for h in range(2):
        buf["picked"][h, :, pl.ds(0, dh)] = dot(
            pick_bf, buf["grads"][:, h * dh : (h + 1) * dh], 1, 0
        ).astype(BF)

    right, left = (x + 1) % nx, (x + nx - 1) % nx
    rows = buf["rows"]

    def row_slot(shard):
        return rows.at[pl.ds(pl.multiple_of(shard * cap, cap), cap), :]

    id_rows_sib = alloc("recv")
    id_step_one = alloc("recv", 4)
    id_from_left, id_from_right = id_step_one, id_step_one + 2
    id_far = alloc("recv")
    send(buf["picked"].at[sib], row_slot(g), id_rows_sib, dev_sib, single=True)
    if nx > 1:
        for to, side in ((jnp.where(c == 0, right, left), c), (jnp.where(c == 0, left, right), sib)):
            for h in range(2):
                dst, recv_id = row_slot(g), id_step_one + 2 * side + c
                send(buf["picked"].at[h], dst, recv_id, dev(z, y, to, h), single=True)
    for j in range(2):
        y_to = 2 * c + j
        for cc in range(2):
            own = jnp.logical_and(y_to == y, c == cc)
            mine, dst = q_ref.at[:, j * HD : (j + 1) * HD], buf["qh"].at[my_rows, :]
            send(mine, dst, id_q, dev(z, y_to, x, cc), own)
            keep(mine, dst, id_q, own)
    rows[pl.ds(pl.multiple_of(g * cap, cap), cap), :] = buf["picked"][c]

    buf["dkp"][...] = jnp.zeros_like(buf["dkp"])
    buf["dvp"][...] = jnp.zeros_like(buf["dvp"])
    buf["dqt"][...] = jnp.zeros_like(buf["dqt"])
    soft = buf["soft"]
    soft[...] = jnp.zeros_like(soft)
    soft[HD : HD + 8, :] = jnp.full((8, NY * HD), NEG, F32)

    halves = (slice(0, HD), slice(HD, 2 * HD))
    ring = [(name, half, FAR_WAY[name]) for name in ("kk", "vv") for half in range(2)]
    dev_next = (dev_down, dev_up)

    needed = lay.needed

    def source(direction, d):
        return (z + d) % nz if direction == 0 else (z + nz - d) % nz

    def ring_step(t):
        for name, half, far_way in ring:
            if t == 0 and half == 0:
                recv(buf[name].at[z], id_k if name == "kk" else id_v)
            for direction in (1, 0):
                b = source(direction, t)
                ref = buf[name].at[b, halves[half], :]
                is_far = direction == far_way

                def useless(d):
                    return jnp.logical_not(needed(b, direction == 0, d, is_far))

                if 1 <= t <= near:
                    recv(ref, ident(name, half, direction, t), useless(t))
                if t + 1 <= near:
                    key = ident(name, half, direction, t + 1)
                    send(ref, ref, key, dev_next[direction], useless(t + 1))
                if t == relay and is_far:
                    to = dev(z_jump[direction], y, x, c)
                    send(ref, ref, ident(name, half, direction, far), to, useless(far))

    def ring_far():
        for name, half, far_way in ring:
            b = source(far_way, far)
            ref = buf[name].at[b, halves[half], :]
            useless = jnp.logical_not(needed(b, far_way == 0, far, True))
            recv(ref, ident(name, half, far_way, far), useless)

    ring_step(0)

    def allowed():
        key = c * 2 * HD + lax.broadcasted_iota(jnp.int32, (2 * HD, NY * HD), 0)
        query = lax.broadcasted_iota(jnp.int32, (2 * HD, NY * HD), 1)
        return key <= query

    factor2 = factor * LOG2E

    def forward_block(b, diagonal):
        keys, values = buf["kk"][b], buf["vv"][b]
        scores = dot(keys, buf["qh"][...], 1, 1) * factor2
        if diagonal:
            scores = jnp.where(allowed(), scores, NEG)
        old = soft[HD : HD + 1, :]
        new = jnp.maximum(old, jnp.max(scores, axis=0, keepdims=True))
        weights = jnp.exp2(scores - new)
        decay = jnp.exp2(old - new)
        norm = soft[HD + 8 : HD + 9, :] * decay + jnp.sum(weights, axis=0, keepdims=True)
        soft[0:HD, :] = soft[0:HD, :] * decay + dot(values, weights.astype(BF), 0, 0)
        soft[HD : HD + 1, :] = new
        soft[HD + 8 : HD + 9, :] = norm

    def forward_pair(t):
        pl.when(z >= t)(lambda: forward_block((z + nz - t) % nz, False))
        if t <= nz - 1 - t:
            pl.when(z + t >= nz)(lambda: forward_block((z + t) % nz, False))

    def rows_step_two():
        if nx == 1:
            return
        for cc in range(2):
            recv(row_slot(2 * left + cc), id_from_left + cc)
            recv(row_slot(2 * right + cc), id_from_right + cc)
        send(row_slot(2 * left), row_slot(2 * left), id_far, dev(z, y, right, c), single=True)
        ref = row_slot(2 * right + 1)
        send(ref, ref, id_far, dev(z, y, left, c), single=True)

    id_slice, id_proj, id_go = alloc("recv"), alloc("recv"), alloc("recv")
    id_gate = alloc("recv")
    row_iota = lax.broadcasted_iota(jnp.int32, (HD, shards * cap), 0)

    def project():
        recv(row_slot(2 * x + sib), id_rows_sib)
        if nx > 1:
            recv(rows.at[pl.ds(0, 2 * cap), :], id_far)
        lanes = lax.broadcasted_iota(jnp.int32, (1, shards * cap), 1)
        place = jnp.full((1, shards * cap), -1, jnp.int32)
        for i in range(shards):
            within = lanes - i * cap
            live = jnp.logical_and(within >= 0, within < counts[i])
            place = jnp.where(live, starts[i] + within, place)
        compact = (row_iota == place).astype(F32).astype(BF)
        block = buf["block"]
        block[...] = dot(compact, rows[...], 1, 0).astype(BF)
        for i in range(hz):
            for yy in range(NY):
                k = i * NY + yy
                buf["slice_out"][yy, :, i * HD : (i + 1) * HD] = block[:, k * HD : (k + 1) * HD]
        gate_rows = block[:, dh:].astype(F32).T
        buf["gates"][y] = gate_rows[0:8, :]
        for dy in range(1, NY):
            y_to = (y + dy) % NY
            send(buf["gates"].at[y], buf["gates"].at[y], id_gate, dev(z, y_to, x, c))
        weight_in.wait()
        recv(buf["weight"].at[sib], id_w)
        part = buf["proj_part"]
        part[sib] = dot(block[:, :dh], buf["weight"][sib], 1, 1)
        send(part.at[sib], buf["proj_in"], id_proj, dev_sib)
        part[c] = dot(block[:, :dh], buf["weight"][c], 1, 1)

    def out_gradient():
        recv(buf["proj_in"], id_proj)
        total = buf["proj_part"][c] + buf["proj_in"][...]
        gate = buf["block"][:, dh:].astype(F32)
        for j in range(2):
            buf["go_out"][j] = (gate * total[:, j * HD : (j + 1) * HD]).astype(BF)
        for j in range(2):
            y_to = 2 * c + j
            for cc in range(2):
                own = jnp.logical_and(y_to == y, c == cc)
                send(buf["go_out"].at[j], buf["goh"].at[my_rows, :], id_go, dev(z, y_to, x, cc), own)
                keep(buf["go_out"].at[j], buf["goh"].at[my_rows, :], id_go, own)

        for dy in range(1, NY):
            y_to = (y + dy) % NY
            src, dst = buf["slice_out"].at[y_to, :, my_cols], buf["slices"].at[my_rows, my_cols]
            send(src, dst, id_slice, dev(z, y_to, x, c), single=True)
        buf["slices"][my_rows, my_cols] = buf["slice_out"][y, :, my_cols]

    rows_step_two()
    for t in range(1, far + 1):
        if t <= near:
            ring_step(t)
        else:
            ring_far()
        if t == 1:
            recv(buf["qh"], id_q)
            forward_block(z, True)
        if t == min(2, far):
            project()
            out_gradient()
        forward_pair(t)

    id_soft = alloc("recv")
    send(soft, buf["soft_in"], id_soft, dev_sib)
    recv(buf["slices"].at[: (NY - 1) * HD, :share], id_slice)
    id_slice_x = alloc("recv")
    for dx in range(1, nx):
        ref = buf["slices"].at[:, my_cols]
        send(ref, ref, id_slice_x, dev(z, y, (x + dx) % nx, c), single=True)
    recv(buf["goh"], id_go)
    recv(buf["gates"].at[pl.ds(0, NY - 1)], id_gate)
    recv(buf["soft_in"], id_soft)
    head_cols = pl.ds(pl.multiple_of(y * HD, HD), HD)
    soft_in = buf["soft_in"]
    max_a, max_b = soft[HD : HD + 1, :], soft_in[HD : HD + 1, :]
    top = jnp.maximum(max_a, max_b)
    scale_a, scale_b = jnp.exp2(max_a - top), jnp.exp2(max_b - top)
    norm = soft[HD + 8 : HD + 9, :] * scale_a + soft_in[HD + 8 : HD + 9, :] * scale_b
    buf["lse"][0:1, :] = top + jnp.log2(norm)
    scale_a, scale_b = scale_a / norm, scale_b / norm
    for i in range(NY):
        span = slice(i * HD, (i + 1) * HD)
        out_t = soft[0:HD, span] * scale_a[:, span] + soft_in[0:HD, span] * scale_b[:, span]
        out_t = out_t.astype(BF).astype(F32)
        gate_row = buf["gates"][i, 0:1, :]
        buf["outs"][span, head_cols] = (gate_row * out_t).T.astype(BF)
        delta = jnp.sum(out_t * buf["goh"][span, :].astype(F32).T, axis=0, keepdims=True)
        buf["delta"][0:1, span] = delta
        buf["router_out"][i] = jnp.broadcast_to(delta / gate_row, (8, HD))

    id_outs, id_outs_sib, id_router_y = alloc("recv"), alloc("recv"), alloc("recv")

    def out_part(head, core):
        return buf["outs"].at[
            pl.ds(pl.multiple_of(core * 2 * HD, HD), 2 * HD),
            pl.ds(pl.multiple_of(head * HD, HD), HD),
        ]

    for dy in range(1, NY):
        y_to = (y + dy) % NY
        to = dev(z, y_to, x, c)
        send(out_part(y, c), out_part(y, c), id_outs, to)
        send(buf["router_out"].at[y_to], buf["router_y"].at[y], id_router_y, to)
    buf["router_y"][y] = buf["router_out"][y]

    def backward_block(b, diagonal):
        keys, values = buf["kk"][b], buf["vv"][b]
        queries, go = buf["qh"][...], buf["goh"][...]
        scores = dot(keys, queries, 1, 1) * factor2
        weights = jnp.exp2(scores - buf["lse"][0:1, :])
        if diagonal:
            weights = jnp.where(allowed(), weights, 0.0)
        grad_weights = dot(values, go, 1, 1)
        grad_scores = (weights * (grad_weights - buf["delta"][0:1, :])).astype(BF)
        buf["dvp"][b] = dot(weights.astype(BF), go, 1, 0)
        buf["dkp"][b] = dot(grad_scores, queries, 1, 0)
        buf["dqt"][...] += dot(keys, grad_scores, 0, 0)

    def backward_pair(t):
        pl.when(z >= t)(lambda: backward_block((z + nz - t) % nz, False))
        if t <= nz - 1 - t:
            pl.when(z + t >= nz)(lambda: backward_block((z + t) % nz, False))

    def target(direction, d):
        return (z + nz - d) % nz if direction == 0 else (z + d) % nz

    id_kv_fin, id_dq = alloc("recv"), alloc("recv")
    side = y % 2

    def kv_part(kind, b, part):
        return (buf["dkp"] if kind == 0 else buf["dvp"]).at[b, part, :]

    def kv_useless(b, kind, direction, d):
        return jnp.logical_not(needed(b, direction == 1, d, direction == kind))

    def kv_far():
        for kind in range(2):
            b = target(kind, far)
            useless = kv_useless(b, kind, kind, far)
            for part in halves:
                out = buf["kv_send"].at[kind, kind, near, part, :]
                out[...] = kv_part(kind, b, part)[...].astype(BF)
                key = ident("chain", kind, kind, part.start, near)
                to = dev(z_jump[kind], y, x, c)
                send(out, buf["kv_recv"].at[kind, kind, near, part, :], key, to, useless)

    def kv_taken(total, kind, direction, t, part, useless):
        ref = buf["kv_recv"].at[kind, direction, t, part, :]
        recv(ref, ident("chain", kind, direction, part.start, t), useless)

        @pl.when(jnp.logical_not(useless))
        def _():
            total[...] += ref[...].astype(F32)

    def kv_step(t):
        d = near - t
        for kind in range(2):
            for part in halves:
                for direction in range(2):
                    b = target(direction, d)
                    total = kv_part(kind, b, part)
                    if t > 0:
                        useless = kv_useless(b, kind, direction, d + 1)
                        kv_taken(total, kind, direction, t - 1, part, useless)
                    if d == relay and direction == kind:
                        useless = kv_useless(b, kind, direction, far)
                        kv_taken(total, kind, direction, near, part, useless)
                    out = buf["kv_send"].at[kind, direction, t, part, :]
                    useless = kv_useless(b, kind, direction, d)

                    @pl.when(jnp.logical_not(useless))
                    def _():
                        out[...] = total[...].astype(BF)

                    if d > 1:
                        key = ident("chain", kind, direction, part.start, t)
                        dst = buf["kv_recv"].at[kind, direction, t, part, :]
                        send(out, dst, key, dev_next[direction], useless)
                    else:
                        to = dev(down if direction == 0 else up, 2 * c + part.start // HD, x, half_y)
                        dst = kv_land.at[direction, kind, side]
                        send(out, dst, ident("land", direction, kind), to, useless)

    def dw_part(b, half):
        rows_of = buf["slices"][:, pl.ds(pl.multiple_of((b % hz) * HD, HD), HD)]
        return dot(rows_of, buf["outs"][:, half * 2 * HD : (half + 1) * 2 * HD], 0, 0)

    def dw_send(half, direction, d, t, takes, to):
        b = target(direction, d)
        skip = b // hz != c
        out, inc = buf["dw_send"].at[half, direction, t], buf["dw_recv"]
        for u in takes:
            recv(inc.at[half, direction, u], ident("dw", half, direction, u), skip)

        @pl.when(jnp.logical_not(skip))
        def _():
            total = dw_part(b, half)
            for u in takes:
                total = total + inc[half, direction, u].astype(F32)
            out[...] = total.astype(BF)

        send(out, inc.at[half, direction, t], ident("dw", half, direction, t), to, skip)

    def dw_far():
        for half in range(2):
            to = dev(z_jump[half], y, x, half if relay == 0 else c)
            dw_send(half, half, far, near, [], to)

    def dw_step(t):
        for half in range(2):
            for direction in range(2):
                d = near - t
                takes = [t - 1] if t > 0 else []
                if d == relay and direction == half:
                    takes.append(near)
                to = dev_next[direction]
                if d == 1:
                    to = dev(down if direction == 0 else up, y, x, half)
                dw_send(half, direction, d, t, takes, to)

    id_dw_own = alloc("recv")
    not_holder = z // hz != c
    holder = jnp.logical_not(not_holder)

    def dw_own_block():
        @pl.when(holder)
        def _():
            for half in range(2):
                buf["dw_mine"][half] = dw_part(z, half)
            buf["dw_own"][...] = buf["dw_mine"][c]

        send(buf["dw_mine"].at[sib], buf["dw_own"], id_dw_own, dev_sib, not_holder)

    def dw_last():
        recv(buf["dw_own"], id_dw_own, holder)
        for half in range(2):

            @pl.when(c == half)
            def _():
                total = buf["dw_own"][...]
                takes = [(direction, near - 1) for direction in range(2) if near > 0]
                if relay == 0:
                    takes.append((half, near))
                for direction, t in takes:
                    ref = buf["dw_recv"].at[half, direction, t]
                    recv(ref, ident("dw", half, direction, t))
                    total = total + ref[...].astype(F32)
                buf["dw_fin"][...] = total

    def share_outs():
        recv(buf["outs"].at[: 2 * HD, : (NY - 1) * HD], id_outs)
        for dy in range(1, NY):
            ref = out_part((y + dy) % NY, c)
            send(ref, ref, id_outs_sib, dev_sib)

    def take_outs():
        if nx > 1:
            recv(buf["slices"].at[:, : (nx - 1) * share], id_slice_x)
        recv(buf["outs"].at[: 2 * HD, : (NY - 1) * HD], id_outs_sib)

    id_router_x = alloc("recv")

    def router_send():
        recv(buf["router_y"].at[: NY - 1], id_router_y)
        total = buf["router_y"][0]
        for i in range(1, NY):
            total = total + buf["router_y"][i]
        buf["router_x"][x] = total
        for dx in range(1, nx):
            x_to = (x + dx) % nx
            ref = buf["router_x"].at[x]
            send(ref, ref, id_router_x, dev(z, y, x_to, c))

    def router_last():
        if nx > 1:
            recv(buf["router_x"].at[: nx - 1], id_router_x)
        total = buf["router_x"][0]
        for i in range(1, nx):
            total = total + buf["router_x"][i]
        token_row = lax.broadcasted_iota(jnp.int32, (HD, cap), 0)
        token_slot = lax.broadcasted_iota(jnp.int32, (HD, cap), 1)
        own = jnp.logical_and(token_row == own_start + token_slot, token_slot < own_count)
        spread = dot(own.astype(F32).astype(BF), pick_bf, 1, 0)
        placed = dot(total, spread, 1, 0, lax.Precision.HIGHEST)
        sig = 1.0 / (1.0 + jnp.exp(-logit_row))
        lg_ref[...] = placed[0:1, :] * sig * (1.0 - sig)


    def send_own_part():
        for kind in range(2):
            for j in range(2):
                buf["kv_fin"][kind, j] = kv_part(kind, z, halves[j])[...].astype(BF)
                y_to = 2 * c + j
                own = jnp.logical_and(y_to == y, half_y == c)
                src, dst = buf["kv_fin"].at[kind, j], kv_land.at[2, kind, side]
                send(src, dst, id_kv_fin, dev(z, y_to, x, half_y), own)
                keep(src, dst, id_kv_fin, own)

    def send_query_grads():
        for i in range(NY):
            buf["dq_out"][i] = (buf["dqt"][:, i * HD : (i + 1) * HD].T * factor).astype(BF)
            own = jnp.logical_and(y == i, half_y == c)
            src, dst = buf["dq_out"].at[i], dq_land.at[side, c]
            send(src, dst, id_dq, dev(z, i, x, half_y), own)
            keep(src, dst, id_dq, own)

    for d in range(far, 0, -1):
        backward_pair(d)
        if d == far:
            kv_far()
        if d == near:
            kv_step(0)
    backward_block(z, True)
    send_query_grads()
    send_own_part()
    share_outs()
    if near > 1:
        kv_step(1)
    router_send()
    take_outs()
    dw_far()
    if near > 0:
        dw_step(0)
    for t in range(2, near):
        kv_step(t)
        dw_step(t - 1)
    dw_own_block()
    router_last()
    if near > 1:
        dw_step(near - 1)
    dw_last()
    dw_out = pltpu.make_async_copy(buf["dw_fin"], dw_land, local_sems.at[alloc("local")])
    dw_out.start()

    recv(dq_land, id_dq)
    recv(kv_land.at[2], id_kv_fin)
    for direction in range(2):
        for kind in range(2):
            useless = kv_useless(z, kind, direction, 1)
            recv(kv_land.at[direction, kind], ident("land", direction, kind), useless)
    dw_out.wait()
    for entry in pool + singles:
        if entry is not None:
            wait_sent(entry)


POOL = 24
RECV_SEMS = 89
SEND_SEMS = 38
VMEM_LIMIT = 60 * 1024 * 1024


def finish(nz, dq_land, kv_land, dw_land, lg_in, dq_ref, dk_ref, dv_ref, dw_ref, lg_ref):
    lay = Layout(nz, 1, HD, HD, HD)
    z = lax.axis_index("seq") // NY
    for j in range(2):
        cols = slice(j * HD, (j + 1) * HD)
        dq_ref[:, cols] = (dq_land[j, 0].astype(F32) + dq_land[j, 1].astype(F32)).astype(BF)
        for kind, ref, scale in ((0, dk_ref, HD ** (-0.5)), (1, dv_ref, 1.0)):
            total = kv_land[2, kind, j].astype(F32)
            for way in range(2):
                useful = lay.needed(z, way == 1, 1, way == kind)
                total = total + jnp.where(useful, kv_land[way, kind, j].astype(F32), 0.0)
            ref[:, cols] = (total * scale).astype(BF)
    dw_ref[...] = dw_land[...]
    lg_ref[...] = lg_in[...]


def shards_fn(nz, nx):
    def run(grad, logit, index, count, weight, q, k, v):
        lay = Layout(nz, nx, grad.shape[0], index.shape[0], grad.shape[1])
        scratch = lay.scratch()
        names = list(scratch)
        any_ = pl.BlockSpec(memory_space=pl.ANY)
        smem = pl.BlockSpec(memory_space=pltpu.SMEM)
        vmem = pl.BlockSpec(memory_space=pltpu.VMEM)

        def kernel(*refs):
            fused(lay, names, *refs)

        lands = pl.pallas_call(
            kernel,
            out_shape=(
                jax.ShapeDtypeStruct((2, 2, HD, HD), BF),
                jax.ShapeDtypeStruct((3, 2, 2, HD, HD), BF),
                jax.ShapeDtypeStruct((HD, 2 * HD), F32),
                jax.ShapeDtypeStruct((1, HD), F32),
            ),
            in_specs=[any_, vmem, smem, smem, any_, any_, any_, any_],
            out_specs=(any_, any_, any_, vmem),
            scratch_shapes=list(scratch.values())
            + [
                pltpu.SemaphoreType.DMA((SEND_SEMS,)),
                pltpu.SemaphoreType.DMA((RECV_SEMS,)),
                pltpu.SemaphoreType.DMA((3,)),
            ],
            compiler_params=pltpu.CompilerParams(
                collective_id=0, has_side_effects=True, vmem_limit_bytes=VMEM_LIMIT
            ),
            name="routed_backward",
        )(grad, logit.reshape(1, -1), index, count, weight, q, k, v)
        out = pl.pallas_call(
            functools.partial(finish, nz),
            out_shape=(
                jax.ShapeDtypeStruct(q.shape, BF),
                jax.ShapeDtypeStruct(q.shape, BF),
                jax.ShapeDtypeStruct(q.shape, BF),
                jax.ShapeDtypeStruct((HD, q.shape[1]), F32),
                jax.ShapeDtypeStruct((1, HD), F32),
            ),
            in_specs=[vmem] * 4,
            out_specs=(vmem,) * 5,
            compiler_params=pltpu.CompilerParams(vmem_limit_bytes=VMEM_LIMIT),
            name="finish",
        )(*lands)
        return (*out[:4], out[4].reshape(-1))

    return run


def solution(mesh):
    nz = mesh.shape["seq"] // NY
    nx = mesh.shape["grp"] // 2
    placed = (
        P(("seq", "grp"), None),
        P(("seq", "grp")),
        P(("seq", "grp")),
        P(),
        P("grp", None),
        P("seq", "grp"),
        P("seq", "grp"),
        P("seq", "grp"),
    )
    return jax.shard_map(
        shards_fn(nz, nx),
        mesh=mesh,
        in_specs=placed,
        out_specs=(
            P("seq", "grp"),
            P("seq", "grp"),
            P("seq", "grp"),
            P("seq", "grp"),
            P(("seq", "grp")),
        ),
        check_vma=False,
    )
```

```python
import functools

import jax
import jax.numpy as jnp
from jax import lax
from jax.experimental import pallas as pl
from jax.experimental.pallas import tpu as pltpu
from jax.sharding import PartitionSpec as P

HD = 128
NY = 4
MESH = pl.DeviceIdType.MESH
BF = jnp.bfloat16
F32 = jnp.float32
NEG = -1e30
FAR_WAY = dict(kk=1, vv=0)
LOG2E = 1.4426950408889634


def dot(a, b, ca, cb, precision=None):
    return lax.dot_general(
        a, b, (((ca,), (cb,)), ((), ())), preferred_element_type=F32, precision=precision
    )


class Layout:
    def __init__(self, nz, nx, tok, cap, d):
        self.nz, self.nx, self.tok, self.cap, self.d = nz, nx, tok, cap, d
        self.dh = d // 2
        self.hz = nz // 2
        self.far = nz // 2
        self.near = nz - 1 - self.far
        self.relay = max(self.near - 1, 0)

    def needed(self, b, wrapped, d, is_far):
        if not wrapped:
            return b + d <= self.nz - 1
        if d == self.far:
            return b <= self.far - 1
        return b <= (self.far if is_far and d <= self.relay else self.near) - 1

    def scratch(self):
        nz, nx, cap, d, dh, hz = self.nz, self.nx, self.cap, self.d, self.dh, self.hz
        v = pltpu.VMEM
        steps = max(self.far, 1)
        names = dict(
            grads=v((self.tok, d), BF),
            weight=v((2, 2 * HD, dh), BF),
            picked=v((2, cap, dh + HD), BF),
            rows=v((2 * nx * cap, dh + HD), BF),
            block=v((HD, dh + HD), BF),
            slice_out=v((NY, HD, hz * HD), BF),
            slices=v((NY * HD, hz * HD), BF),
            gates=v((NY, 8, HD), F32),
            proj_part=v((2, HD, 2 * HD), F32),
            proj_in=v((HD, 2 * HD), F32),
            go_out=v((2, HD, HD), BF),
            qh=v((NY * HD, HD), BF),
            goh=v((NY * HD, HD), BF),
            kk=v((nz, 2 * HD, HD), BF),
            vv=v((nz, 2 * HD, HD), BF),
            soft=v((HD + 16, NY * HD), F32),
            soft_in=v((HD + 16, NY * HD), F32),
            lse=v((8, NY * HD), F32),
            scales=v((16, NY * HD), F32),
            outs_t=v((HD, NY * HD), F32),
            delta=v((8, NY * HD), F32),
            outs=v((NY * HD, NY * HD), BF),
            dqt=v((HD, NY * HD), F32),
            dkp=v((nz, 2 * HD, HD), F32),
            dvp=v((nz, 2 * HD, HD), F32),
            dw_mine=v((2, HD, 2 * HD), F32),
            dw_own=v((HD, 2 * HD), F32),
            dw_acc=v((2, 2, HD, 2 * HD), F32),
            kv_send=v((2, 2, steps, 2 * HD, HD), BF),
            kv_recv=v((2, 2, steps, 2 * HD, HD), BF),
            dw_send=v((2, 2, steps, HD, 2 * HD), BF),
            dw_recv=v((2, 2, steps, HD, 2 * HD), BF),
            kv_fin=v((2, 2, HD, HD), BF),
            dq_out=v((NY, HD, HD), BF),
            dw_fin=v((HD, 2 * HD), F32),
            router_out=v((NY, 8, HD), F32),
            router_y=v((NY, 8, HD), F32),
            router_x=v((nx, 8, HD), F32),
        )
        return names


def fused(lay, names, *refs):
    (g_ref, logit_ref, idx_ref, cnt_ref, w_ref, q_ref, k_ref, v_ref) = refs[:8]
    (dq_land, kv_land, dw_land, lg_ref) = refs[8:12]
    buf = dict(zip(names, refs[12 : 12 + len(names)]))
    send_sems, recv_sems, local_sems = refs[12 + len(names) :]
    nz, nx, cap, dh, hz = lay.nz, lay.nx, lay.cap, lay.dh, lay.hz
    shards = 2 * nx
    factor = HD ** (-0.5)

    s, g = lax.axis_index("seq"), lax.axis_index("grp")
    z, y, x, c = s // NY, s % NY, g // 2, g % 2
    sib = 1 - c

    def dev(z_, y_, x_, c_):
        return (z_ * NY + y_, x_ * 2 + c_)

    up, down = (z + 1) % nz, (z + nz - 1) % nz
    dev_up, dev_down = dev(up, y, x, c), dev(down, y, x, c)
    dev_sib = dev(z, y, x, sib)
    near, far, relay = lay.near, lay.far, lay.relay
    jump = far - relay
    z_jump = ((z + nz - jump) % nz, (z + jump) % nz)
    my_rows = pl.ds(pl.multiple_of(y * HD, HD), HD)
    share = hz // nx * HD
    my_cols = pl.ds(pl.multiple_of(x * share, HD), share)

    counter = {"send": 0, "recv": 0, "local": 0}

    def alloc(kind, n=1):
        first = counter[kind]
        counter[kind] += n
        return first

    ids = {}

    def ident(*key):
        if key not in ids:
            ids[key] = alloc("recv")
        return ids[key]

    pool = [None] * POOL
    singles = []

    def wait_sent(entry):
        unless, copy = entry
        if unless is None:
            copy.wait_send()
        else:
            pl.when(jnp.logical_not(unless))(lambda: copy.wait_send())

    def send(src, dst, recv_id, to, unless=None, single=False):
        if single:
            slot = POOL + len(singles)
        else:
            slot = alloc("send") % POOL
            if pool[slot] is not None:
                wait_sent(pool[slot])
        copy = pltpu.make_async_remote_copy(
            src_ref=src,
            dst_ref=dst,
            send_sem=send_sems.at[slot],
            recv_sem=recv_sems.at[recv_id],
            device_id=to,
            device_id_type=MESH,
        )
        if single:
            singles.append((unless, copy))
        else:
            pool[slot] = (unless, copy)
        if unless is None:
            copy.start()
        else:
            pl.when(jnp.logical_not(unless))(lambda: copy.start())

    def keep(src, dst, recv_id, own):
        copy = pltpu.make_async_copy(src, dst, recv_sems.at[recv_id])
        pl.when(own)(lambda: copy.start())

    def recv(dst, recv_id, unless=None):
        copy = pltpu.make_async_remote_copy(
            src_ref=dst,
            dst_ref=dst,
            send_sem=send_sems.at[0],
            recv_sem=recv_sems.at[recv_id],
            device_id=dev_sib,
            device_id_type=MESH,
        )
        if unless is None:
            copy.wait_recv()
        else:
            pl.when(jnp.logical_not(unless))(lambda: copy.wait_recv())

    grads_in = pltpu.make_async_copy(g_ref, buf["grads"], local_sems.at[alloc("local")])
    grads_in.start()
    own_half = pl.multiple_of(c * dh, HD)
    other_half = pl.multiple_of(sib * dh, HD)
    weight_in = pltpu.make_async_copy(
        w_ref.at[:, pl.ds(own_half, dh)], buf["weight"].at[c], local_sems.at[alloc("local")]
    )
    weight_in.start()

    partners = [dev_sib, dev_up, dev_down]
    partners += [dev(up, y, x, sib), dev(down, y, x, sib)]
    partners += [dev(zz, y, x, cc) for zz in z_jump for cc in range(2)]
    for dy in range(1, NY):
        for cc in range(2):
            partners.append(dev(z, (y + dy) % NY, x, cc))
    for dx in range(1, nx):
        for cc in range(2):
            partners.append(dev(z, y, (x + dx) % nx, cc))
    barrier = pltpu.get_barrier_semaphore()
    for partner in partners:
        pl.semaphore_signal(barrier, inc=1, device_id=partner, device_id_type=MESH)
    pl.semaphore_wait(barrier, len(partners))

    half_y = y // 2
    id_k, id_v, id_q = alloc("recv"), alloc("recv"), alloc("recv")
    for src, name, base in ((k_ref, "kk", id_k), (v_ref, "vv", id_v)):
        for j in range(2):
            y_to = 2 * c + j
            own = jnp.logical_and(y_to == y, half_y == c)
            part = pl.ds(pl.multiple_of((y % 2) * HD, HD), HD)
            mine, dst = src.at[:, j * HD : (j + 1) * HD], buf[name].at[z, part, :]
            send(mine, dst, base, dev(z, y_to, x, half_y), own)
            keep(mine, dst, base, own)
    id_w = alloc("recv")
    send(w_ref.at[:, pl.ds(other_half, dh)], buf["weight"].at[c], id_w, dev_sib, single=True)

    slot = lax.broadcasted_iota(jnp.int32, (cap, HD), 0)
    lane = lax.broadcasted_iota(jnp.int32, (cap, HD), 1)
    index = jnp.zeros((cap, HD), jnp.int32)
    for j in range(cap):
        index = jnp.where(slot == j, idx_ref[j], index)
    first = s * shards
    starts, total = [], jnp.int32(0)
    counts = []
    for i in range(shards):
        starts.append(total)
        counts.append(cnt_ref[first + i])
        total = total + counts[-1]
    own_start, own_count = jnp.int32(0), jnp.int32(0)
    for i in range(shards):
        own_start = jnp.where(g == i, starts[i], own_start)
        own_count = jnp.where(g == i, counts[i], own_count)
    pick = jnp.logical_and(index == lane, slot < own_count)
    pick_bf = pick.astype(F32).astype(BF)
    logit_row = logit_ref[...]
    chosen_logit = jnp.sum(
        jnp.where(pick, jnp.broadcast_to(logit_row, (cap, HD)), 0.0), axis=1, keepdims=True
    )
    gate_col = 1.0 / (1.0 + jnp.exp(-chosen_logit))
    gate_tile = jnp.broadcast_to(gate_col, (cap, HD)).astype(BF)
    grads_in.wait()
    for h in range(2):
        buf["picked"][h, :, pl.ds(dh, HD)] = gate_tile
    for h in range(2):
        buf["picked"][h, :, pl.ds(0, dh)] = dot(
            pick_bf, buf["grads"][:, h * dh : (h + 1) * dh], 1, 0
        ).astype(BF)

    right, left = (x + 1) % nx, (x + nx - 1) % nx
    rows = buf["rows"]

    def row_slot(shard):
        return rows.at[pl.ds(pl.multiple_of(shard * cap, cap), cap), :]

    id_rows_sib = alloc("recv")
    id_step_one = alloc("recv", 4)
    id_from_left, id_from_right = id_step_one, id_step_one + 2
    id_far = alloc("recv")
    send(buf["picked"].at[sib], row_slot(g), id_rows_sib, dev_sib, single=True)
    if nx > 1:
        for to, side in ((jnp.where(c == 0, right, left), c), (jnp.where(c == 0, left, right), sib)):
            for h in range(2):
                dst, recv_id = row_slot(g), id_step_one + 2 * side + c
                send(buf["picked"].at[h], dst, recv_id, dev(z, y, to, h), single=True)
    for j in range(2):
        y_to = 2 * c + j
        for cc in range(2):
            own = jnp.logical_and(y_to == y, c == cc)
            mine, dst = q_ref.at[:, j * HD : (j + 1) * HD], buf["qh"].at[my_rows, :]
            send(mine, dst, id_q, dev(z, y_to, x, cc), own)
            keep(mine, dst, id_q, own)
    rows[pl.ds(pl.multiple_of(g * cap, cap), cap), :] = buf["picked"][c]

    buf["dkp"][...] = jnp.zeros_like(buf["dkp"])
    buf["dvp"][...] = jnp.zeros_like(buf["dvp"])
    buf["dqt"][...] = jnp.zeros_like(buf["dqt"])
    soft = buf["soft"]
    soft[...] = jnp.zeros_like(soft)
    soft[HD : HD + 8, :] = jnp.full((8, NY * HD), NEG, F32)

    halves = (slice(0, HD), slice(HD, 2 * HD))
    ring = [(name, half, FAR_WAY[name]) for name in ("kk", "vv") for half in range(2)]
    dev_next = (dev_down, dev_up)

    needed = lay.needed

    def source(direction, d):
        return (z + d) % nz if direction == 0 else (z + nz - d) % nz

    def ring_step(t):
        for name, half, far_way in ring:
            if t == 0 and half == 0:
                recv(buf[name].at[z], id_k if name == "kk" else id_v)
            for direction in (1, 0):
                b = source(direction, t)
                ref = buf[name].at[b, halves[half], :]
                is_far = direction == far_way

                def useless(d):
                    return jnp.logical_not(needed(b, direction == 0, d, is_far))

                if 1 <= t <= near:
                    recv(ref, ident(name, half, direction, t), useless(t))
                if t + 1 <= near:
                    key = ident(name, half, direction, t + 1)
                    send(ref, ref, key, dev_next[direction], useless(t + 1))
                if t == relay and is_far:
                    to = dev(z_jump[direction], y, x, c)
                    send(ref, ref, ident(name, half, direction, far), to, useless(far))

    def ring_far():
        for name, half, far_way in ring:
            b = source(far_way, far)
            ref = buf[name].at[b, halves[half], :]
            useless = jnp.logical_not(needed(b, far_way == 0, far, True))
            recv(ref, ident(name, half, far_way, far), useless)

    ring_step(0)

    def allowed():
        key = c * 2 * HD + lax.broadcasted_iota(jnp.int32, (2 * HD, NY * HD), 0)
        query = lax.broadcasted_iota(jnp.int32, (2 * HD, NY * HD), 1)
        return key <= query

    factor2 = factor * LOG2E

    def forward_block(b, diagonal):
        keys, values = buf["kk"][b], buf["vv"][b]
        scores = dot(keys, buf["qh"][...], 1, 1) * factor2
        if diagonal:
            scores = jnp.where(allowed(), scores, NEG)
        old = soft[HD : HD + 1, :]
        new = jnp.maximum(old, jnp.max(scores, axis=0, keepdims=True))
        weights = jnp.exp2(scores - new)
        decay = jnp.exp2(old - new)
        norm = soft[HD + 8 : HD + 9, :] * decay + jnp.sum(weights, axis=0, keepdims=True)
        soft[0:HD, :] = soft[0:HD, :] * decay + dot(values, weights.astype(BF), 0, 0)
        soft[HD : HD + 1, :] = new
        soft[HD + 8 : HD + 9, :] = norm

    def forward_pair(t):
        pl.when(z >= t)(lambda: forward_block((z + nz - t) % nz, False))
        if t <= nz - 1 - t:
            pl.when(z + t >= nz)(lambda: forward_block((z + t) % nz, False))

    def rows_step_two():
        if nx == 1:
            return
        for cc in range(2):
            recv(row_slot(2 * left + cc), id_from_left + cc)
            recv(row_slot(2 * right + cc), id_from_right + cc)
        send(row_slot(2 * left), row_slot(2 * left), id_far, dev(z, y, right, c), single=True)
        ref = row_slot(2 * right + 1)
        send(ref, ref, id_far, dev(z, y, left, c), single=True)

    id_slice, id_proj, id_go = alloc("recv"), alloc("recv"), alloc("recv")
    id_gate = alloc("recv")
    row_iota = lax.broadcasted_iota(jnp.int32, (HD, shards * cap), 0)

    def project():
        recv(row_slot(2 * x + sib), id_rows_sib)
        if nx > 1:
            recv(rows.at[pl.ds(0, 2 * cap), :], id_far)
        lanes = lax.broadcasted_iota(jnp.int32, (1, shards * cap), 1)
        place = jnp.full((1, shards * cap), -1, jnp.int32)
        for i in range(shards):
            within = lanes - i * cap
            live = jnp.logical_and(within >= 0, within < counts[i])
            place = jnp.where(live, starts[i] + within, place)
        compact = (row_iota == place).astype(F32).astype(BF)
        block = buf["block"]
        block[...] = dot(compact, rows[...], 1, 0).astype(BF)
        for i in range(hz):
            for yy in range(NY):
                k = i * NY + yy
                buf["slice_out"][yy, :, i * HD : (i + 1) * HD] = block[:, k * HD : (k + 1) * HD]
        gate_rows = block[:, dh:].astype(F32).T
        buf["gates"][y] = gate_rows[0:8, :]
        for dy in range(1, NY):
            y_to = (y + dy) % NY
            send(buf["gates"].at[y], buf["gates"].at[y], id_gate, dev(z, y_to, x, c))
        weight_in.wait()
        recv(buf["weight"].at[sib], id_w)
        part = buf["proj_part"]
        part[sib] = dot(block[:, :dh], buf["weight"][sib], 1, 1)
        send(part.at[sib], buf["proj_in"], id_proj, dev_sib)
        part[c] = dot(block[:, :dh], buf["weight"][c], 1, 1)

    def out_gradient():
        recv(buf["proj_in"], id_proj)
        total = buf["proj_part"][c] + buf["proj_in"][...]
        gate = buf["block"][:, dh:].astype(F32)
        for j in range(2):
            buf["go_out"][j] = (gate * total[:, j * HD : (j + 1) * HD]).astype(BF)
        for j in range(2):
            y_to = 2 * c + j
            for cc in range(2):
                own = jnp.logical_and(y_to == y, c == cc)
                send(buf["go_out"].at[j], buf["goh"].at[my_rows, :], id_go, dev(z, y_to, x, cc), own)
                keep(buf["go_out"].at[j], buf["goh"].at[my_rows, :], id_go, own)

        for dy in range(1, NY):
            y_to = (y + dy) % NY
            src, dst = buf["slice_out"].at[y_to, :, my_cols], buf["slices"].at[my_rows, my_cols]
            send(src, dst, id_slice, dev(z, y_to, x, c), single=True)
        buf["slices"][my_rows, my_cols] = buf["slice_out"][y, :, my_cols]

    rows_step_two()
    for t in range(1, far + 1):
        if t <= near:
            ring_step(t)
        else:
            ring_far()
        if t == 1:
            recv(buf["qh"], id_q)
            forward_block(z, True)
        if t == min(2, far):
            project()
            out_gradient()
        forward_pair(t)

    id_soft = alloc("recv")
    send(soft, buf["soft_in"], id_soft, dev_sib)
    recv(buf["slices"].at[: (NY - 1) * HD, :share], id_slice)
    id_slice_x = alloc("recv")
    for dx in range(1, nx):
        ref = buf["slices"].at[:, my_cols]
        send(ref, ref, id_slice_x, dev(z, y, (x + dx) % nx, c), single=True)
    recv(buf["gates"].at[pl.ds(0, NY - 1)], id_gate)
    recv(buf["soft_in"], id_soft)
    head_cols = pl.ds(pl.multiple_of(y * HD, HD), HD)
    soft_in = buf["soft_in"]
    max_a, max_b = soft[HD : HD + 1, :], soft_in[HD : HD + 1, :]
    top = jnp.maximum(max_a, max_b)
    scale_a, scale_b = jnp.exp2(max_a - top), jnp.exp2(max_b - top)
    norm = soft[HD + 8 : HD + 9, :] * scale_a + soft_in[HD + 8 : HD + 9, :] * scale_b
    buf["lse"][0:1, :] = top + jnp.log2(norm)
    buf["scales"][0:1, :] = scale_a / norm
    buf["scales"][8:9, :] = scale_b / norm
    id_outs, id_outs_sib, id_router_y = alloc("recv"), alloc("recv"), alloc("recv")

    def out_part(head, core):
        return buf["outs"].at[
            pl.ds(pl.multiple_of(core * 2 * HD, HD), 2 * HD),
            pl.ds(pl.multiple_of(head * HD, HD), HD),
        ]

    for i in range(NY):
        piece = (2 * c + i) % NY
        span = pl.ds(pl.multiple_of(piece * HD, HD), HD)
        out_t = soft[0:HD, span] * buf["scales"][0:1, span] + soft_in[0:HD, span] * buf["scales"][8:9, span]
        out_t = out_t.astype(BF).astype(F32)
        buf["outs_t"][:, span] = out_t
        gate_row = buf["gates"][piece, 0:1, :]
        buf["outs"][span, head_cols] = (gate_row * out_t).T.astype(BF)
        if i == 1:
            for dy in range(1, NY):
                to = dev(z, (y + dy) % NY, x, c)
                send(out_part(y, c), out_part(y, c), id_outs, to)
    recv(buf["goh"], id_go)
    for i in range(NY):
        span = slice(i * HD, (i + 1) * HD)
        out_t = buf["outs_t"][:, span]
        gate_row = buf["gates"][i, 0:1, :]
        delta = jnp.sum(out_t * buf["goh"][span, :].astype(F32).T, axis=0, keepdims=True)
        buf["delta"][0:1, span] = delta
        buf["router_out"][i] = jnp.broadcast_to(delta / gate_row, (8, HD))

    for dy in range(1, NY):
        y_to = (y + dy) % NY
        to = dev(z, y_to, x, c)
        send(buf["router_out"].at[y_to], buf["router_y"].at[y], id_router_y, to)
    buf["router_y"][y] = buf["router_out"][y]

    def backward_block(b, diagonal):
        keys, values = buf["kk"][b], buf["vv"][b]
        queries, go = buf["qh"][...], buf["goh"][...]
        scores = dot(keys, queries, 1, 1) * factor2
        weights = jnp.exp2(scores - buf["lse"][0:1, :])
        if diagonal:
            weights = jnp.where(allowed(), weights, 0.0)
        grad_weights = dot(values, go, 1, 1)
        grad_scores = (weights * (grad_weights - buf["delta"][0:1, :])).astype(BF)
        buf["dvp"][b] = dot(weights.astype(BF), go, 1, 0)
        buf["dkp"][b] = dot(grad_scores, queries, 1, 0)
        buf["dqt"][...] += dot(keys, grad_scores, 0, 0)

    def backward_pair(t):
        pl.when(z >= t)(lambda: backward_block((z + nz - t) % nz, False))
        if t <= nz - 1 - t:
            pl.when(z + t >= nz)(lambda: backward_block((z + t) % nz, False))

    def target(direction, d):
        return (z + nz - d) % nz if direction == 0 else (z + d) % nz

    id_kv_fin, id_dq = alloc("recv"), alloc("recv")
    side = y % 2

    def kv_part(kind, b, part):
        return (buf["dkp"] if kind == 0 else buf["dvp"]).at[b, part, :]

    def kv_useless(b, kind, direction, d):
        return jnp.logical_not(needed(b, direction == 1, d, direction == kind))

    def kv_far():
        for kind in range(2):
            b = target(kind, far)
            useless = kv_useless(b, kind, kind, far)
            for part in halves:
                out = buf["kv_send"].at[kind, kind, near, part, :]
                out[...] = kv_part(kind, b, part)[...].astype(BF)
                key = ident("chain", kind, kind, part.start, near)
                to = dev(z_jump[kind], y, x, c)
                send(out, buf["kv_recv"].at[kind, kind, near, part, :], key, to, useless)

    def kv_taken(total, kind, direction, t, part, useless):
        ref = buf["kv_recv"].at[kind, direction, t, part, :]
        recv(ref, ident("chain", kind, direction, part.start, t), useless)

        @pl.when(jnp.logical_not(useless))
        def _():
            total[...] += ref[...].astype(F32)

    def kv_step(t):
        d = near - t
        for kind in range(2):
            for part in halves:
                for direction in range(2):
                    b = target(direction, d)
                    total = kv_part(kind, b, part)
                    if t > 0:
                        useless = kv_useless(b, kind, direction, d + 1)
                        kv_taken(total, kind, direction, t - 1, part, useless)
                    if d == relay and direction == kind:
                        useless = kv_useless(b, kind, direction, far)
                        kv_taken(total, kind, direction, near, part, useless)
                    out = buf["kv_send"].at[kind, direction, t, part, :]
                    useless = kv_useless(b, kind, direction, d)

                    @pl.when(jnp.logical_not(useless))
                    def _():
                        out[...] = total[...].astype(BF)

                    if d > 1:
                        key = ident("chain", kind, direction, part.start, t)
                        dst = buf["kv_recv"].at[kind, direction, t, part, :]
                        send(out, dst, key, dev_next[direction], useless)
                    else:
                        to = dev(down if direction == 0 else up, 2 * c + part.start // HD, x, half_y)
                        dst = kv_land.at[direction, kind, side]
                        send(out, dst, ident("land", direction, kind), to, useless)

    def dw_part(b, half):
        rows_of = buf["slices"][:, pl.ds(pl.multiple_of((b % hz) * HD, HD), HD)]
        return dot(rows_of, buf["outs"][:, half * 2 * HD : (half + 1) * 2 * HD], 0, 0)

    def dw_ways(d):
        for half in range(2):
            for direction in range(2):
                if d < far or direction == half:
                    b = target(direction, d)
                    yield half, direction, b, b // hz != c

    def dw_ready():
        for half, direction, b, skip in dw_ways(2):

            @pl.when(jnp.logical_not(skip))
            def _():
                buf["dw_acc"][half, direction] = dw_part(b, half)

    def dw_send(d):
        inc = buf["dw_recv"]
        for half, direction, b, skip in dw_ways(d):
            out = buf["dw_send"].at[half, direction, d - 1]
            takes = [u for u in (3, 4) if d == 2 and (u < far or direction == half)]
            for u in takes:
                recv(inc.at[half, direction, u - 1], ident("dw", half, direction, u), skip)

            @pl.when(jnp.logical_not(skip))
            def _():
                total = buf["dw_acc"][half, direction] if d == 2 else dw_part(b, half)
                for u in takes:
                    total = total + inc[half, direction, u - 1].astype(F32)
                out[...] = total.astype(BF)

            if d == far:
                to = dev(z_jump[direction], y, x, c)
            elif d == 3:
                to = dev_next[direction]
            else:
                to = dev(b, y, x, half)
            send(out, inc.at[half, direction, d - 1], ident("dw", half, direction, d), to, skip)

    id_dw_own = alloc("recv")
    not_holder = z // hz != c
    holder = jnp.logical_not(not_holder)

    def dw_own_block():
        @pl.when(holder)
        def _():
            for half in range(2):
                buf["dw_mine"][half] = dw_part(z, half)
            buf["dw_own"][...] = buf["dw_mine"][c]

        send(buf["dw_mine"].at[sib], buf["dw_own"], id_dw_own, dev_sib, not_holder)

    def dw_last():
        recv(buf["dw_own"], id_dw_own, holder)
        for half in range(2):

            @pl.when(c == half)
            def _():
                total = buf["dw_own"][...]
                for d in (1, 2):
                    for direction in range(2):
                        ref = buf["dw_recv"].at[half, direction, d - 1]
                        recv(ref, ident("dw", half, direction, d))
                        total = total + ref[...].astype(F32)
                buf["dw_fin"][...] = total

    def share_outs():
        recv(buf["outs"].at[: 2 * HD, : (NY - 1) * HD], id_outs)
        for dy in range(1, NY):
            ref = out_part((y + dy) % NY, c)
            send(ref, ref, id_outs_sib, dev_sib)

    def take_outs():
        if nx > 1:
            recv(buf["slices"].at[:, : (nx - 1) * share], id_slice_x)
        recv(buf["outs"].at[: 2 * HD, : (NY - 1) * HD], id_outs_sib)

    id_router_x = alloc("recv")

    def router_send():
        recv(buf["router_y"].at[: NY - 1], id_router_y)
        total = buf["router_y"][0]
        for i in range(1, NY):
            total = total + buf["router_y"][i]
        buf["router_x"][x] = total
        for dx in range(1, nx):
            x_to = (x + dx) % nx
            ref = buf["router_x"].at[x]
            send(ref, ref, id_router_x, dev(z, y, x_to, c))

    def router_last():
        if nx > 1:
            recv(buf["router_x"].at[: nx - 1], id_router_x)
        total = buf["router_x"][0]
        for i in range(1, nx):
            total = total + buf["router_x"][i]
        token_row = lax.broadcasted_iota(jnp.int32, (HD, cap), 0)
        token_slot = lax.broadcasted_iota(jnp.int32, (HD, cap), 1)
        own = jnp.logical_and(token_row == own_start + token_slot, token_slot < own_count)
        spread = dot(own.astype(F32).astype(BF), pick_bf, 1, 0)
        placed = dot(total, spread, 1, 0, lax.Precision.HIGHEST)
        sig = 1.0 / (1.0 + jnp.exp(-logit_row))
        lg_ref[...] = placed[0:1, :] * sig * (1.0 - sig)


    def send_own_part():
        for kind in range(2):
            for j in range(2):
                buf["kv_fin"][kind, j] = kv_part(kind, z, halves[j])[...].astype(BF)
                y_to = 2 * c + j
                own = jnp.logical_and(y_to == y, half_y == c)
                src, dst = buf["kv_fin"].at[kind, j], kv_land.at[2, kind, side]
                send(src, dst, id_kv_fin, dev(z, y_to, x, half_y), own)
                keep(src, dst, id_kv_fin, own)

    def send_query_grads():
        for i in range(NY):
            buf["dq_out"][i] = (buf["dqt"][:, i * HD : (i + 1) * HD].T * factor).astype(BF)
            own = jnp.logical_and(y == i, half_y == c)
            src, dst = buf["dq_out"].at[i], dq_land.at[side, c]
            send(src, dst, id_dq, dev(z, i, x, half_y), own)
            keep(src, dst, id_dq, own)

    for d in range(far, 0, -1):
        backward_pair(d)
        if d == far:
            kv_far()
        if d == near:
            kv_step(0)
    backward_block(z, True)
    send_query_grads()
    send_own_part()
    share_outs()
    if near > 1:
        kv_step(1)
    router_send()
    take_outs()
    dw_send(4)
    dw_send(3)
    dw_send(1)
    dw_ready()
    kv_step(2)
    dw_own_block()
    router_last()
    dw_send(2)
    dw_last()
    dw_out = pltpu.make_async_copy(buf["dw_fin"], dw_land, local_sems.at[alloc("local")])
    dw_out.start()

    recv(dq_land, id_dq)
    recv(kv_land.at[2], id_kv_fin)
    for direction in range(2):
        for kind in range(2):
            useless = kv_useless(z, kind, direction, 1)
            recv(kv_land.at[direction, kind], ident("land", direction, kind), useless)
    dw_out.wait()
    for entry in pool + singles:
        if entry is not None:
            wait_sent(entry)


POOL = 24
RECV_SEMS = 89
SEND_SEMS = 38
VMEM_LIMIT = 60 * 1024 * 1024


def finish(nz, dq_land, kv_land, dw_land, lg_in, dq_ref, dk_ref, dv_ref, dw_ref, lg_ref):
    lay = Layout(nz, 1, HD, HD, HD)
    z = lax.axis_index("seq") // NY
    for j in range(2):
        cols = slice(j * HD, (j + 1) * HD)
        dq_ref[:, cols] = (dq_land[j, 0].astype(F32) + dq_land[j, 1].astype(F32)).astype(BF)
        for kind, ref, scale in ((0, dk_ref, HD ** (-0.5)), (1, dv_ref, 1.0)):
            total = kv_land[2, kind, j].astype(F32)
            for way in range(2):
                useful = lay.needed(z, way == 1, 1, way == kind)
                total = total + jnp.where(useful, kv_land[way, kind, j].astype(F32), 0.0)
            ref[:, cols] = (total * scale).astype(BF)
    dw_ref[...] = dw_land[...]
    lg_ref[...] = lg_in[...]


def shards_fn(nz, nx):
    def run(grad, logit, index, count, weight, q, k, v):
        lay = Layout(nz, nx, grad.shape[0], index.shape[0], grad.shape[1])
        scratch = lay.scratch()
        names = list(scratch)
        any_ = pl.BlockSpec(memory_space=pl.ANY)
        smem = pl.BlockSpec(memory_space=pltpu.SMEM)
        vmem = pl.BlockSpec(memory_space=pltpu.VMEM)

        def kernel(*refs):
            fused(lay, names, *refs)

        lands = pl.pallas_call(
            kernel,
            out_shape=(
                jax.ShapeDtypeStruct((2, 2, HD, HD), BF),
                jax.ShapeDtypeStruct((3, 2, 2, HD, HD), BF),
                jax.ShapeDtypeStruct((HD, 2 * HD), F32),
                jax.ShapeDtypeStruct((1, HD), F32),
            ),
            in_specs=[any_, vmem, smem, smem, any_, any_, any_, any_],
            out_specs=(any_, any_, any_, vmem),
            scratch_shapes=list(scratch.values())
            + [
                pltpu.SemaphoreType.DMA((SEND_SEMS,)),
                pltpu.SemaphoreType.DMA((RECV_SEMS,)),
                pltpu.SemaphoreType.DMA((3,)),
            ],
            compiler_params=pltpu.CompilerParams(
                collective_id=0, has_side_effects=True, vmem_limit_bytes=VMEM_LIMIT
            ),
            name="routed_backward",
        )(grad, logit.reshape(1, -1), index, count, weight, q, k, v)
        out = pl.pallas_call(
            functools.partial(finish, nz),
            out_shape=(
                jax.ShapeDtypeStruct(q.shape, BF),
                jax.ShapeDtypeStruct(q.shape, BF),
                jax.ShapeDtypeStruct(q.shape, BF),
                jax.ShapeDtypeStruct((HD, q.shape[1]), F32),
                jax.ShapeDtypeStruct((1, HD), F32),
            ),
            in_specs=[vmem] * 4,
            out_specs=(vmem,) * 5,
            compiler_params=pltpu.CompilerParams(vmem_limit_bytes=VMEM_LIMIT),
            name="finish",
        )(*lands)
        return (*out[:4], out[4].reshape(-1))

    return run


def solution(mesh):
    nz = mesh.shape["seq"] // NY
    nx = mesh.shape["grp"] // 2
    placed = (
        P(("seq", "grp"), None),
        P(("seq", "grp")),
        P(("seq", "grp")),
        P(),
        P("grp", None),
        P("seq", "grp"),
        P("seq", "grp"),
        P("seq", "grp"),
    )
    return jax.shard_map(
        shards_fn(nz, nx),
        mesh=mesh,
        in_specs=placed,
        out_specs=(
            P("seq", "grp"),
            P("seq", "grp"),
            P("seq", "grp"),
            P("seq", "grp"),
            P(("seq", "grp")),
        ),
        check_vma=False,
    )
```

```python
import functools

import jax
import jax.numpy as jnp
from jax import lax
from jax.experimental import pallas as pl
from jax.experimental.pallas import tpu as pltpu
from jax.sharding import PartitionSpec as P

HD = 128
NY = 4
MESH = pl.DeviceIdType.MESH
BF = jnp.bfloat16
F32 = jnp.float32
NEG = -1e30
FAR_WAY = dict(kk=1, vv=0)
LOG2E = 1.4426950408889634


def dot(a, b, ca, cb, precision=None):
    return lax.dot_general(
        a, b, (((ca,), (cb,)), ((), ())), preferred_element_type=F32, precision=precision
    )


class Layout:
    def __init__(self, nz, nx, tok, cap, d):
        self.nz, self.nx, self.tok, self.cap, self.d = nz, nx, tok, cap, d
        self.dh = d // 2
        self.hz = nz // 2
        self.far = nz // 2
        self.near = nz - 1 - self.far
        self.relay = max(self.near - 1, 0)

    def needed(self, b, wrapped, d, is_far):
        if not wrapped:
            return b + d <= self.nz - 1
        if d == self.far:
            return b <= self.far - 1
        return b <= (self.far if is_far and d <= self.relay else self.near) - 1

    def scratch(self):
        nz, nx, cap, d, dh, hz = self.nz, self.nx, self.cap, self.d, self.dh, self.hz
        v = pltpu.VMEM
        steps = max(self.far, 1)
        names = dict(
            grads=v((self.tok, d), BF),
            weight=v((2, 2 * HD, dh), BF),
            picked=v((2, cap, dh + HD), BF),
            rows=v((2 * nx * cap, dh + HD), BF),
            block=v((HD, dh + HD), BF),
            slice_out=v((NY, HD, hz * HD), BF),
            slices=v((NY * HD, hz * HD), BF),
            gates=v((NY, 8, HD), F32),
            proj_part=v((2, HD, 2 * HD), F32),
            proj_in=v((HD, 2 * HD), F32),
            go_out=v((2, HD, HD), BF),
            qh=v((NY * HD, HD), BF),
            goh=v((NY * HD, HD), BF),
            kk=v((nz, 2 * HD, HD), BF),
            vv=v((nz, 2 * HD, HD), BF),
            soft=v((HD + 16, NY * HD), F32),
            soft_in=v((HD + 16, NY * HD), F32),
            lse=v((8, NY * HD), F32),
            scales=v((16, NY * HD), F32),
            outs_t=v((HD, NY * HD), F32),
            delta=v((8, NY * HD), F32),
            outs=v((NY * HD, NY * HD), BF),
            dqt=v((HD, NY * HD), F32),
            dkp=v((nz, 2 * HD, HD), F32),
            dvp=v((nz, 2 * HD, HD), F32),
            dw_mine=v((2, HD, 2 * HD), F32),
            dw_own=v((HD, 2 * HD), F32),
            dw_acc=v((2, 2, HD, 2 * HD), F32),
            kv_send=v((2, 2, steps, 2 * HD, HD), BF),
            kv_recv=v((2, 2, steps, 2 * HD, HD), BF),
            dw_send=v((2, 2, steps, HD, 2 * HD), BF),
            dw_recv=v((2, 2, steps, HD, 2 * HD), BF),
            kv_fin=v((2, 2, HD, HD), BF),
            dq_out=v((NY, HD, HD), BF),
            dw_fin=v((HD, 2 * HD), F32),
            router_out=v((NY, 8, HD), F32),
            router_y=v((NY, 8, HD), F32),
            router_x=v((nx, 8, HD), F32),
        )
        return names


def fused(lay, names, *refs):
    (g_ref, logit_ref, idx_ref, cnt_ref, w_ref, q_ref, k_ref, v_ref) = refs[:8]
    (dq_land, kv_land, dw_land, lg_ref) = refs[8:12]
    buf = dict(zip(names, refs[12 : 12 + len(names)]))
    send_sems, recv_sems, local_sems = refs[12 + len(names) :]
    nz, nx, cap, dh, hz = lay.nz, lay.nx, lay.cap, lay.dh, lay.hz
    shards = 2 * nx
    factor = HD ** (-0.5)

    s, g = lax.axis_index("seq"), lax.axis_index("grp")
    z, y, x, c = s // NY, s % NY, g // 2, g % 2
    sib = 1 - c

    def dev(z_, y_, x_, c_):
        return (z_ * NY + y_, x_ * 2 + c_)

    up, down = (z + 1) % nz, (z + nz - 1) % nz
    dev_up, dev_down = dev(up, y, x, c), dev(down, y, x, c)
    dev_sib = dev(z, y, x, sib)
    near, far, relay = lay.near, lay.far, lay.relay
    jump = far - relay
    z_jump = ((z + nz - jump) % nz, (z + jump) % nz)
    my_rows = pl.ds(pl.multiple_of(y * HD, HD), HD)
    share = hz // nx * HD
    my_cols = pl.ds(pl.multiple_of(x * share, HD), share)

    counter = {"send": 0, "recv": 0, "local": 0}

    def alloc(kind, n=1):
        first = counter[kind]
        counter[kind] += n
        return first

    ids = {}

    def ident(*key):
        if key not in ids:
            ids[key] = alloc("recv")
        return ids[key]

    pool = [None] * POOL
    singles = []

    def wait_sent(entry):
        unless, copy = entry
        if unless is None:
            copy.wait_send()
        else:
            pl.when(jnp.logical_not(unless))(lambda: copy.wait_send())

    def send(src, dst, recv_id, to, unless=None, single=False):
        if single:
            slot = POOL + len(singles)
        else:
            slot = alloc("send") % POOL
            if pool[slot] is not None:
                wait_sent(pool[slot])
        copy = pltpu.make_async_remote_copy(
            src_ref=src,
            dst_ref=dst,
            send_sem=send_sems.at[slot],
            recv_sem=recv_sems.at[recv_id],
            device_id=to,
            device_id_type=MESH,
        )
        if single:
            singles.append((unless, copy))
        else:
            pool[slot] = (unless, copy)
        if unless is None:
            copy.start()
        else:
            pl.when(jnp.logical_not(unless))(lambda: copy.start())

    def keep(src, dst, recv_id, own):
        copy = pltpu.make_async_copy(src, dst, recv_sems.at[recv_id])
        pl.when(own)(lambda: copy.start())

    def recv(dst, recv_id, unless=None):
        copy = pltpu.make_async_remote_copy(
            src_ref=dst,
            dst_ref=dst,
            send_sem=send_sems.at[0],
            recv_sem=recv_sems.at[recv_id],
            device_id=dev_sib,
            device_id_type=MESH,
        )
        if unless is None:
            copy.wait_recv()
        else:
            pl.when(jnp.logical_not(unless))(lambda: copy.wait_recv())

    grads_in = pltpu.make_async_copy(g_ref, buf["grads"], local_sems.at[alloc("local")])
    grads_in.start()
    own_half = pl.multiple_of(c * dh, HD)
    other_half = pl.multiple_of(sib * dh, HD)
    weight_in = pltpu.make_async_copy(
        w_ref.at[:, pl.ds(own_half, dh)], buf["weight"].at[c], local_sems.at[alloc("local")]
    )
    weight_in.start()

    partners = [dev_sib, dev_up, dev_down]
    partners += [dev(up, y, x, sib), dev(down, y, x, sib)]
    partners += [dev(zz, y, x, cc) for zz in z_jump for cc in range(2)]
    for dy in range(1, NY):
        for cc in range(2):
            partners.append(dev(z, (y + dy) % NY, x, cc))
    for dx in range(1, nx):
        for cc in range(2):
            partners.append(dev(z, y, (x + dx) % nx, cc))
    barrier = pltpu.get_barrier_semaphore()
    for partner in partners:
        pl.semaphore_signal(barrier, inc=1, device_id=partner, device_id_type=MESH)
    pl.semaphore_wait(barrier, len(partners))

    half_y = y // 2
    id_k, id_v, id_q = alloc("recv"), alloc("recv"), alloc("recv")
    for src, name, base in ((k_ref, "kk", id_k), (v_ref, "vv", id_v)):
        for j in range(2):
            y_to = 2 * c + j
            own = jnp.logical_and(y_to == y, half_y == c)
            part = pl.ds(pl.multiple_of((y % 2) * HD, HD), HD)
            mine, dst = src.at[:, j * HD : (j + 1) * HD], buf[name].at[z, part, :]
            send(mine, dst, base, dev(z, y_to, x, half_y), own)
            keep(mine, dst, base, own)
    id_w = alloc("recv")
    send(w_ref.at[:, pl.ds(other_half, dh)], buf["weight"].at[c], id_w, dev_sib, single=True)

    slot = lax.broadcasted_iota(jnp.int32, (cap, HD), 0)
    lane = lax.broadcasted_iota(jnp.int32, (cap, HD), 1)
    index = jnp.zeros((cap, HD), jnp.int32)
    for j in range(cap):
        index = jnp.where(slot == j, idx_ref[j], index)
    first = s * shards
    starts, total = [], jnp.int32(0)
    counts = []
    for i in range(shards):
        starts.append(total)
        counts.append(cnt_ref[first + i])
        total = total + counts[-1]
    own_start, own_count = jnp.int32(0), jnp.int32(0)
    for i in range(shards):
        own_start = jnp.where(g == i, starts[i], own_start)
        own_count = jnp.where(g == i, counts[i], own_count)
    pick = jnp.logical_and(index == lane, slot < own_count)
    pick_bf = pick.astype(F32).astype(BF)
    logit_row = logit_ref[...]
    chosen_logit = jnp.sum(
        jnp.where(pick, jnp.broadcast_to(logit_row, (cap, HD)), 0.0), axis=1, keepdims=True
    )
    gate_col = 1.0 / (1.0 + jnp.exp(-chosen_logit))
    gate_tile = jnp.broadcast_to(gate_col, (cap, HD)).astype(BF)
    grads_in.wait()
    for h in range(2):
        buf["picked"][h, :, pl.ds(dh, HD)] = gate_tile
    for h in range(2):
        buf["picked"][h, :, pl.ds(0, dh)] = dot(
            pick_bf, buf["grads"][:, h * dh : (h + 1) * dh], 1, 0
        ).astype(BF)

    right, left = (x + 1) % nx, (x + nx - 1) % nx
    rows = buf["rows"]

    def row_slot(shard):
        return rows.at[pl.ds(pl.multiple_of(shard * cap, cap), cap), :]

    id_rows_sib = alloc("recv")
    id_step_one = alloc("recv", 4)
    id_from_left, id_from_right = id_step_one, id_step_one + 2
    id_far = alloc("recv")
    send(buf["picked"].at[sib], row_slot(g), id_rows_sib, dev_sib, single=True)
    if nx > 1:
        for to, side in ((jnp.where(c == 0, right, left), c), (jnp.where(c == 0, left, right), sib)):
            for h in range(2):
                dst, recv_id = row_slot(g), id_step_one + 2 * side + c
                send(buf["picked"].at[h], dst, recv_id, dev(z, y, to, h), single=True)
    for j in range(2):
        y_to = 2 * c + j
        for cc in range(2):
            own = jnp.logical_and(y_to == y, c == cc)
            mine, dst = q_ref.at[:, j * HD : (j + 1) * HD], buf["qh"].at[my_rows, :]
            send(mine, dst, id_q, dev(z, y_to, x, cc), own)
            keep(mine, dst, id_q, own)
    rows[pl.ds(pl.multiple_of(g * cap, cap), cap), :] = buf["picked"][c]

    buf["dkp"][...] = jnp.zeros_like(buf["dkp"])
    buf["dvp"][...] = jnp.zeros_like(buf["dvp"])
    buf["dqt"][...] = jnp.zeros_like(buf["dqt"])
    soft = buf["soft"]
    soft[...] = jnp.zeros_like(soft)
    soft[HD : HD + 8, :] = jnp.full((8, NY * HD), NEG, F32)

    halves = (slice(0, HD), slice(HD, 2 * HD))
    ring = [(name, half, FAR_WAY[name]) for name in ("kk", "vv") for half in range(2)]
    dev_next = (dev_down, dev_up)

    needed = lay.needed

    def source(direction, d):
        return (z + d) % nz if direction == 0 else (z + nz - d) % nz

    def ring_step(t):
        for name, half, far_way in ring:
            if t == 0 and half == 0:
                recv(buf[name].at[z], id_k if name == "kk" else id_v)
            for direction in (1, 0):
                b = source(direction, t)
                ref = buf[name].at[b, halves[half], :]
                is_far = direction == far_way

                def useless(d):
                    return jnp.logical_not(needed(b, direction == 0, d, is_far))

                if 1 <= t <= near:
                    recv(ref, ident(name, half, direction, t), useless(t))
                if t + 1 <= near:
                    key = ident(name, half, direction, t + 1)
                    send(ref, ref, key, dev_next[direction], useless(t + 1))
                if t == relay and is_far:
                    to = dev(z_jump[direction], y, x, c)
                    send(ref, ref, ident(name, half, direction, far), to, useless(far))

    def ring_far():
        for name, half, far_way in ring:
            b = source(far_way, far)
            ref = buf[name].at[b, halves[half], :]
            useless = jnp.logical_not(needed(b, far_way == 0, far, True))
            recv(ref, ident(name, half, far_way, far), useless)

    ring_step(0)

    def allowed():
        key = c * 2 * HD + lax.broadcasted_iota(jnp.int32, (2 * HD, NY * HD), 0)
        query = lax.broadcasted_iota(jnp.int32, (2 * HD, NY * HD), 1)
        return key <= query

    factor2 = factor * LOG2E

    def forward_block(b, diagonal):
        keys, values = buf["kk"][b], buf["vv"][b]
        scores = dot(keys, buf["qh"][...], 1, 1) * factor2
        if diagonal:
            scores = jnp.where(allowed(), scores, NEG)
        old = soft[HD : HD + 1, :]
        new = jnp.maximum(old, jnp.max(scores, axis=0, keepdims=True))
        weights = jnp.exp2(scores - new)
        decay = jnp.exp2(old - new)
        norm = soft[HD + 8 : HD + 9, :] * decay + jnp.sum(weights, axis=0, keepdims=True)
        soft[0:HD, :] = soft[0:HD, :] * decay + dot(values, weights.astype(BF), 0, 0)
        soft[HD : HD + 1, :] = new
        soft[HD + 8 : HD + 9, :] = norm

    def forward_pair(t):
        pl.when(z >= t)(lambda: forward_block((z + nz - t) % nz, False))
        if t <= nz - 1 - t:
            pl.when(z + t >= nz)(lambda: forward_block((z + t) % nz, False))

    def rows_step_two():
        if nx == 1:
            return
        for cc in range(2):
            recv(row_slot(2 * left + cc), id_from_left + cc)
            recv(row_slot(2 * right + cc), id_from_right + cc)
        send(row_slot(2 * left), row_slot(2 * left), id_far, dev(z, y, right, c), single=True)
        ref = row_slot(2 * right + 1)
        send(ref, ref, id_far, dev(z, y, left, c), single=True)

    id_slice, id_proj, id_go = alloc("recv"), alloc("recv"), alloc("recv")
    id_gate = alloc("recv")
    row_iota = lax.broadcasted_iota(jnp.int32, (HD, shards * cap), 0)

    def project():
        recv(row_slot(2 * x + sib), id_rows_sib)
        if nx > 1:
            recv(rows.at[pl.ds(0, 2 * cap), :], id_far)
        lanes = lax.broadcasted_iota(jnp.int32, (1, shards * cap), 1)
        place = jnp.full((1, shards * cap), -1, jnp.int32)
        for i in range(shards):
            within = lanes - i * cap
            live = jnp.logical_and(within >= 0, within < counts[i])
            place = jnp.where(live, starts[i] + within, place)
        compact = (row_iota == place).astype(F32).astype(BF)
        block = buf["block"]
        block[...] = dot(compact, rows[...], 1, 0).astype(BF)
        for i in range(hz):
            for yy in range(NY):
                k = i * NY + yy
                buf["slice_out"][yy, :, i * HD : (i + 1) * HD] = block[:, k * HD : (k + 1) * HD]
        gate_rows = block[:, dh:].astype(F32).T
        buf["gates"][y] = gate_rows[0:8, :]
        for dy in range(1, NY):
            y_to = (y + dy) % NY
            send(buf["gates"].at[y], buf["gates"].at[y], id_gate, dev(z, y_to, x, c))
        weight_in.wait()
        recv(buf["weight"].at[sib], id_w)
        part = buf["proj_part"]
        part[sib] = dot(block[:, :dh], buf["weight"][sib], 1, 1)
        send(part.at[sib], buf["proj_in"], id_proj, dev_sib)
        part[c] = dot(block[:, :dh], buf["weight"][c], 1, 1)

    def out_gradient():
        recv(buf["proj_in"], id_proj)
        total = buf["proj_part"][c] + buf["proj_in"][...]
        gate = buf["block"][:, dh:].astype(F32)
        for j in range(2):
            buf["go_out"][j] = (gate * total[:, j * HD : (j + 1) * HD]).astype(BF)
        for j in range(2):
            y_to = 2 * c + j
            for cc in range(2):
                own = jnp.logical_and(y_to == y, c == cc)
                send(buf["go_out"].at[j], buf["goh"].at[my_rows, :], id_go, dev(z, y_to, x, cc), own)
                keep(buf["go_out"].at[j], buf["goh"].at[my_rows, :], id_go, own)

        for dy in range(1, NY):
            y_to = (y + dy) % NY
            src, dst = buf["slice_out"].at[y_to, :, my_cols], buf["slices"].at[my_rows, my_cols]
            send(src, dst, id_slice, dev(z, y_to, x, c), single=True)
        buf["slices"][my_rows, my_cols] = buf["slice_out"][y, :, my_cols]

    rows_step_two()
    for t in range(1, far + 1):
        if t <= near:
            ring_step(t)
        else:
            ring_far()
        if t == 1:
            recv(buf["qh"], id_q)
            forward_block(z, True)
        if t == min(2, far):
            project()
            out_gradient()
        forward_pair(t)

    id_soft = alloc("recv")
    send(soft, buf["soft_in"], id_soft, dev_sib)
    recv(buf["slices"].at[: (NY - 1) * HD, :share], id_slice)
    id_slice_x = alloc("recv")
    for dx in range(1, nx):
        ref = buf["slices"].at[:, my_cols]
        send(ref, ref, id_slice_x, dev(z, y, (x + dx) % nx, c), single=True)
    recv(buf["gates"].at[pl.ds(0, NY - 1)], id_gate)
    recv(buf["soft_in"], id_soft)
    head_cols = pl.ds(pl.multiple_of(y * HD, HD), HD)
    soft_in = buf["soft_in"]
    max_a, max_b = soft[HD : HD + 1, :], soft_in[HD : HD + 1, :]
    top = jnp.maximum(max_a, max_b)
    scale_a, scale_b = jnp.exp2(max_a - top), jnp.exp2(max_b - top)
    norm = soft[HD + 8 : HD + 9, :] * scale_a + soft_in[HD + 8 : HD + 9, :] * scale_b
    buf["lse"][0:1, :] = top + jnp.log2(norm)
    buf["scales"][0:1, :] = scale_a / norm
    buf["scales"][8:9, :] = scale_b / norm
    id_outs, id_outs_sib, id_router_y = alloc("recv"), alloc("recv"), alloc("recv")

    def out_part(head, core):
        return buf["outs"].at[
            pl.ds(pl.multiple_of(core * 2 * HD, HD), 2 * HD),
            pl.ds(pl.multiple_of(head * HD, HD), HD),
        ]

    for i in range(NY):
        piece = (2 * c + i) % NY
        span = pl.ds(pl.multiple_of(piece * HD, HD), HD)
        out_t = soft[0:HD, span] * buf["scales"][0:1, span] + soft_in[0:HD, span] * buf["scales"][8:9, span]
        out_t = out_t.astype(BF).astype(F32)
        buf["outs_t"][:, span] = out_t
        gate_row = buf["gates"][piece, 0:1, :]
        buf["outs"][span, head_cols] = (gate_row * out_t).T.astype(BF)
        if i == 1:
            for dy in range(1, NY):
                to = dev(z, (y + dy) % NY, x, c)
                send(out_part(y, c), out_part(y, c), id_outs, to)
    recv(buf["goh"], id_go)
    for i in range(NY):
        span = slice(i * HD, (i + 1) * HD)
        out_t = buf["outs_t"][:, span]
        gate_row = buf["gates"][i, 0:1, :]
        delta = jnp.sum(out_t * buf["goh"][span, :].astype(F32).T, axis=0, keepdims=True)
        buf["delta"][0:1, span] = delta
        buf["router_out"][i] = jnp.broadcast_to(delta / gate_row, (8, HD))

    for dy in range(1, NY):
        y_to = (y + dy) % NY
        to = dev(z, y_to, x, c)
        send(buf["router_out"].at[y_to], buf["router_y"].at[y], id_router_y, to)
    buf["router_y"][y] = buf["router_out"][y]

    def backward_block(b, diagonal):
        keys, values = buf["kk"][b], buf["vv"][b]
        queries, go = buf["qh"][...], buf["goh"][...]
        scores = dot(keys, queries, 1, 1) * factor2
        weights = jnp.exp2(scores - buf["lse"][0:1, :])
        if diagonal:
            weights = jnp.where(allowed(), weights, 0.0)
        grad_weights = dot(values, go, 1, 1)
        grad_scores = (weights * (grad_weights - buf["delta"][0:1, :])).astype(BF)
        buf["dvp"][b] = dot(weights.astype(BF), go, 1, 0)
        buf["dkp"][b] = dot(grad_scores, queries, 1, 0)
        buf["dqt"][...] += dot(keys, grad_scores, 0, 0)

    def backward_pair(t):
        pl.when(z >= t)(lambda: backward_block((z + nz - t) % nz, False))
        if t <= nz - 1 - t:
            pl.when(z + t >= nz)(lambda: backward_block((z + t) % nz, False))

    def target(direction, d):
        return (z + nz - d) % nz if direction == 0 else (z + d) % nz

    id_kv_fin, id_dq = alloc("recv"), alloc("recv")
    side = y % 2

    def kv_part(kind, b, part):
        return (buf["dkp"] if kind == 0 else buf["dvp"]).at[b, part, :]

    def kv_useless(b, kind, direction, d):
        return jnp.logical_not(needed(b, direction == 1, d, direction == kind))

    def kv_far():
        for kind in range(2):
            b = target(kind, far)
            useless = kv_useless(b, kind, kind, far)
            for part in halves:
                out = buf["kv_send"].at[kind, kind, near, part, :]
                out[...] = kv_part(kind, b, part)[...].astype(BF)
                key = ident("chain", kind, kind, part.start, near)
                to = dev(z_jump[kind], y, x, c)
                send(out, buf["kv_recv"].at[kind, kind, near, part, :], key, to, useless)

    def kv_taken(total, kind, direction, t, part, useless):
        ref = buf["kv_recv"].at[kind, direction, t, part, :]
        recv(ref, ident("chain", kind, direction, part.start, t), useless)

        @pl.when(jnp.logical_not(useless))
        def _():
            total[...] += ref[...].astype(F32)

    def kv_step(t):
        d = near - t
        for kind in range(2):
            for part in halves:
                for direction in range(2):
                    b = target(direction, d)
                    total = kv_part(kind, b, part)
                    if t > 0:
                        useless = kv_useless(b, kind, direction, d + 1)
                        kv_taken(total, kind, direction, t - 1, part, useless)
                    if d == relay and direction == kind:
                        useless = kv_useless(b, kind, direction, far)
                        kv_taken(total, kind, direction, near, part, useless)
                    out = buf["kv_send"].at[kind, direction, t, part, :]
                    useless = kv_useless(b, kind, direction, d)

                    @pl.when(jnp.logical_not(useless))
                    def _():
                        out[...] = total[...].astype(BF)

                    if d > 1:
                        key = ident("chain", kind, direction, part.start, t)
                        dst = buf["kv_recv"].at[kind, direction, t, part, :]
                        send(out, dst, key, dev_next[direction], useless)
                    else:
                        to = dev(down if direction == 0 else up, 2 * c + part.start // HD, x, half_y)
                        dst = kv_land.at[direction, kind, side]
                        send(out, dst, ident("land", direction, kind), to, useless)

    def dw_part(b, half):
        rows_of = buf["slices"][:, pl.ds(pl.multiple_of((b % hz) * HD, HD), HD)]
        return dot(rows_of, buf["outs"][:, half * 2 * HD : (half + 1) * 2 * HD], 0, 0)

    def dw_ways(d):
        for half in range(2):
            for direction in range(2):
                if d < far or direction == half:
                    b = target(direction, d)
                    yield half, direction, b, b // hz != c

    def dw_ready():
        for half, direction, b, skip in dw_ways(2):

            @pl.when(jnp.logical_not(skip))
            def _():
                buf["dw_acc"][half, direction] = dw_part(b, half)

    def dw_send(d):
        inc = buf["dw_recv"]
        for half, direction, b, skip in dw_ways(d):
            out = buf["dw_send"].at[half, direction, d - 1]
            takes = [u for u in (3, 4) if d == 2 and (u < far or direction == half)]
            for u in takes:
                recv(inc.at[half, direction, u - 1], ident("dw", half, direction, u), skip)

            @pl.when(jnp.logical_not(skip))
            def _():
                total = buf["dw_acc"][half, direction] if d == 2 else dw_part(b, half)
                for u in takes:
                    total = total + inc[half, direction, u - 1].astype(F32)
                out[...] = total.astype(BF)

            if d == far:
                to = dev(z_jump[direction], y, x, c)
            elif d == 3:
                to = dev_next[direction]
            else:
                to = dev(b, y, x, half)
            send(out, inc.at[half, direction, d - 1], ident("dw", half, direction, d), to, skip)

    id_dw_own = alloc("recv")
    not_holder = z // hz != c
    holder = jnp.logical_not(not_holder)

    def dw_own_block():
        @pl.when(holder)
        def _():
            for half in range(2):
                buf["dw_mine"][half] = dw_part(z, half)
            buf["dw_own"][...] = buf["dw_mine"][c]

        send(buf["dw_mine"].at[sib], buf["dw_own"], id_dw_own, dev_sib, not_holder)

    def dw_last():
        recv(buf["dw_own"], id_dw_own, holder)
        for half in range(2):

            @pl.when(c == half)
            def _():
                total = buf["dw_own"][...]
                for d in (1, 2):
                    for direction in range(2):
                        ref = buf["dw_recv"].at[half, direction, d - 1]
                        recv(ref, ident("dw", half, direction, d))
                        total = total + ref[...].astype(F32)
                buf["dw_fin"][...] = total

    def share_outs():
        recv(buf["outs"].at[: 2 * HD, : (NY - 1) * HD], id_outs)
        for dy in range(1, NY):
            ref = out_part((y + dy) % NY, c)
            send(ref, ref, id_outs_sib, dev_sib)

    def take_outs():
        if nx > 1:
            recv(buf["slices"].at[:, : (nx - 1) * share], id_slice_x)
        recv(buf["outs"].at[: 2 * HD, : (NY - 1) * HD], id_outs_sib)

    id_router_x = alloc("recv")

    def router_send():
        recv(buf["router_y"].at[: NY - 1], id_router_y)
        total = buf["router_y"][0]
        for i in range(1, NY):
            total = total + buf["router_y"][i]
        buf["router_x"][x] = total
        for dx in range(1, nx):
            x_to = (x + dx) % nx
            ref = buf["router_x"].at[x]
            send(ref, ref, id_router_x, dev(z, y, x_to, c))

    def router_last():
        if nx > 1:
            recv(buf["router_x"].at[: nx - 1], id_router_x)
        total = buf["router_x"][0]
        for i in range(1, nx):
            total = total + buf["router_x"][i]
        token_row = lax.broadcasted_iota(jnp.int32, (HD, cap), 0)
        token_slot = lax.broadcasted_iota(jnp.int32, (HD, cap), 1)
        own = jnp.logical_and(token_row == own_start + token_slot, token_slot < own_count)
        spread = dot(own.astype(F32).astype(BF), pick_bf, 1, 0)
        placed = dot(total, spread, 1, 0, lax.Precision.HIGHEST)
        sig = 1.0 / (1.0 + jnp.exp(-logit_row))
        lg_ref[...] = placed[0:1, :] * sig * (1.0 - sig)


    def send_own_part():
        for kind in range(2):
            for j in range(2):
                buf["kv_fin"][kind, j] = kv_part(kind, z, halves[j])[...].astype(BF)
                y_to = 2 * c + j
                own = jnp.logical_and(y_to == y, half_y == c)
                src, dst = buf["kv_fin"].at[kind, j], kv_land.at[2, kind, side]
                send(src, dst, id_kv_fin, dev(z, y_to, x, half_y), own)
                keep(src, dst, id_kv_fin, own)

    def send_query_grads():
        for i in range(NY):
            buf["dq_out"][i] = (buf["dqt"][:, i * HD : (i + 1) * HD].T * factor).astype(BF)
            own = jnp.logical_and(y == i, half_y == c)
            src, dst = buf["dq_out"].at[i], dq_land.at[side, c]
            send(src, dst, id_dq, dev(z, i, x, half_y), own)
            keep(src, dst, id_dq, own)

    for d in range(far, 0, -1):
        backward_pair(d)
        if d == far:
            kv_far()
        if d == near:
            kv_step(0)
    backward_block(z, True)
    send_query_grads()
    send_own_part()
    share_outs()
    if near > 1:
        kv_step(1)
    take_outs()
    dw_send(4)
    dw_send(3)
    dw_send(1)
    router_send()
    dw_ready()
    kv_step(2)
    dw_own_block()
    router_last()
    dw_send(2)
    dw_last()
    dw_out = pltpu.make_async_copy(buf["dw_fin"], dw_land, local_sems.at[alloc("local")])
    dw_out.start()

    recv(dq_land, id_dq)
    recv(kv_land.at[2], id_kv_fin)
    for direction in range(2):
        for kind in range(2):
            useless = kv_useless(z, kind, direction, 1)
            recv(kv_land.at[direction, kind], ident("land", direction, kind), useless)
    dw_out.wait()
    for entry in pool + singles:
        if entry is not None:
            wait_sent(entry)


POOL = 24
RECV_SEMS = 89
SEND_SEMS = 38
VMEM_LIMIT = 60 * 1024 * 1024


def finish(nz, dq_land, kv_land, dw_land, lg_in, dq_ref, dk_ref, dv_ref, dw_ref, lg_ref):
    lay = Layout(nz, 1, HD, HD, HD)
    z = lax.axis_index("seq") // NY
    for j in range(2):
        cols = slice(j * HD, (j + 1) * HD)
        dq_ref[:, cols] = (dq_land[j, 0].astype(F32) + dq_land[j, 1].astype(F32)).astype(BF)
        for kind, ref, scale in ((0, dk_ref, HD ** (-0.5)), (1, dv_ref, 1.0)):
            total = kv_land[2, kind, j].astype(F32)
            for way in range(2):
                useful = lay.needed(z, way == 1, 1, way == kind)
                total = total + jnp.where(useful, kv_land[way, kind, j].astype(F32), 0.0)
            ref[:, cols] = (total * scale).astype(BF)
    dw_ref[...] = dw_land[...]
    lg_ref[...] = lg_in[...]


def shards_fn(nz, nx):
    def run(grad, logit, index, count, weight, q, k, v):
        lay = Layout(nz, nx, grad.shape[0], index.shape[0], grad.shape[1])
        scratch = lay.scratch()
        names = list(scratch)
        any_ = pl.BlockSpec(memory_space=pl.ANY)
        smem = pl.BlockSpec(memory_space=pltpu.SMEM)
        vmem = pl.BlockSpec(memory_space=pltpu.VMEM)

        def kernel(*refs):
            fused(lay, names, *refs)

        lands = pl.pallas_call(
            kernel,
            out_shape=(
                jax.ShapeDtypeStruct((2, 2, HD, HD), BF),
                jax.ShapeDtypeStruct((3, 2, 2, HD, HD), BF),
                jax.ShapeDtypeStruct((HD, 2 * HD), F32),
                jax.ShapeDtypeStruct((1, HD), F32),
            ),
            in_specs=[any_, vmem, smem, smem, any_, any_, any_, any_],
            out_specs=(any_, any_, any_, vmem),
            scratch_shapes=list(scratch.values())
            + [
                pltpu.SemaphoreType.DMA((SEND_SEMS,)),
                pltpu.SemaphoreType.DMA((RECV_SEMS,)),
                pltpu.SemaphoreType.DMA((3,)),
            ],
            compiler_params=pltpu.CompilerParams(
                collective_id=0, has_side_effects=True, vmem_limit_bytes=VMEM_LIMIT
            ),
            name="routed_backward",
        )(grad, logit.reshape(1, -1), index, count, weight, q, k, v)
        out = pl.pallas_call(
            functools.partial(finish, nz),
            out_shape=(
                jax.ShapeDtypeStruct(q.shape, BF),
                jax.ShapeDtypeStruct(q.shape, BF),
                jax.ShapeDtypeStruct(q.shape, BF),
                jax.ShapeDtypeStruct((HD, q.shape[1]), F32),
                jax.ShapeDtypeStruct((1, HD), F32),
            ),
            in_specs=[vmem] * 4,
            out_specs=(vmem,) * 5,
            compiler_params=pltpu.CompilerParams(vmem_limit_bytes=VMEM_LIMIT),
            name="finish",
        )(*lands)
        return (*out[:4], out[4].reshape(-1))

    return run


def solution(mesh):
    nz = mesh.shape["seq"] // NY
    nx = mesh.shape["grp"] // 2
    placed = (
        P(("seq", "grp"), None),
        P(("seq", "grp")),
        P(("seq", "grp")),
        P(),
        P("grp", None),
        P("seq", "grp"),
        P("seq", "grp"),
        P("seq", "grp"),
    )
    return jax.shard_map(
        shards_fn(nz, nx),
        mesh=mesh,
        in_specs=placed,
        out_specs=(
            P("seq", "grp"),
            P("seq", "grp"),
            P("seq", "grp"),
            P("seq", "grp"),
            P(("seq", "grp")),
        ),
        check_vma=False,
    )
```
